768 devices in a mesh: circ: 16 (over x, z_lo), rad: 6 (over z_hi, core), mode: 8 (over y).
Axes of the slice: x: 4, y: 8, z: 12 (z_hi: 3, z_lo: 4; z = z_hi * 4 + z_lo), core: 2. Of those that a mesh axis runs over, the one named last changes fastest.
Arguments:
- adjoint_prev: float32 [3, 64, 48, 2048], P(None, 'circ', 'rad', 'mode'), may hold values from -6 to 6
- cell_class: int32 [64, 48, 2048], P('circ', 'rad', 'mode'), may hold values from 0 to 7
- class_moduli: float32 [8], replicated, may hold values from 0.2 to 5
- flow_sens: float32 [16, 6, 8, 8, 3, 512], P('circ', 'rad', 'mode'), may hold values from -12 to 12
- flow_nodes: int32 [16, 6, 8, 8, 512], P('circ', 'rad', 'mode'), may hold values from 0 to 8191
- flow_count: int32 [16, 6, 8, 8], P('circ', 'rad', 'mode'), may hold values from 64 to 512, as said below
- surf_ids: int32 [16, 6, 8, 512], P('circ', 'rad', 'mode'), may hold values from 0 to 8191
- mode_shapes: float32 [16, 6, 8, 24, 3, 512], P('circ', 'rad', 'mode'), may hold values from -0.03125 to 0.03125
Outputs:
- adjoint: float32 [3, 64, 48, 2048], P(None, 'circ', 'rad', 'mode')
- gen_force: float32 [24, 16], P('mode', 'circ')
The draws below stay inside these ranges and needn't reach their ends.
Inputs may be any that keep to these rules, and one draw needn't show every extreme that they name: In each group of devices that share c and r, one destination d, drawn, has flow_count equal to 512 from every source k; all other counts lie in 64 to 256. `flow_nodes`: A cell index within a block, last dimension fastest. `surf_ids`: A cell index within the listing block, last dimension fastest.
All inputs are finite; a program needn't handle non-finite values.
Results may differ from the reference program's by a relative error of at most 0.0003.
Values sent between devices are 32-bit elements; how exact they have to be, the bound alone decides.
No kernel may reach another device: no remote copies, remote signals or barrier semaphores. Data moves between devices by JAX's collectives and lax.ppermute only.
A program may use at most 32 MiB of HBM per device.

```python
import math
import jax
import jax.numpy as jnp
from jax import lax

CC = 4
CR = 8
CA = 256
SURF = 512
SLOT = 512
NMODES = 24
NCLASS = 8
CELLS = 8192
NC = 64
NR = 48
NA = 2048
N_CIRC = 16
N_RAD = 6
N_MODE = 8


def draw_flow_count(key, part):
    key = jax.random.fold_in(key, 7)
    base_key, hot_key = jax.random.split(key)
    shape = (N_CIRC, N_RAD, N_MODE, N_MODE)
    base = jax.random.randint(base_key, shape, SLOT // 8, SLOT // 2 + 1)
    hottest = jax.random.randint(hot_key, (N_CIRC, N_RAD, 1, 1), 0, N_MODE)
    target = lax.broadcasted_iota(jnp.int32, shape, 3)
    return jnp.where(target == hottest, SLOT, base).astype(jnp.int32)


def place_ends(drawn, key, least, largest):
    longest = drawn.shape.index(max(drawn.shape))
    spots = []
    for shift in (0, 1):
        where = [jax.random.randint(jax.random.fold_in(key, axis), (), 0, length) for axis, length in enumerate(drawn.shape)]
        where[longest] = (where[longest] + shift) % drawn.shape[longest]
        spots.append(tuple(where))
    return drawn.at[spots[0]].set(least).at[spots[1]].set(largest)


def spiked(result, key, source, target, shards_of, factor):
    def block_of(position):
        return (jnp.arange(result.shape[position]) // (result.shape[position] // shards_of)).reshape((-1,) + (1,) * (result.ndim - 1 - position))

    one_side = jax.random.permutation(key, shards_of)[block_of(target)]
    far = (block_of(target) + shards_of // 2) % shards_of
    return jnp.where((block_of(source) == one_side) | (block_of(source) == far), factor * result, result)


def block_scale(own_key, dims, cuts, least, top_value):
    factor_of, own = 1.0, jax.random.fold_in(own_key, 6)
    for position, parts in cuts:
        heights = jnp.exp(jax.random.uniform(jax.random.fold_in(own, position), (parts,), jnp.float32, least / len(cuts), top_value / len(cuts)))
        factor_of = factor_of * jnp.repeat(heights, dims[position] // parts).reshape([-1 if axis == position else 1 for axis in range(len(dims))])
    return factor_of


def noise(rng, dims, scale, most, cuts=(), kind=jnp.bfloat16):
    drawn = scale * jax.random.normal(rng, dims, jnp.float32)
    if cuts:
        drawn = drawn * block_scale(rng, dims, cuts, -0.22, 0.18)
    return jnp.clip(drawn, -most, most).astype(kind)


def gaussian_with(own_key, dims, scale, reach, shards, heavy, held_as=jnp.bfloat16):
    drawn = scale * jax.random.normal(own_key, dims, jnp.float32)
    if shards:
        drawn = drawn * block_scale(own_key, dims, shards, -0.22, 0.18)
    return jnp.clip(spiked(drawn, jax.random.fold_in(own_key, 3), *heavy), -reach, reach).astype(held_as)


def setup_inputs(seed: int = 0) -> dict:
    key_of = jax.random.split(jax.random.key(seed), 9)
    adjoint_prev = noise(key_of[0], (3, NC, NR, NA), 1.0, 6.0, ((1, 16), (2, 6), (3, 8)), jnp.float32)
    cell_class = place_ends(jax.random.randint(key_of[1], (NC, NR, NA), 0, NCLASS), jax.random.fold_in(key_of[1], 1), 0, NCLASS - 1).astype(jnp.int32)
    class_moduli = jnp.clip(jnp.exp(jax.random.uniform(key_of[2], (NCLASS,), jnp.float32, math.log(0.2), math.log(5.0))), 0.2, 5.0)
    flow_sens = noise(key_of[3], (N_CIRC, N_RAD, N_MODE, N_MODE, 3, SLOT), 2.0, 12.0, ((0, 16), (1, 6), (2, 8)), jnp.float32)
    flow_nodes = place_ends(jax.random.randint(key_of[4], (N_CIRC, N_RAD, N_MODE, N_MODE, SLOT), 0, CELLS), jax.random.fold_in(key_of[4], 1), 0, CELLS - 1).astype(jnp.int32)
    flow_count = draw_flow_count(jax.random.fold_in(key_of[8], 71), 0)
    surf_ids = place_ends(jax.random.randint(key_of[6], (N_CIRC, N_RAD, N_MODE, SURF), 0, CELLS), jax.random.fold_in(key_of[6], 1), 0, CELLS - 1).astype(jnp.int32)
    mode_shapes = gaussian_with(key_of[7], (N_CIRC, N_RAD, N_MODE, NMODES, 3, SURF), (3 * SURF * N_RAD * N_MODE) ** -0.5, 0.03125, ((0, 16), (1, 6), (2, 8)), (2, 3, 8, 2.0), jnp.float32)
    return dict(adjoint_prev=adjoint_prev, cell_class=cell_class, class_moduli=class_moduli, flow_sens=flow_sens, flow_nodes=flow_nodes, flow_count=flow_count, surf_ids=surf_ids, mode_shapes=mode_shapes)


coupling = 0.5
relaxation = 0.6


def neighbour_offsets():
    return [(a, b, c) for a in (-1, 0, 1) for b in (-1, 0, 1) for c in (-1, 0, 1) if (a, b, c) != (0, 0, 0)]


def relax(lam_pad, e_pad, rhs):
    s1, s2, s3 = e_pad.shape

    def near(array, dx, dy, dz):
        return array[..., 1 + dx:s1 - 1 + dx, 1 + dy:s2 - 1 + dy, 1 + dz:s3 - 1 + dz]

    centre = near(lam_pad, 0, 0, 0)
    e_centre = near(e_pad, 0, 0, 0)
    action = jnp.zeros_like(centre)
    diagonal = jnp.zeros_like(centre)
    for dx, dy, dz in neighbour_offsets():
        square = float(dx * dx + dy * dy + dz * dz)
        link = (0.5 / square) * (e_centre + near(e_pad, dx, dy, dz))
        diff = centre - near(lam_pad, dx, dy, dz)
        along = (dx * diff[0] + dy * diff[1] + dz * diff[2]) / square
        direction = jnp.array([dx, dy, dz], jnp.float32)[:, None, None, None]
        action = action + link[None] * (diff + coupling * direction * along[None])
        diagonal = diagonal + link[None] * (1.0 + coupling * direction * direction / square)
    return centre + relaxation * (rhs - action) / diagonal


def pad_field(field):
    wrapped = jnp.concatenate([field[..., -1:, :, :], field, field[..., :1, :, :]], axis=-3)
    widths = [(0, 0)] * (field.ndim - 2) + [(1, 1), (1, 1)]
    return jnp.pad(wrapped, widths)


def reference(adjoint_prev, cell_class, class_moduli, flow_sens, flow_nodes, flow_count, surf_ids, mode_shapes):
    cells_circ = CC * N_CIRC
    cells_rad = CR * N_RAD
    cells_axial = CA * N_MODE
    moduli = class_moduli[cell_class]
    shape = flow_nodes.shape
    live = lax.broadcasted_iota(jnp.int32, shape, 4) < flow_count[..., None]
    values = jnp.where(live[:, :, :, :, None, :], flow_sens, jnp.float32(0.0))
    local_c = flow_nodes // (CR * CA)
    local_r = (flow_nodes // CA) % CR
    local_a = flow_nodes % CA
    block_c = lax.broadcasted_iota(jnp.int32, shape, 0)
    block_r = lax.broadcasted_iota(jnp.int32, shape, 1)
    block_d = lax.broadcasted_iota(jnp.int32, shape, 3)
    target = ((block_c * CC + local_c) * cells_rad + block_r * CR + local_r) * cells_axial + block_d * CA + local_a
    target = target.astype(jnp.int32).reshape(-1)
    flat_values = jnp.moveaxis(values, 4, 0).reshape(3, -1)
    total_cells = cells_circ * cells_rad * cells_axial
    rhs = jnp.zeros((3, total_cells), jnp.float32).at[:, target].add(flat_values)
    rhs = rhs.reshape(3, cells_circ, cells_rad, cells_axial)
    moduli_pad = pad_field(moduli)
    middle = relax(pad_field(adjoint_prev), moduli_pad, rhs)
    final = relax(pad_field(middle), moduli_pad, rhs)
    blocks = final.reshape(3, N_CIRC, CC, N_RAD, CR, N_MODE, CA)
    blocks = blocks.transpose(1, 3, 5, 0, 2, 4, 6).reshape(N_CIRC, N_RAD, N_MODE, 3, CC * CR * CA)
    picked = jnp.take_along_axis(blocks, surf_ids[:, :, :, None, :], axis=4)
    force = jnp.einsum('crkmps,crkps->mc', mode_shapes, picked, precision=lax.Precision.HIGHEST)
    return final, force
```

```python
import functools

import jax
import jax.numpy as jnp
from jax import lax
from jax.experimental import pallas as pl
from jax.experimental.pallas import tpu as pltpu
from jax.sharding import PartitionSpec as P

coupling = 0.5
relaxation = 0.6

face_own, face_other = 0.5 * (1.0 + coupling), 0.5
edge_own, edge_other = 0.25 * (1.0 + 0.5 * coupling), 0.25
corner_own = (1.0 + coupling / 3.0) / 6.0
edge_cross = 0.25 * coupling / 2.0
corner_cross = coupling / 18.0
centre_weight = 2 * face_own + 4 * face_other + 8 * edge_own + 4 * edge_other + 8 * corner_own

F32 = jnp.float32
BF16 = jnp.bfloat16
NT = (((1,), (1,)), ((), ()))


def split(x):
    high = x.astype(BF16).astype(F32)
    return high, x - high


def pack_kernel(moduli, count, prev, cls, sens, nodes, send, e_out, values, hits):
    _, blocks, slots = sens.shape
    ncirc, nrad, naxial = cls.shape
    lines = ncirc * nrad
    k = lax.axis_index("mode")
    lane = lax.broadcasted_iota(jnp.int32, (nrad, 128), 1)
    to_low, to_high = [], []
    for c in range(ncirc):
        level = cls[c]
        e = jnp.zeros(level.shape, F32)
        for i in range(moduli.shape[0]):
            e = jnp.where(level == i, moduli[i], e)
        e_out[c] = e
        low = jnp.zeros((nrad, 128), F32)
        high = jnp.zeros((nrad, 128), F32)
        for f in range(4):
            field = prev[f, c] if f < 3 else e
            first = pltpu.roll(field[:, :128], 4 * f + 2, 1)
            last = pltpu.roll(field[:, naxial - 128 :], 4 * f + 2, 1)
            low = jnp.where((lane == 4 * f + 2) | (lane == 4 * f + 3), first, low)
            high = jnp.where((lane == 4 * f) | (lane == 4 * f + 1), last, high)
        to_low.append(low)
        to_high.append(high)

    values[...] = jnp.zeros(values.shape, BF16)
    slot = lax.broadcasted_iota(jnp.int32, (3, slots), 1)
    row = lax.broadcasted_iota(jnp.int32, (16, slots), 0)
    place = lax.broadcasted_iota(jnp.int32, (2 * lines, slots), 0)
    for d in range(blocks):
        vals = jnp.concatenate([sens[i, d : d + 1] for i in range(3)], axis=0)
        vals = jnp.where(slot < count[d], vals, 0.0)
        node = nodes[d : d + 1]
        for q in range(slots // 128):
            cut = slice(128 * q, 128 * (q + 1))
            send[d, 4 * q : 4 * q + 3, :] = vals[:, cut]
            send[d, 4 * q + 3 : 4 * q + 4, :] = node[:, cut].astype(F32)
        high, low = split(vals)
        tile = jnp.zeros((16, slots), F32)
        for i in range(3):
            tile = jnp.where(row == 2 * i, high[i : i + 1], tile)
            tile = jnp.where(row == 8 + 2 * i, low[i : i + 1], tile)
        values[16 * d : 16 * (d + 1), slots * d : slots * (d + 1)] = tile.astype(BF16)
        axial = node % naxial
        line = node // naxial
        key = jnp.where(axial == 0, line, jnp.where(axial == naxial - 1, line + lines, -1))
        hits[:, slots * d : slots * (d + 1)] = jnp.where(key == place, 1.0, 0.0).astype(BF16)

    planes = lax.dot_general(hits[...], values[...], NT, preferred_element_type=F32)
    planes = planes + pltpu.roll(planes, 120, 1)
    wide = lax.broadcasted_iota(jnp.int32, (lines, 128), 1)
    even = (wide == 16) | (wide == 18) | (wide == 20)
    odd = (wide == 17) | (wide == 19) | (wide == 21)
    for d in range(blocks):
        beside = jnp.zeros((lines, 128), F32)
        if d + 1 < blocks:
            moved = pltpu.roll(planes[:lines], (17 - 16 * (d + 1)) % 128, 1)
            beside = jnp.where(odd, moved, beside)
        if d > 0:
            moved = pltpu.roll(planes[lines:], (16 - 16 * (d - 1)) % 128, 1)
            beside = jnp.where(even, moved, beside)
        for c in range(ncirc):
            out = beside[nrad * c : nrad * (c + 1)]
            out = out + jnp.where(k == d + 1, to_low[c], 0.0) + jnp.where(k == d - 1, to_high[c], 0.0)
            send[d, 16 + nrad * c : 16 + nrad * (c + 1), :] = out


def scatter_kernel(got, prev, e, rhs, ends, first, second, left, right):
    blocks = got.shape[0]
    _, ncirc, nrad, naxial = prev.shape
    lines = ncirc * nrad
    row = lax.broadcasted_iota(jnp.int32, (lines, 128), 0)
    cell = lax.broadcasted_iota(jnp.int32, (naxial, 128), 0)
    for d in range(blocks):
        for q in range(4):
            cut = slice(128 * (4 * d + q), 128 * (4 * d + q + 1))
            node = got[d, 4 * q + 3 : 4 * q + 4, :].astype(jnp.int32)
            right[:, cut] = jnp.where(cell == node % naxial, 1.0, 0.0).astype(BF16)
            hit = row == node // naxial
            for i in range(3):
                for j, part in enumerate(split(got[d, 4 * q + i : 4 * q + i + 1, :])):
                    at = lines * (2 * i + j)
                    left[at : at + lines, cut] = jnp.where(hit, part, 0.0).astype(BF16)
    dense = lax.dot_general(left[...], right[...], NT, preferred_element_type=F32)
    for i in range(3):
        total = dense[2 * lines * i : 2 * lines * i + lines] + dense[2 * lines * i + lines : 2 * lines * (i + 1)]
        for c in range(ncirc):
            rhs[i, c] = total[nrad * c : nrad * (c + 1)]
    for c in range(ncirc):
        at = slice(16 + nrad * c, 16 + nrad * (c + 1))
        total = got[0, at, :]
        for d in range(1, blocks):
            total = total + got[d, at, :]
        ends[c] = total
    odd = lax.axis_index("circ") % 2
    for out, at_high in ((first, 1 - odd), (second, odd)):
        base = at_high * (ncirc - 2)
        edge = at_high * (ncirc - 1)
        for t in range(2):
            cut = slice(128 * t, 128 * (t + 1))
            for f in range(4):
                for j in range(2):
                    source = prev[f, base + j] if f < 3 else e[base + j]
                    out[4 * f + 2 * t + j] = source[:, cut]
            for i in range(3):
                out[16 + 2 * i + t] = rhs[i, edge][:, cut]
        for j in range(2):
            out[22 + j] = ends[base + j]


def turn_kernel(prev, e, rhs, ends, got_first, got_second, turned, first, second):
    _, ncirc, nrad, _ = prev.shape
    odd_circ = lax.axis_index("circ") % 2 == 1

    def put(index, c, plane):
        turned[index, pl.ds(c, nrad, stride=8), :] = plane

    for c in range(ncirc):
        for t in range(2):
            cut = slice(128 * t, 128 * (t + 1))
            for f in range(4):
                source = prev[f, c] if f < 3 else e[c]
                put(2 * f + t, c, source[:, cut])
            for i in range(3):
                put(8 + 2 * i + t, c, rhs[i, c][:, cut])
        put(14, c, ends[c])

    def sides(tile):
        a, b = got_first[tile], got_second[tile]
        return jnp.where(odd_circ, a, b), jnp.where(odd_circ, b, a)

    for index in range(8):
        for j in range(2):
            low, high = sides(2 * index + j)
            put(index, 6 + j, low)
            put(index, 4 + j, high)
    for index in range(6):
        low, high = sides(16 + index)
        put(8 + index, 7, low)
        put(8 + index, 4, high)
        put(8 + index, 6, low)
        put(8 + index, 5, high)
    for j in range(2):
        low, high = sides(22 + j)
        put(14, 6 + j, low)
        put(14, 4 + j, high)

    odd = lax.axis_index("rad") % 2
    for out, at_high in ((first, 1 - odd), (second, odd)):
        for index in range(15):
            for j in range(2):
                plane = at_high * (nrad - 2) + j
                at = 2 * index + j
                if 8 <= index < 14:
                    if j:
                        continue
                    plane = at_high * (nrad - 1)
                    at = 16 + index - 8
                elif index == 14:
                    at = 22 + j
                out[at] = turned[index, pl.ds(pl.multiple_of(8 * plane, 8), 8), :]


def sums(x):
    up = pltpu.roll(x, x.shape[1] - 1, 1)
    down = pltpu.roll(x, 1, 1)
    return up + down, up - down


def across(x):
    up = pltpu.roll(x, 7, 0)
    down = pltpu.roll(x, 1, 0)
    return up + down, up - down


def spread(x):
    sn, dn = sums(x)
    sm, dm = across(x)
    smsn, dmsn = across(sn)
    smdn, dmdn = across(dn)
    return sn, dn, sm, dm, smsn, dmsn, smdn, dmdn


def leading_terms(x, s):
    sn, _, sm, _, both = s[0], s[1], s[2], s[3], s[4]
    near = sm + sn
    return face_other * near + edge_other * both, face_own * x + edge_own * near + corner_own * both


def plane_terms(x, own, other, both):
    centre = face_own * own + face_other * other + edge_own * both
    side = face_other * x + edge_own * own + edge_other * other + corner_own * both
    return centre, side


def cross_terms(s):
    _, dn, _, dm, _, dmsn, smdn, dmdn = s
    return edge_cross * dm + corner_cross * dmsn, edge_cross * dn + corner_cross * smdn, dmdn


def vector_terms(v):
    s0, s1, s2 = spread(v[0]), spread(v[1]), spread(v[2])
    p0, q0 = plane_terms(v[0], s0[2], s0[0], s0[4])
    p1, q1 = leading_terms(v[1], s1)
    p2, q2 = plane_terms(v[2], s2[0], s2[2], s2[4])
    rm0, _, w0 = cross_terms(s0)
    rm1, rn1, _ = cross_terms(s1)
    _, rn2, w2 = cross_terms(s2)
    p0 = p0 + edge_cross * w2
    q0 = q0 + corner_cross * w2
    p2 = p2 + edge_cross * w0
    q2 = q2 + corner_cross * w0
    d0, d1, d2 = rm1, rm0 + rn2, rn1
    return (p0, p1, p2), (q0 + d0, q1 + d1, q2 + d2), (q0 - d0, q1 - d1, q2 - d2)


def scalar_terms(e):
    s = spread(e)
    p0, q0 = plane_terms(e, s[2], s[0], s[4])
    p1, q1 = leading_terms(e, s)
    p2, q2 = plane_terms(e, s[0], s[2], s[4])
    rm, rn, w = cross_terms(s)
    return (p0, p1, p2), (q0, q1, q2), rm, rn, w


def stiffness(e, below, here, above):
    diag = [
        centre_weight * e + here[0][i] + below[1][i] + above[1][i] for i in range(3)
    ]
    c01 = above[2] - below[2]
    c12 = above[3] - below[3]
    c02 = edge_cross * here[4] + corner_cross * (above[4] + below[4])
    return diag, c01, c02, c12


def residual(v, e, rhs, stiff, below, here, above, below_e, here_e, above_e):
    (d0, d1, d2), c01, c02, c12 = stiff
    own = (
        d0 * v[0] + c01 * v[1] + c02 * v[2],
        c01 * v[0] + d1 * v[1] + c12 * v[2],
        c02 * v[0] + c12 * v[1] + d2 * v[2],
    )
    out = []
    for i in range(3):
        plain = here[0][i] + above[1][i] + below[2][i]
        scaled = here_e[0][i] + above_e[1][i] + below_e[2][i]
        out.append(rhs[i] - own[i] + e * plain + scaled)
    return out


def sweep_kernel(
    devices, turned, got_first, got_second, shapes, ids, adjoint, force, keep, sums_of
):
    nrad = turned.shape[1] // 8
    ncirc = adjoint.shape[1]
    rad, mode = lax.axis_index("rad"), lax.axis_index("mode")
    odd = rad % 2 == 1

    def from_low(tile):
        return jnp.where(odd, got_first[tile], got_second[tile])

    def from_high(tile):
        return jnp.where(odd, got_second[tile], got_first[tile])

    def tile_at(index, plane):
        if 0 <= plane < nrad:
            return turned[index, 8 * plane : 8 * (plane + 1), :]
        low = plane < 0
        j = plane + 2 if low else plane - nrad
        if index == 14:
            at = 22 + j
        elif index >= 8:
            at = 16 + index - 8
        else:
            at = 2 * index + j
        return from_low(at) if low else from_high(at)

    def field_at(f, plane, ends):
        shift = 4 * f + 2 if f < 4 else 17 + 2 * (f - 4)
        return jnp.concatenate(
            [tile_at(2 * f, plane), tile_at(2 * f + 1, plane), pltpu.roll(ends, 128 - shift, 1)], axis=1
        )

    lane = lax.broadcasted_iota(jnp.int32, (8, 384), 1)
    outside = ((lane == 383) & (mode == 0)) | ((lane == 256) & (mode == lax.axis_size("mode") - 1))
    fields, terms, e_terms, scaled_terms = {}, {}, {}, {}
    middle, stiff, inverse = {}, {}, {}
    for plane in range(-2, nrad + 2):
        ends = tile_at(14, plane)
        v = [field_at(f, plane, ends) for f in range(3)]
        e = field_at(3, plane, ends)
        fields[plane] = (v, e, ends)
        terms[plane] = vector_terms(v)
        scaled_terms[plane] = vector_terms([e * x for x in v])
        e_terms[plane] = scalar_terms(e)
        at = plane - 1
        if at < -1:
            continue
        v, e, ends = fields[at]
        stiff[at] = stiffness(e, e_terms[at - 1], e_terms[at], e_terms[at + 1])
        inverse[at] = [relaxation / x for x in stiff[at][0]]
        rhs = [field_at(4 + i, at, ends) for i in range(3)]
        rest = residual(
            v, e, rhs, stiff[at],
            terms[at - 1], terms[at], terms[at + 1],
            scaled_terms[at - 1], scaled_terms[at], scaled_terms[at + 1],
        )
        drop = outside
        if at == -1:
            drop = drop | (rad == 0)
        if at == nrad:
            drop = drop | (rad == lax.axis_size("rad") - 1)
        middle[at] = [jnp.where(drop, 0.0, v[i] + inverse[at][i] * rest[i]) for i in range(3)]

    terms, scaled_terms = {}, {}
    for plane in range(-1, nrad + 1):
        v, e = middle[plane], fields[plane][1]
        terms[plane] = vector_terms(v)
        scaled_terms[plane] = vector_terms([e * x for x in v])
        at = plane - 1
        if at < 0:
            continue
        v, e = middle[at], fields[at][1]
        rhs = [field_at(4 + i, at, fields[at][2]) for i in range(3)]
        rest = residual(
            v, e, rhs, stiff[at],
            terms[at - 1], terms[at], terms[at + 1],
            scaled_terms[at - 1], scaled_terms[at], scaled_terms[at + 1],
        )
        for i in range(3):
            final = v[i] + inverse[at][i] * rest[i]
            for t in range(2):
                keep[2 * i + t, 8 * at : 8 * (at + 1), :] = final[:, 128 * t : 128 * (t + 1)]

    parts = []
    for i in range(3):
        for c in range(ncirc):
            both = [keep[2 * i + t, pl.ds(c, nrad, stride=8), :] for t in range(2)]
            plane = jnp.concatenate(both, axis=1)
            adjoint[i, c] = plane
            parts.append(plane)
    lines = ncirc * nrad
    flat = jnp.concatenate(parts, axis=0)
    high, low = split(flat)
    table = jnp.concatenate([high, low], axis=0).astype(BF16)
    node = ids[...]
    cell = lax.broadcasted_iota(jnp.int32, (256, node.shape[1]), 0)
    pick = jnp.where(cell == node % 256, 1.0, 0.0).astype(BF16)
    rows = jnp.dot(table, pick, preferred_element_type=F32)
    rows = rows[: 3 * lines] + rows[3 * lines :]
    line = lax.broadcasted_iota(jnp.int32, (lines, node.shape[1]), 0)
    hit = line == node // 256
    picked = [
        jnp.sum(jnp.where(hit, rows[lines * i : lines * (i + 1)], 0.0), axis=0, keepdims=True)
        for i in range(3)
    ]
    weighted = sum(shapes[i] * picked[i] for i in range(3))
    sums_of[...] = jnp.broadcast_to(jnp.sum(weighted, axis=1, keepdims=True), sums_of.shape)
    owned = sums_of.shape[0] // devices
    lane = lax.broadcasted_iota(jnp.int32, (devices, 128), 1)
    out = jnp.zeros((devices, 128), F32)
    for j in range(owned):
        out = jnp.where(lane == j, sums_of[pl.ds(j, devices, stride=owned), :], out)
    for r in range(force.shape[0] // devices):
        force[devices * r : devices * (r + 1), 0, :] = out


def swaps(axis, start, wrap):
    count = lax.axis_size(axis)
    pairs = []
    for i in range(start, count, 2):
        j = (i + 1) % count
        if j > i or wrap:
            pairs += [(i, j), (j, i)]
    return pairs


def call(kernel, outs, scratch=(), smem=0, ins=0):
    spec = [pl.BlockSpec(memory_space=pltpu.SMEM)] * smem + [pl.BlockSpec(memory_space=pltpu.VMEM)] * ins
    return pl.pallas_call(
        kernel,
        out_shape=[jax.ShapeDtypeStruct(o, F32) for o in outs],
        in_specs=spec,
        out_specs=[pl.BlockSpec(memory_space=pltpu.VMEM)] * len(outs),
        scratch_shapes=list(scratch),
        compiler_params=pltpu.CompilerParams(vmem_limit_bytes=48 * 1024 * 1024),
    )


def on_device(
    adjoint_prev, cell_class, class_moduli, flow_sens, flow_nodes, flow_count, surf_ids, mode_shapes
):
    _, ncirc, nrad, naxial = adjoint_prev.shape
    n_mode, n_rad = lax.axis_size("mode"), lax.axis_size("rad")
    slots = flow_nodes.shape[-1]
    lines = ncirc * nrad
    cells = (ncirc, nrad, naxial)
    message = (24, 8, 128)
    send, e = call(
        pack_kernel,
        [(n_mode, 48, 128), cells],
        [pltpu.VMEM((128, n_mode * slots), BF16), pltpu.VMEM((2 * lines, n_mode * slots), BF16)],
        2, 4,
    )(class_moduli, flow_count[0, 0, 0], adjoint_prev, cell_class, jnp.swapaxes(flow_sens[0, 0, 0], 0, 1), flow_nodes[0, 0, 0])
    got = lax.all_to_all(send, "mode", split_axis=0, concat_axis=0, tiled=True)
    rhs, ends, first, second = call(
        scatter_kernel,
        [(3,) + cells, (ncirc, nrad, 128), message, message],
        [pltpu.VMEM((6 * lines, n_mode * slots), BF16), pltpu.VMEM((naxial, n_mode * slots), BF16)],
        0, 3,
    )(got, adjoint_prev, e)
    first = lax.ppermute(first, "circ", swaps("circ", 0, True))
    second = lax.ppermute(second, "circ", swaps("circ", 1, True))
    turned, first, second = call(turn_kernel, [(15, 8 * nrad, 128), message, message], (), 0, 6)(
        adjoint_prev, e, rhs, ends, first, second
    )
    first = lax.ppermute(first, "rad", swaps("rad", 0, False))
    second = lax.ppermute(second, "rad", swaps("rad", 1, False))
    modes = mode_shapes.shape[3]
    owned = modes // n_mode
    final, force = call(
        functools.partial(sweep_kernel, n_mode),
        [adjoint_prev.shape, (n_rad * n_mode, 1, 128)],
        [pltpu.VMEM((6, 8 * nrad, 128), F32), pltpu.VMEM((modes, 128), F32)],
        0, 5,
    )(turned, first, second, jnp.swapaxes(mode_shapes[0, 0, 0], 0, 1), surf_ids[0, 0])
    parts = lax.all_to_all(force, ("rad", "mode"), split_axis=0, concat_axis=0, tiled=True)
    own_force = jnp.sum(parts[:, 0, :owned], axis=0)
    return (final, own_force.reshape(owned, 1))


def solution(mesh):
    in_specs = (
        P(None, "circ", "rad", "mode"),
        P("circ", "rad", "mode"),
        P(),
        P("circ", "rad", "mode", None, None, None),
        P("circ", "rad", "mode", None, None),
        P("circ", "rad", "mode", None),
        P("circ", "rad", "mode", None),
        P("circ", "rad", "mode", None, None, None),
    )
    out_specs = (P(None, "circ", "rad", "mode"), P("mode", "circ"))
    return jax.shard_map(
        on_device, mesh=mesh, in_specs=in_specs, out_specs=out_specs, check_vma=False
    )
```

```python
import functools

import jax
import jax.numpy as jnp
from jax import lax
from jax.experimental import pallas as pl
from jax.experimental.pallas import tpu as pltpu
from jax.sharding import PartitionSpec as P

coupling = 0.5
relaxation = 0.6

face_own, face_other = 0.5 * (1.0 + coupling), 0.5
edge_own, edge_other = 0.25 * (1.0 + 0.5 * coupling), 0.25
corner_own = (1.0 + coupling / 3.0) / 6.0
edge_cross = 0.25 * coupling / 2.0
corner_cross = coupling / 18.0
centre_weight = 2 * face_own + 4 * face_other + 8 * edge_own + 4 * edge_other + 8 * corner_own

F32 = jnp.float32
BF16 = jnp.bfloat16
NT = (((1,), (1,)), ((), ()))


def split(x):
    high = x.astype(BF16).astype(F32)
    return high, x - high


def pack_kernel(
    moduli_in, count_in, prev_in, cls_in, sens_in, nodes_in, send, e_out,
    values, hits, moduli, count, prev, cls, sens, nodes, sems,
):
    copies = [
        pltpu.make_async_copy(source, target, sems.at[i])
        for i, (source, target) in enumerate(
            (
                (sens_in, sens), (nodes_in, nodes), (prev_in, prev), (cls_in, cls),
                (count_in, count), (moduli_in, moduli),
            )
        )
    ]
    for copy in copies:
        copy.start()
    values[...] = jnp.zeros(values.shape, BF16)
    for copy in copies:
        copy.wait()
    _, blocks, slots = sens.shape
    ncirc, nrad, naxial = cls.shape
    lines = ncirc * nrad
    k = lax.axis_index("mode")
    lane = lax.broadcasted_iota(jnp.int32, (nrad, 128), 1)
    to_low, to_high = [], []
    for c in range(ncirc):
        level = cls[c]
        e = jnp.zeros(level.shape, F32)
        for i in range(moduli.shape[0]):
            e = jnp.where(level == i, moduli[i], e)
        e_out[c] = e
        low = jnp.zeros((nrad, 128), F32)
        high = jnp.zeros((nrad, 128), F32)
        for f in range(4):
            field = prev[f, c] if f < 3 else e
            first = pltpu.roll(field[:, :128], 4 * f + 2, 1)
            last = pltpu.roll(field[:, naxial - 128 :], 4 * f + 2, 1)
            low = jnp.where((lane == 4 * f + 2) | (lane == 4 * f + 3), first, low)
            high = jnp.where((lane == 4 * f) | (lane == 4 * f + 1), last, high)
        to_low.append(low)
        to_high.append(high)

    slot = lax.broadcasted_iota(jnp.int32, (3, slots), 1)
    row = lax.broadcasted_iota(jnp.int32, (16, slots), 0)
    place = lax.broadcasted_iota(jnp.int32, (2 * lines, slots), 0)
    for d in range(blocks):
        vals = jnp.concatenate([sens[i, d : d + 1] for i in range(3)], axis=0)
        vals = jnp.where(slot < count[d], vals, 0.0)
        node = nodes[d : d + 1]
        for q in range(slots // 128):
            cut = slice(128 * q, 128 * (q + 1))
            send[d, 4 * q : 4 * q + 3, :] = vals[:, cut]
            send[d, 4 * q + 3 : 4 * q + 4, :] = node[:, cut].astype(F32)
        high, low = split(vals)
        tile = jnp.zeros((16, slots), F32)
        for i in range(3):
            tile = jnp.where(row == 2 * i, high[i : i + 1], tile)
            tile = jnp.where(row == 8 + 2 * i, low[i : i + 1], tile)
        values[16 * d : 16 * (d + 1), slots * d : slots * (d + 1)] = tile.astype(BF16)
        axial = node % naxial
        line = node // naxial
        key = jnp.where(axial == 0, line, jnp.where(axial == naxial - 1, line + lines, -1))
        hits[:, slots * d : slots * (d + 1)] = jnp.where(key == place, 1.0, 0.0).astype(BF16)

    planes = lax.dot_general(hits[...], values[...], NT, preferred_element_type=F32)
    planes = planes + pltpu.roll(planes, 120, 1)
    wide = lax.broadcasted_iota(jnp.int32, (lines, 128), 1)
    even = (wide == 16) | (wide == 18) | (wide == 20)
    odd = (wide == 17) | (wide == 19) | (wide == 21)
    for d in range(blocks):
        beside = jnp.zeros((lines, 128), F32)
        if d + 1 < blocks:
            moved = pltpu.roll(planes[:lines], (17 - 16 * (d + 1)) % 128, 1)
            beside = jnp.where(odd, moved, beside)
        if d > 0:
            moved = pltpu.roll(planes[lines:], (16 - 16 * (d - 1)) % 128, 1)
            beside = jnp.where(even, moved, beside)
        for c in range(ncirc):
            out = beside[nrad * c : nrad * (c + 1)]
            out = out + jnp.where(k == d + 1, to_low[c], 0.0) + jnp.where(k == d - 1, to_high[c], 0.0)
            send[d, 16 + nrad * c : 16 + nrad * (c + 1), :] = out


def scatter_kernel(got, prev, e, rhs, ends, first, second, left, right):
    blocks = got.shape[0]
    _, ncirc, nrad, naxial = prev.shape
    lines = ncirc * nrad
    row = lax.broadcasted_iota(jnp.int32, (lines, 128), 0)
    cell = lax.broadcasted_iota(jnp.int32, (naxial, 128), 0)
    for d in range(blocks):
        for q in range(4):
            cut = slice(128 * (4 * d + q), 128 * (4 * d + q + 1))
            node = got[d, 4 * q + 3 : 4 * q + 4, :].astype(jnp.int32)
            right[:, cut] = jnp.where(cell == node % naxial, 1.0, 0.0).astype(BF16)
            hit = row == node // naxial
            for i in range(3):
                for j, part in enumerate(split(got[d, 4 * q + i : 4 * q + i + 1, :])):
                    at = lines * (2 * i + j)
                    left[at : at + lines, cut] = jnp.where(hit, part, 0.0).astype(BF16)
    dense = lax.dot_general(left[...], right[...], NT, preferred_element_type=F32)
    for i in range(3):
        total = dense[2 * lines * i : 2 * lines * i + lines] + dense[2 * lines * i + lines : 2 * lines * (i + 1)]
        for c in range(ncirc):
            rhs[i, c] = total[nrad * c : nrad * (c + 1)]
    for c in range(ncirc):
        at = slice(16 + nrad * c, 16 + nrad * (c + 1))
        total = got[0, at, :]
        for d in range(1, blocks):
            total = total + got[d, at, :]
        ends[c] = total
    odd = lax.axis_index("circ") % 2
    for out, at_high in ((first, 1 - odd), (second, odd)):
        base = at_high * (ncirc - 2)
        edge = at_high * (ncirc - 1)
        for t in range(2):
            cut = slice(128 * t, 128 * (t + 1))
            for f in range(4):
                for j in range(2):
                    source = prev[f, base + j] if f < 3 else e[base + j]
                    out[4 * f + 2 * t + j] = source[:, cut]
            for i in range(3):
                out[16 + 2 * i + t] = rhs[i, edge][:, cut]
        for j in range(2):
            out[22 + j] = ends[base + j]


def turn_kernel(prev, e, rhs, ends, got_second, got_first, turned, first, second):
    _, ncirc, nrad, _ = prev.shape
    odd_circ = lax.axis_index("circ") % 2 == 1

    def put(index, c, plane):
        turned[index, pl.ds(c, nrad, stride=8), :] = plane

    for c in range(ncirc):
        for t in range(2):
            cut = slice(128 * t, 128 * (t + 1))
            for f in range(4):
                source = prev[f, c] if f < 3 else e[c]
                put(2 * f + t, c, source[:, cut])
            for i in range(3):
                put(8 + 2 * i + t, c, rhs[i, c][:, cut])
        put(14, c, ends[c])

    def sides(tile):
        a, b = got_first[tile], got_second[tile]
        return jnp.where(odd_circ, a, b), jnp.where(odd_circ, b, a)

    for index in range(8):
        for j in range(2):
            low, high = sides(2 * index + j)
            put(index, 6 + j, low)
            put(index, 4 + j, high)
    for index in range(6):
        low, high = sides(16 + index)
        put(8 + index, 7, low)
        put(8 + index, 4, high)
        put(8 + index, 6, low)
        put(8 + index, 5, high)
    for j in range(2):
        low, high = sides(22 + j)
        put(14, 6 + j, low)
        put(14, 4 + j, high)

    odd = lax.axis_index("rad") % 2
    for out, at_high in ((first, 1 - odd), (second, odd)):
        for index in range(15):
            for j in range(2):
                plane = at_high * (nrad - 2) + j
                at = 2 * index + j
                if 8 <= index < 14:
                    if j:
                        continue
                    plane = at_high * (nrad - 1)
                    at = 16 + index - 8
                elif index == 14:
                    at = 22 + j
                out[at] = turned[index, pl.ds(pl.multiple_of(8 * plane, 8), 8), :]


def sums(x):
    up = pltpu.roll(x, x.shape[1] - 1, 1)
    down = pltpu.roll(x, 1, 1)
    return up + down, up - down


def across(x):
    up = pltpu.roll(x, 7, 0)
    down = pltpu.roll(x, 1, 0)
    return up + down, up - down


def spread(x):
    sn, dn = sums(x)
    sm, dm = across(x)
    smsn, dmsn = across(sn)
    smdn, dmdn = across(dn)
    return sn, dn, sm, dm, smsn, dmsn, smdn, dmdn


def leading_terms(x, s):
    sn, _, sm, _, both = s[0], s[1], s[2], s[3], s[4]
    near = sm + sn
    return face_other * near + edge_other * both, face_own * x + edge_own * near + corner_own * both


def plane_terms(x, own, other, both):
    centre = face_own * own + face_other * other + edge_own * both
    side = face_other * x + edge_own * own + edge_other * other + corner_own * both
    return centre, side


def cross_terms(s):
    _, dn, _, dm, _, dmsn, smdn, dmdn = s
    return edge_cross * dm + corner_cross * dmsn, edge_cross * dn + corner_cross * smdn, dmdn


def vector_terms(v):
    s0, s1, s2 = spread(v[0]), spread(v[1]), spread(v[2])
    p0, q0 = plane_terms(v[0], s0[2], s0[0], s0[4])
    p1, q1 = leading_terms(v[1], s1)
    p2, q2 = plane_terms(v[2], s2[0], s2[2], s2[4])
    rm0, _, w0 = cross_terms(s0)
    rm1, rn1, _ = cross_terms(s1)
    _, rn2, w2 = cross_terms(s2)
    p0 = p0 + edge_cross * w2
    q0 = q0 + corner_cross * w2
    p2 = p2 + edge_cross * w0
    q2 = q2 + corner_cross * w0
    d0, d1, d2 = rm1, rm0 + rn2, rn1
    return (p0, p1, p2), (q0 + d0, q1 + d1, q2 + d2), (q0 - d0, q1 - d1, q2 - d2)


def scalar_terms(e):
    s = spread(e)
    p0, q0 = plane_terms(e, s[2], s[0], s[4])
    p1, q1 = leading_terms(e, s)
    p2, q2 = plane_terms(e, s[0], s[2], s[4])
    rm, rn, w = cross_terms(s)
    return (p0, p1, p2), (q0, q1, q2), rm, rn, w


def moved(v, e):
    plain, scaled = vector_terms(v), vector_terms([e * x for x in v])
    return [list(plain[j]) + list(scaled[j]) for j in range(3)]


def weighed(e):
    p, q, rm, rn, w = scalar_terms(e)
    zero = jnp.zeros_like(w)
    side = corner_cross * w
    return [
        list(p) + [zero, zero, edge_cross * w],
        list(q) + [rm, rn, side],
        list(q) + [-rm, -rn, side],
    ]


def plus(*parts):
    return [functools.reduce(lambda a, b: a + b, column) for column in zip(*parts)]


def stiffness(e, part):
    diag = [centre_weight * e + x for x in part[:3]]
    return diag, [relaxation / x for x in diag], part[3], part[4], part[5]


def remainder(v, e, rhs, stiff, part):
    (d0, d1, d2), _, c01, c12, c02 = stiff
    own = (
        d0 * v[0] + c01 * v[1] + c02 * v[2],
        c01 * v[0] + d1 * v[1] + c12 * v[2],
        c02 * v[0] + c12 * v[1] + d2 * v[2],
    )
    return [rhs[i] - own[i] + e * part[i] + part[3 + i] for i in range(3)]


def relaxed(v, stiff, rest):
    return [v[i] + stiff[1][i] * rest[i] for i in range(3)]


def outside_mask():
    lane = lax.broadcasted_iota(jnp.int32, (8, 384), 1)
    mode = lax.axis_index("mode")
    return ((lane == 383) & (mode == 0)) | ((lane == 256) & (mode == lax.axis_size("mode") - 1))


def own_tile(turned, index, plane):
    return turned[index, 8 * plane : 8 * (plane + 1), :]


def field_of(tile, f, ends):
    shift = 4 * f + 2 if f < 4 else 17 + 2 * (f - 4)
    return jnp.concatenate([tile(2 * f), tile(2 * f + 1), pltpu.roll(ends, 128 - shift, 1)], axis=1)


def cells_of(turned, plane, first, last):
    tile = lambda index: own_tile(turned, index, plane)
    ends = tile(14)
    return [field_of(tile, f, ends) for f in range(first, last)]


def put_final(keep, plane, final):
    for i in range(3):
        for t in range(2):
            keep[2 * i + t, 8 * plane : 8 * (plane + 1), :] = final[i][:, 128 * t : 128 * (t + 1)]


BEYOND, EDGE, CARRY, REST, HELD, SCALE, COUNT = 0, 12, 24, 30, 33, 36, 39
OWN, DOWN, UP = 0, 1, 2


def inner_kernel(turned, ids, left, keep, pick, nodes, sem):
    nrad = turned.shape[1] // 8
    copy = pltpu.make_async_copy(ids, nodes, sem)
    copy.start()
    outside = outside_mask()
    last = nrad - 1
    adds, middle, stiff = {}, {}, {}

    def leave(side, at, arrays):
        for j, x in enumerate(arrays):
            left[side, at + j] = x

    for plane in range(nrad):
        v, e = cells_of(turned, plane, 0, 3), cells_of(turned, plane, 3, 4)[0]
        adds[plane] = [a + b for a, b in zip(moved(v, e), weighed(e))]
        if plane == 0:
            leave(0, BEYOND, adds[0][DOWN])
        if plane == 1:
            leave(0, EDGE, plus(adds[0][OWN], adds[1][DOWN]))
        if plane == last:
            leave(1, EDGE, plus(adds[last][OWN], adds[last - 1][UP]))
            leave(1, BEYOND, adds[last][UP])
        at = plane - 1
        if at < 1:
            continue
        v, e = cells_of(turned, at, 0, 3), cells_of(turned, at, 3, 4)[0]
        part = plus(adds[at - 1][UP], adds[at][OWN], adds[at + 1][DOWN])
        stiff[at] = stiffness(e, part[6:])
        rest = remainder(v, e, cells_of(turned, at, 4, 7), stiff[at], part)
        middle[at] = [jnp.where(outside, 0.0, x) for x in relaxed(v, stiff[at], rest)]

    adds = {}
    for plane in range(1, last):
        e = cells_of(turned, plane, 3, 4)[0]
        adds[plane] = moved(middle[plane], e)
        if plane == 1:
            leave(0, CARRY, adds[1][DOWN])
        if plane == last - 1:
            leave(1, CARRY, adds[last - 1][UP])
        for at in (plane - 1, plane):
            if at < 1 or (at == plane and plane < last - 1):
                continue
            beside = []
            if at - 1 in adds:
                beside.append(adds[at - 1][UP])
            if at + 1 in adds:
                beside.append(adds[at + 1][DOWN])
            part = plus(adds[at][OWN], *beside)
            v, e = middle[at], cells_of(turned, at, 3, 4)[0]
            rest = remainder(v, e, cells_of(turned, at, 4, 7), stiff[at], part)
            if len(beside) == 2:
                put_final(keep, at, relaxed(v, stiff[at], rest))
            else:
                side = 0 if at == 1 else 1
                leave(side, REST, rest)
                leave(side, HELD, v)
                leave(side, SCALE, stiff[at][1])
    copy.wait()
    cell = lax.broadcasted_iota(jnp.int32, pick.shape, 0)
    pick[...] = jnp.where(cell == nodes[...] % 256, 1.0, 0.0).astype(BF16)


def sweep_kernel(
    devices, turned, got_second, got_first, left, kept, pick, ids, shapes_in,
    adjoint, force, keep, sums_of, shapes, sem,
):
    copy = pltpu.make_async_copy(shapes_in, shapes, sem)
    copy.start()
    nrad = turned.shape[1] // 8
    ncirc = adjoint.shape[1]
    rad = lax.axis_index("rad")
    odd = rad % 2 == 1
    outside = outside_mask()

    def halo(side, j, first, last):
        def tile(index):
            if index == 14:
                at = 22 + j
            elif index >= 8:
                at = 16 + index - 8
            else:
                at = 2 * index + j
            a, b = got_first[at], got_second[at]
            return jnp.where(odd, b, a) if side else jnp.where(odd, a, b)

        ends = tile(14)
        return [field_of(tile, f, ends) for f in range(first, last)]

    def handed(side, at, count):
        return [left[side, at + j] for j in range(count)]

    for side in range(2):
        inward = DOWN if side else UP
        near, far = (0, 1) if side else (1, 0)
        edge, next_in = (nrad - 1, nrad - 2) if side else (0, 1)
        v, e = halo(side, far, 0, 3), halo(side, far, 3, 4)[0]
        beyond = moved(v, e)[inward] + weighed(e)[inward]
        v, e = halo(side, near, 0, 3), halo(side, near, 3, 4)[0]
        here = [a + b for a, b in zip(moved(v, e), weighed(e))]
        part = plus(handed(side, BEYOND, 12), here[OWN], beyond)
        stiff = stiffness(e, part[6:])
        rest = remainder(v, e, halo(side, near, 4, 7), stiff, part)
        drop = outside | (rad == (lax.axis_size("rad") - 1 if side else 0))
        beside = moved([jnp.where(drop, 0.0, x) for x in relaxed(v, stiff, rest)], e)

        v, e = cells_of(turned, edge, 0, 3), cells_of(turned, edge, 3, 4)[0]
        rhs = cells_of(turned, edge, 4, 7)
        part = plus(handed(side, EDGE, 12), here[inward])
        stiff = stiffness(e, part[6:])
        v = [jnp.where(outside, 0.0, x) for x in relaxed(v, stiff, remainder(v, e, rhs, stiff, part))]
        here = moved(v, e)
        part = plus(handed(side, CARRY, 6), here[OWN], beside[inward])
        put_final(keep, edge, relaxed(v, stiff, remainder(v, e, rhs, stiff, part)))

        e = cells_of(turned, next_in, 3, 4)[0]
        add, rest = here[inward], handed(side, REST, 3)
        v, scale = handed(side, HELD, 3), handed(side, SCALE, 3)
        put_final(
            keep, next_in, [v[i] + scale[i] * (rest[i] + e * add[i] + add[3 + i]) for i in range(3)]
        )

    inside = slice(16, 8 * (nrad - 2))
    for index in range(6):
        keep[index, inside, :] = kept[index, inside, :]
    parts = []
    for i in range(3):
        for c in range(ncirc):
            both = [keep[2 * i + t, pl.ds(c, nrad, stride=8), :] for t in range(2)]
            plane = jnp.concatenate(both, axis=1)
            adjoint[i, c] = plane
            parts.append(plane)
    lines = ncirc * nrad
    flat = jnp.concatenate(parts, axis=0)
    high, low = split(flat)
    table = jnp.concatenate([high, low], axis=0).astype(BF16)
    node = ids[...]
    rows = jnp.dot(table, pick[...], preferred_element_type=F32)
    rows = rows[: 3 * lines] + rows[3 * lines :]
    line = lax.broadcasted_iota(jnp.int32, (lines, node.shape[1]), 0)
    hit = line == node // 256
    picked = [
        jnp.sum(jnp.where(hit, rows[lines * i : lines * (i + 1)], 0.0), axis=0, keepdims=True)
        for i in range(3)
    ]
    copy.wait()
    weighted = sum(shapes[i] * picked[i] for i in range(3))
    sums_of[...] = jnp.broadcast_to(jnp.sum(weighted, axis=1, keepdims=True), sums_of.shape)
    owned = sums_of.shape[0] // devices
    lane = lax.broadcasted_iota(jnp.int32, (devices, 128), 1)
    out = jnp.zeros((devices, 128), F32)
    for j in range(owned):
        out = jnp.where(lane == j, sums_of[pl.ds(j, devices, stride=owned), :], out)
    for r in range(force.shape[0] // devices):
        force[devices * r : devices * (r + 1), 0, :] = out


def swaps(axis, start, wrap):
    count = lax.axis_size(axis)
    pairs = []
    for i in range(start, count, 2):
        j = (i + 1) % count
        if j > i or wrap:
            pairs += [(i, j), (j, i)]
    return pairs


VMEM = pl.BlockSpec(memory_space=pltpu.VMEM)
HBM = pl.BlockSpec(memory_space=pltpu.HBM)


def call(kernel, ins, outs, scratch=(), flops=1_000_000, limit=40 * 1024 * 1024):
    outs = [o if isinstance(o, jax.ShapeDtypeStruct) else jax.ShapeDtypeStruct(o, F32) for o in outs]
    return pl.pallas_call(
        kernel,
        out_shape=outs,
        in_specs=ins,
        out_specs=[VMEM] * len(outs),
        scratch_shapes=list(scratch),
        compiler_params=pltpu.CompilerParams(vmem_limit_bytes=limit),
        cost_estimate=pl.CostEstimate(flops=flops, bytes_accessed=1_000_000, transcendentals=0),
    )


def on_device(
    adjoint_prev, cell_class, class_moduli, flow_sens, flow_nodes, flow_count, surf_ids, mode_shapes
):
    _, ncirc, nrad, naxial = adjoint_prev.shape
    n_mode, n_rad = lax.axis_size("mode"), lax.axis_size("rad")
    slots = flow_nodes.shape[-1]
    lines = ncirc * nrad
    cells = (ncirc, nrad, naxial)
    message = (24, 8, 128)
    args = (
        class_moduli, flow_count[0, 0, 0], adjoint_prev, cell_class,
        jnp.swapaxes(flow_sens[0, 0, 0], 0, 1), flow_nodes[0, 0, 0],
    )
    send, e = call(
        pack_kernel,
        [HBM] * 6,
        [(n_mode, 48, 128), cells],
        [pltpu.VMEM((128, n_mode * slots), BF16), pltpu.VMEM((2 * lines, n_mode * slots), BF16)]
        + [pltpu.SMEM(x.shape, x.dtype) for x in args[:2]]
        + [pltpu.VMEM(x.shape, x.dtype) for x in args[2:]]
        + [pltpu.SemaphoreType.DMA((6,))],
        limit=63 * 1024 * 1024 + 512 * 1024,
    )(*args)
    got = lax.all_to_all(send, "mode", split_axis=0, concat_axis=0, tiled=True)
    rhs, ends, first, second = call(
        scatter_kernel,
        [VMEM] * 3,
        [(3,) + cells, (ncirc, nrad, 128), message, message],
        [pltpu.VMEM((6 * lines, n_mode * slots), BF16), pltpu.VMEM((naxial, n_mode * slots), BF16)],
    )(got, adjoint_prev, e)
    second = lax.ppermute(second, "circ", swaps("circ", 1, True))
    first = lax.ppermute(first, "circ", swaps("circ", 0, True))
    turned, first, second = call(turn_kernel, [VMEM] * 6, [(15, 8 * nrad, 128), message, message])(
        adjoint_prev, e, rhs, ends, second, first
    )
    second = lax.ppermute(second, "rad", swaps("rad", 1, False))
    first = lax.ppermute(first, "rad", swaps("rad", 0, False))
    modes = mode_shapes.shape[3]
    owned = modes // n_mode
    ids = surf_ids[0, 0]
    shapes = jnp.swapaxes(mode_shapes[0, 0, 0], 0, 1)
    kept = (6, 8 * nrad, 128)
    left, keep, pick = call(
        inner_kernel,
        [VMEM, HBM],
        [(2, COUNT, 8, 384), kept, jax.ShapeDtypeStruct((naxial, ids.shape[1]), BF16)],
        [pltpu.VMEM(ids.shape, ids.dtype), pltpu.SemaphoreType.DMA],
        flops=10_000_000,
    )(turned, ids)
    final, force = call(
        functools.partial(sweep_kernel, n_mode),
        [VMEM] * 7 + [HBM],
        [adjoint_prev.shape, (n_rad * n_mode, 1, 128)],
        [
            pltpu.VMEM(kept, F32), pltpu.VMEM((modes, 128), F32),
            pltpu.VMEM(shapes.shape, F32), pltpu.SemaphoreType.DMA,
        ],
    )(turned, second, first, left, keep, pick, ids, shapes)
    parts = lax.all_to_all(force, ("rad", "mode"), split_axis=0, concat_axis=0, tiled=True)
    own_force = jnp.sum(parts[:, 0, :owned], axis=0)
    return (final, own_force.reshape(owned, 1))


def solution(mesh):
    in_specs = (
        P(None, "circ", "rad", "mode"),
        P("circ", "rad", "mode"),
        P(),
        P("circ", "rad", "mode", None, None, None),
        P("circ", "rad", "mode", None, None),
        P("circ", "rad", "mode", None),
        P("circ", "rad", "mode", None),
        P("circ", "rad", "mode", None, None, None),
    )
    out_specs = (P(None, "circ", "rad", "mode"), P("mode", "circ"))
    return jax.shard_map(
        on_device, mesh=mesh, in_specs=in_specs, out_specs=out_specs, check_vma=False
    )
```

```python
import functools

import jax
import jax.numpy as jnp
from jax import lax
from jax.experimental import pallas as pl
from jax.experimental.pallas import tpu as pltpu
from jax.sharding import PartitionSpec as P

coupling = 0.5
relaxation = 0.6

face_own, face_other = 0.5 * (1.0 + coupling), 0.5
edge_own, edge_other = 0.25 * (1.0 + 0.5 * coupling), 0.25
corner_own = (1.0 + coupling / 3.0) / 6.0
edge_cross = 0.25 * coupling / 2.0
corner_cross = coupling / 18.0
centre_weight = 2 * face_own + 4 * face_other + 8 * edge_own + 4 * edge_other + 8 * corner_own

F32 = jnp.float32
BF16 = jnp.bfloat16
NT = (((1,), (1,)), ((), ()))


def split(x):
    high = x.astype(BF16).astype(F32)
    return high, x - high


def pack_kernel(
    moduli_in, count_in, prev_in, cls_in, sens_in, nodes_in, send, e_out,
    moduli, count, prev, cls, sens, nodes, sems,
):
    copies = [
        pltpu.make_async_copy(source, target, sems.at[i])
        for i, (source, target) in enumerate(
            (
                (sens_in, sens), (nodes_in, nodes), (prev_in, prev), (cls_in, cls),
                (count_in, count), (moduli_in, moduli),
            )
        )
    ]
    for copy in copies:
        copy.start()
    for copy in copies:
        copy.wait()
    _, blocks, slots = sens.shape
    ncirc, nrad, naxial = cls.shape
    lines = ncirc * nrad
    k = lax.axis_index("mode")
    lane = lax.broadcasted_iota(jnp.int32, (nrad, 128), 1)
    columns = []
    for c in range(ncirc):
        level = cls[c]
        e = jnp.zeros(level.shape, F32)
        for i in range(moduli.shape[0]):
            e = jnp.where(level == i, moduli[i], e)
        e_out[c] = e
        ends = jnp.zeros((nrad, 128), F32)
        for f in range(4):
            field = prev[f, c] if f < 3 else e
            first = pltpu.roll(field[:, :128], 4 * f + 2, 1)
            last = pltpu.roll(field[:, naxial - 128 :], 4 * f + 2, 1)
            ends = jnp.where((lane == 4 * f + 2) | (lane == 4 * f + 3), first, ends)
            ends = jnp.where((lane == 4 * f) | (lane == 4 * f + 1), last, ends)
        columns.append(ends)
    columns.append(jnp.zeros((128 - lines, 128), F32))
    items = jnp.concatenate(columns, axis=0).T
    halo = items[:8] + pltpu.roll(items[8:16], 32, 1)
    tall = lax.broadcasted_iota(jnp.int32, (8, 128), 0)
    to_high = jnp.where(tall % 4 < 2, halo, 0.0)
    to_low = halo - to_high

    node = nodes[...]
    axial, line = node % naxial, node // naxial
    key = jnp.where(axial == 0, line, jnp.where(axial == naxial - 1, line + lines, -1))
    key = key.astype(F32).astype(BF16)
    place = lax.broadcasted_iota(jnp.int32, (2 * lines, slots), 0).astype(F32).astype(BF16)
    slot = lax.broadcasted_iota(jnp.int32, (1, slots), 1)
    row = lax.broadcasted_iota(jnp.int32, (16, slots), 0) // 2
    zero, one = BF16(0.0), BF16(1.0)
    planes = []
    for d in range(blocks):
        live = slot < count[d]
        tile = jnp.zeros((16, slots), F32)
        for i in range(3):
            value = jnp.where(live, sens[i, d : d + 1], 0.0)
            for q in range(slots // 128):
                send[d, 4 * (i + 1) + q : 4 * (i + 1) + q + 1, :] = value[:, 128 * q : 128 * (q + 1)]
            high, low = split(value)
            tile = jnp.where(row == i, high, jnp.where(row == 4 + i, low, tile))
        for q in range(slots // 128):
            send[d, q : q + 1, :] = node[d : d + 1, 128 * q : 128 * (q + 1)].astype(F32)
        hits = jnp.where(place == jnp.broadcast_to(key[d : d + 1], place.shape), one, zero)
        plane = lax.dot_general(tile.astype(BF16), hits, NT, preferred_element_type=F32)
        plane = jnp.concatenate([plane[:8] + plane[8:], jnp.zeros((8, 128 - 2 * lines), F32)], axis=1)
        planes.append(plane)
    group = lax.broadcasted_iota(jnp.int32, (8, 128), 1) // lines == 2
    even, odd = group & (tall % 2 == 0), group & (tall % 2 == 1)
    for d in range(blocks):
        out = jnp.where(k == d + 1, to_low, 0.0) + jnp.where(k == d - 1, to_high, 0.0)
        if d + 1 < blocks:
            out = jnp.where(odd, pltpu.roll(planes[d + 1], 2 * lines, 1), out)
        if d > 0:
            out = jnp.where(even, pltpu.roll(planes[d - 1], lines, 1), out)
        send[d, 16:24, :] = out


def scatter_kernel(got, prev, e, rhs, ends, first, second):
    blocks = got.shape[0]
    _, ncirc, nrad, naxial = prev.shape
    lines = ncirc * nrad
    row = lax.broadcasted_iota(jnp.int32, (lines, 128), 0).astype(F32).astype(BF16)
    cell = lax.broadcasted_iota(jnp.int32, (128, naxial), 1).astype(F32).astype(BF16)
    nodes = jnp.concatenate([got[d, :4, :] for d in range(blocks)], axis=0).astype(jnp.int32)
    line = (nodes // naxial).astype(F32).astype(BF16)
    tall = jnp.concatenate([nodes % naxial, jnp.zeros((128 - 4 * blocks, 128), jnp.int32)], axis=0)
    tall = tall.astype(F32).T.astype(BF16)
    zero, one = BF16(0.0), BF16(1.0)
    dense = jnp.zeros((6 * lines, naxial), F32)
    for d in range(blocks):
        left, right = [], []
        for q in range(4):
            g = 4 * d + q
            at = jnp.broadcast_to(tall[:, g : g + 1], cell.shape)
            right.append(jnp.where(cell == at, one, zero))
            hit = row == jnp.broadcast_to(line[g : g + 1], row.shape)
            column = []
            for i in range(3):
                for part in split(got[d, 4 * (i + 1) + q : 4 * (i + 1) + q + 1, :]):
                    column.append(jnp.where(hit, jnp.broadcast_to(part.astype(BF16), row.shape), zero))
            left.append(jnp.concatenate(column, axis=0))
        left, right = jnp.concatenate(left, axis=1), jnp.concatenate(right, axis=0)
        dense = dense + jnp.dot(left, right, preferred_element_type=F32)
    for i in range(3):
        total = dense[2 * lines * i : 2 * lines * i + lines] + dense[2 * lines * i + lines : 2 * lines * (i + 1)]
        for c in range(ncirc):
            rhs[i, c] = total[nrad * c : nrad * (c + 1)]
    total = got[0, 16:24, :]
    for d in range(1, blocks):
        total = total + got[d, 16:24, :]
    groups = [total, pltpu.roll(total, 128 - lines, 1), pltpu.roll(total, 128 - 2 * lines, 1)]
    columns = jnp.concatenate(groups + [jnp.zeros((104, 128), F32)], axis=0).T
    for c in range(ncirc):
        ends[c] = columns[nrad * c : nrad * (c + 1)]
    odd = lax.axis_index("circ") % 2
    for out, at_high in ((first, 1 - odd), (second, odd)):
        base = at_high * (ncirc - 2)
        edge = at_high * (ncirc - 1)
        for t in range(2):
            cut = slice(128 * t, 128 * (t + 1))
            for f in range(4):
                for j in range(2):
                    source = prev[f, base + j] if f < 3 else e[base + j]
                    out[4 * f + 2 * t + j] = source[:, cut]
            for i in range(3):
                out[16 + 2 * i + t] = rhs[i, edge][:, cut]
        for j in range(2):
            out[22 + j] = ends[base + j]


def turn_kernel(prev, e, rhs, ends, got_first, got_second, turned, first, second):
    _, ncirc, nrad, _ = prev.shape
    odd_circ = lax.axis_index("circ") % 2 == 1

    def put(index, c, plane):
        turned[index, pl.ds(c, nrad, stride=8), :] = plane

    for c in range(ncirc):
        for t in range(2):
            cut = slice(128 * t, 128 * (t + 1))
            for f in range(4):
                source = prev[f, c] if f < 3 else e[c]
                put(2 * f + t, c, source[:, cut])
            for i in range(3):
                put(8 + 2 * i + t, c, rhs[i, c][:, cut])
        put(14, c, ends[c])

    def sides(tile):
        a, b = got_first[tile], got_second[tile]
        return jnp.where(odd_circ, a, b), jnp.where(odd_circ, b, a)

    for index in range(8):
        for j in range(2):
            low, high = sides(2 * index + j)
            put(index, 6 + j, low)
            put(index, 4 + j, high)
    for index in range(6):
        low, high = sides(16 + index)
        put(8 + index, 7, low)
        put(8 + index, 4, high)
        put(8 + index, 6, low)
        put(8 + index, 5, high)
    for j in range(2):
        low, high = sides(22 + j)
        put(14, 6 + j, low)
        put(14, 4 + j, high)

    odd = lax.axis_index("rad") % 2
    for out, at_high in ((first, 1 - odd), (second, odd)):
        for index in range(15):
            for j in range(2):
                plane = at_high * (nrad - 2) + j
                at = 2 * index + j
                if 8 <= index < 14:
                    if j:
                        continue
                    plane = at_high * (nrad - 1)
                    at = 16 + index - 8
                elif index == 14:
                    at = 22 + j
                out[at] = turned[index, pl.ds(pl.multiple_of(8 * plane, 8), 8), :]


def sums(x):
    up = pltpu.roll(x, x.shape[1] - 1, 1)
    down = pltpu.roll(x, 1, 1)
    return up + down, up - down


def across(x):
    up = pltpu.roll(x, 7, 0)
    down = pltpu.roll(x, 1, 0)
    return up + down, up - down


def spread(x):
    sn, dn = sums(x)
    sm, dm = across(x)
    smsn, dmsn = across(sn)
    smdn, dmdn = across(dn)
    return sn, dn, sm, dm, smsn, dmsn, smdn, dmdn


def leading_terms(x, s):
    sn, _, sm, _, both = s[0], s[1], s[2], s[3], s[4]
    near = sm + sn
    return face_other * near + edge_other * both, face_own * x + edge_own * near + corner_own * both


def plane_terms(x, own, other, both):
    centre = face_own * own + face_other * other + edge_own * both
    side = face_other * x + edge_own * own + edge_other * other + corner_own * both
    return centre, side


def cross_terms(s):
    _, dn, _, dm, _, dmsn, smdn, dmdn = s
    return edge_cross * dm + corner_cross * dmsn, edge_cross * dn + corner_cross * smdn, dmdn


def vector_terms(v):
    s0, s1, s2 = spread(v[0]), spread(v[1]), spread(v[2])
    p0, q0 = plane_terms(v[0], s0[2], s0[0], s0[4])
    p1, q1 = leading_terms(v[1], s1)
    p2, q2 = plane_terms(v[2], s2[0], s2[2], s2[4])
    rm0, _, w0 = cross_terms(s0)
    rm1, rn1, _ = cross_terms(s1)
    _, rn2, w2 = cross_terms(s2)
    p0 = p0 + edge_cross * w2
    q0 = q0 + corner_cross * w2
    p2 = p2 + edge_cross * w0
    q2 = q2 + corner_cross * w0
    d0, d1, d2 = rm1, rm0 + rn2, rn1
    return (p0, p1, p2), (q0 + d0, q1 + d1, q2 + d2), (q0 - d0, q1 - d1, q2 - d2)


def scalar_terms(e):
    s = spread(e)
    p0, q0 = plane_terms(e, s[2], s[0], s[4])
    p1, q1 = leading_terms(e, s)
    p2, q2 = plane_terms(e, s[0], s[2], s[4])
    rm, rn, w = cross_terms(s)
    return (p0, p1, p2), (q0, q1, q2), rm, rn, w


def moved(v, e):
    plain, scaled = vector_terms(v), vector_terms([e * x for x in v])
    return [list(plain[j]) + list(scaled[j]) for j in range(3)]


def weighed(e):
    p, q, rm, rn, w = scalar_terms(e)
    zero = jnp.zeros_like(w)
    side = corner_cross * w
    return [
        list(p) + [zero, zero, edge_cross * w],
        list(q) + [rm, rn, side],
        list(q) + [-rm, -rn, side],
    ]


def plus(*parts):
    return [functools.reduce(lambda a, b: a + b, column) for column in zip(*parts)]


def stiffness(e, part):
    diag = [centre_weight * e + x for x in part[:3]]
    return diag, [relaxation / x for x in diag], part[3], part[4], part[5]


def remainder(v, e, rhs, stiff, part):
    (d0, d1, d2), _, c01, c12, c02 = stiff
    own = (
        d0 * v[0] + c01 * v[1] + c02 * v[2],
        c01 * v[0] + d1 * v[1] + c12 * v[2],
        c02 * v[0] + c12 * v[1] + d2 * v[2],
    )
    return [rhs[i] - own[i] + e * part[i] + part[3 + i] for i in range(3)]


def relaxed(v, stiff, rest):
    return [v[i] + stiff[1][i] * rest[i] for i in range(3)]


def outside_mask():
    lane = lax.broadcasted_iota(jnp.int32, (8, 384), 1)
    mode = lax.axis_index("mode")
    return ((lane == 383) & (mode == 0)) | ((lane == 256) & (mode == lax.axis_size("mode") - 1))


def own_tile(turned, index, plane):
    return turned[index, 8 * plane : 8 * (plane + 1), :]


def field_of(tile, f, ends):
    shift = 4 * f + 2 if f < 4 else 17 + 2 * (f - 4)
    return jnp.concatenate([tile(2 * f), tile(2 * f + 1), pltpu.roll(ends, 128 - shift, 1)], axis=1)


def cells_of(turned, plane, first, last):
    tile = lambda index: own_tile(turned, index, plane)
    ends = tile(14)
    return [field_of(tile, f, ends) for f in range(first, last)]


def put_final(keep, plane, final):
    for i in range(3):
        for t in range(2):
            keep[2 * i + t, 8 * plane : 8 * (plane + 1), :] = final[i][:, 128 * t : 128 * (t + 1)]


BEYOND, EDGE, CARRY, REST, HELD, SCALE, COUNT = 0, 12, 24, 30, 33, 36, 39
OWN, DOWN, UP = 0, 1, 2


def inner_kernel(turned, ids, left, keep, pick, nodes, sem):
    nrad = turned.shape[1] // 8
    copy = pltpu.make_async_copy(ids, nodes, sem)
    copy.start()
    outside = outside_mask()
    last = nrad - 1
    adds, middle, stiff = {}, {}, {}

    def leave(side, at, arrays):
        for j, x in enumerate(arrays):
            left[side, at + j] = x

    for plane in range(nrad):
        v, e = cells_of(turned, plane, 0, 3), cells_of(turned, plane, 3, 4)[0]
        adds[plane] = [a + b for a, b in zip(moved(v, e), weighed(e))]
        if plane == 0:
            leave(0, BEYOND, adds[0][DOWN])
        if plane == 1:
            leave(0, EDGE, plus(adds[0][OWN], adds[1][DOWN]))
        if plane == last:
            leave(1, EDGE, plus(adds[last][OWN], adds[last - 1][UP]))
            leave(1, BEYOND, adds[last][UP])
        at = plane - 1
        if at < 1:
            continue
        v, e = cells_of(turned, at, 0, 3), cells_of(turned, at, 3, 4)[0]
        part = plus(adds[at - 1][UP], adds[at][OWN], adds[at + 1][DOWN])
        stiff[at] = stiffness(e, part[6:])
        rest = remainder(v, e, cells_of(turned, at, 4, 7), stiff[at], part)
        middle[at] = [jnp.where(outside, 0.0, x) for x in relaxed(v, stiff[at], rest)]

    adds = {}
    for plane in range(1, last):
        e = cells_of(turned, plane, 3, 4)[0]
        adds[plane] = moved(middle[plane], e)
        if plane == 1:
            leave(0, CARRY, adds[1][DOWN])
        if plane == last - 1:
            leave(1, CARRY, adds[last - 1][UP])
        for at in (plane - 1, plane):
            if at < 1 or (at == plane and plane < last - 1):
                continue
            beside = []
            if at - 1 in adds:
                beside.append(adds[at - 1][UP])
            if at + 1 in adds:
                beside.append(adds[at + 1][DOWN])
            part = plus(adds[at][OWN], *beside)
            v, e = middle[at], cells_of(turned, at, 3, 4)[0]
            rest = remainder(v, e, cells_of(turned, at, 4, 7), stiff[at], part)
            if len(beside) == 2:
                put_final(keep, at, relaxed(v, stiff[at], rest))
            else:
                side = 0 if at == 1 else 1
                leave(side, REST, rest)
                leave(side, HELD, v)
                leave(side, SCALE, stiff[at][1])
    copy.wait()
    cell = lax.broadcasted_iota(jnp.int32, pick.shape, 0)
    pick[...] = jnp.where(cell == nodes[...] % 256, 1.0, 0.0).astype(BF16)


def sweep_kernel(
    devices, turned, got_second, got_first, left, kept, pick, ids, shapes,
    adjoint, force, keep, sums_of, result, sem,
):
    nrad = turned.shape[1] // 8
    ncirc = result.shape[1]
    rad = lax.axis_index("rad")
    odd = rad % 2 == 1
    outside = outside_mask()

    def halo(side, j, first, last):
        def tile(index):
            if index == 14:
                at = 22 + j
            elif index >= 8:
                at = 16 + index - 8
            else:
                at = 2 * index + j
            a, b = got_first[at], got_second[at]
            return jnp.where(odd, b, a) if side else jnp.where(odd, a, b)

        ends = tile(14)
        return [field_of(tile, f, ends) for f in range(first, last)]

    def handed(side, at, count):
        return [left[side, at + j] for j in range(count)]

    for side in range(2):
        inward = DOWN if side else UP
        near, far = (0, 1) if side else (1, 0)
        edge, next_in = (nrad - 1, nrad - 2) if side else (0, 1)
        v, e = halo(side, far, 0, 3), halo(side, far, 3, 4)[0]
        beyond = moved(v, e)[inward] + weighed(e)[inward]
        v, e = halo(side, near, 0, 3), halo(side, near, 3, 4)[0]
        here = [a + b for a, b in zip(moved(v, e), weighed(e))]
        part = plus(handed(side, BEYOND, 12), here[OWN], beyond)
        stiff = stiffness(e, part[6:])
        rest = remainder(v, e, halo(side, near, 4, 7), stiff, part)
        drop = outside | (rad == (lax.axis_size("rad") - 1 if side else 0))
        beside = moved([jnp.where(drop, 0.0, x) for x in relaxed(v, stiff, rest)], e)

        v, e = cells_of(turned, edge, 0, 3), cells_of(turned, edge, 3, 4)[0]
        rhs = cells_of(turned, edge, 4, 7)
        part = plus(handed(side, EDGE, 12), here[inward])
        stiff = stiffness(e, part[6:])
        v = [jnp.where(outside, 0.0, x) for x in relaxed(v, stiff, remainder(v, e, rhs, stiff, part))]
        here = moved(v, e)
        part = plus(handed(side, CARRY, 6), here[OWN], beside[inward])
        put_final(keep, edge, relaxed(v, stiff, remainder(v, e, rhs, stiff, part)))

        e = cells_of(turned, next_in, 3, 4)[0]
        add, rest = here[inward], handed(side, REST, 3)
        v, scale = handed(side, HELD, 3), handed(side, SCALE, 3)
        put_final(
            keep, next_in, [v[i] + scale[i] * (rest[i] + e * add[i] + add[3 + i]) for i in range(3)]
        )

    inside = slice(16, 8 * (nrad - 2))
    for index in range(6):
        keep[index, inside, :] = kept[index, inside, :]
    parts = []
    for i in range(3):
        for c in range(ncirc):
            both = [keep[2 * i + t, pl.ds(c, nrad, stride=8), :] for t in range(2)]
            plane = jnp.concatenate(both, axis=1)
            result[i, c] = plane
            parts.append(plane)
    copy = pltpu.make_async_copy(result, adjoint, sem)
    copy.start()
    lines = ncirc * nrad
    flat = jnp.concatenate(parts, axis=0)
    high, low = split(flat)
    table = jnp.concatenate([high, low], axis=0).astype(BF16)
    node = ids[...]
    rows = jnp.dot(table, pick[...], preferred_element_type=F32)
    rows = rows[: 3 * lines] + rows[3 * lines :]
    line = lax.broadcasted_iota(jnp.int32, (lines, node.shape[1]), 0)
    hit = line == node // 256
    picked = [
        jnp.sum(jnp.where(hit, rows[lines * i : lines * (i + 1)], 0.0), axis=0, keepdims=True)
        for i in range(3)
    ]
    weighted = sum(shapes[i] * picked[i] for i in range(3))
    sums_of[...] = jnp.broadcast_to(jnp.sum(weighted, axis=1, keepdims=True), sums_of.shape)
    owned = sums_of.shape[0] // devices
    lane = lax.broadcasted_iota(jnp.int32, (devices, 128), 1)
    out = jnp.zeros((devices, 128), F32)
    for j in range(owned):
        out = jnp.where(lane == j, sums_of[pl.ds(j, devices, stride=owned), :], out)
    for r in range(force.shape[0] // devices):
        force[devices * r : devices * (r + 1), 0, :] = out
    copy.wait()


def swaps(axis, start, wrap):
    count = lax.axis_size(axis)
    pairs = []
    for i in range(start, count, 2):
        j = (i + 1) % count
        if j > i or wrap:
            pairs += [(i, j), (j, i)]
    return pairs


VMEM = pl.BlockSpec(memory_space=pltpu.VMEM)
HBM = pl.BlockSpec(memory_space=pltpu.HBM)


def call(kernel, ins, outs, scratch=(), flops=1_000_000, limit=40 * 1024 * 1024, out_specs=None):
    outs = [o if isinstance(o, jax.ShapeDtypeStruct) else jax.ShapeDtypeStruct(o, F32) for o in outs]
    return pl.pallas_call(
        kernel,
        out_shape=outs,
        in_specs=ins,
        out_specs=out_specs or [VMEM] * len(outs),
        scratch_shapes=list(scratch),
        compiler_params=pltpu.CompilerParams(vmem_limit_bytes=limit),
        cost_estimate=pl.CostEstimate(flops=flops, bytes_accessed=1_000_000, transcendentals=0),
    )


def on_device(
    adjoint_prev, cell_class, class_moduli, flow_sens, flow_nodes, flow_count, surf_ids, mode_shapes
):
    _, ncirc, nrad, naxial = adjoint_prev.shape
    n_mode, n_rad = lax.axis_size("mode"), lax.axis_size("rad")
    slots = flow_nodes.shape[-1]
    lines = ncirc * nrad
    cells = (ncirc, nrad, naxial)
    message = (24, 8, 128)
    args = (
        class_moduli, flow_count[0, 0, 0], adjoint_prev, cell_class,
        jnp.swapaxes(flow_sens[0, 0, 0], 0, 1), flow_nodes[0, 0, 0],
    )
    send, e = call(
        pack_kernel,
        [HBM] * 6,
        [(n_mode, 24, 128), cells],
        [pltpu.SMEM(x.shape, x.dtype) for x in args[:2]]
        + [pltpu.VMEM(x.shape, x.dtype) for x in args[2:]]
        + [pltpu.SemaphoreType.DMA((6,))],
        limit=63 * 1024 * 1024 + 512 * 1024,
    )(*args)
    got = lax.all_to_all(send, "mode", split_axis=0, concat_axis=0, tiled=True)
    rhs, ends, first, second = call(
        scatter_kernel,
        [VMEM] * 3,
        [(3,) + cells, (ncirc, nrad, 128), message, message],
    )(got, adjoint_prev, e)
    first = lax.ppermute(first, "circ", swaps("circ", 0, True))
    second = lax.ppermute(second, "circ", swaps("circ", 1, True))
    turned, first, second = call(turn_kernel, [VMEM] * 6, [(15, 8 * nrad, 128), message, message])(
        adjoint_prev, e, rhs, ends, first, second
    )
    second = lax.ppermute(second, "rad", swaps("rad", 1, False))
    first = lax.ppermute(first, "rad", swaps("rad", 0, False))
    modes = mode_shapes.shape[3]
    owned = modes // n_mode
    ids = surf_ids[0, 0]
    shapes = jnp.swapaxes(mode_shapes[0, 0, 0], 0, 1)
    kept = (6, 8 * nrad, 128)
    left, keep, pick = call(
        inner_kernel,
        [VMEM, HBM],
        [(2, COUNT, 8, 384), kept, jax.ShapeDtypeStruct((naxial, ids.shape[1]), BF16)],
        [pltpu.VMEM(ids.shape, ids.dtype), pltpu.SemaphoreType.DMA],
        flops=10_000_000,
    )(turned, ids)
    final, force = call(
        functools.partial(sweep_kernel, n_mode),
        [VMEM] * 8,
        [adjoint_prev.shape, (n_rad * n_mode, 1, 128)],
        [
            pltpu.VMEM(kept, F32), pltpu.VMEM((modes, 128), F32),
            pltpu.VMEM(adjoint_prev.shape, F32), pltpu.SemaphoreType.DMA,
        ],
        out_specs=[HBM, VMEM],
    )(turned, second, first, left, keep, pick, ids, shapes)
    parts = lax.all_to_all(force, ("rad", "mode"), split_axis=0, concat_axis=0, tiled=True)
    own_force = jnp.sum(parts[:, 0, :owned], axis=0)
    return (final, own_force.reshape(owned, 1))


def solution(mesh):
    in_specs = (
        P(None, "circ", "rad", "mode"),
        P("circ", "rad", "mode"),
        P(),
        P("circ", "rad", "mode", None, None, None),
        P("circ", "rad", "mode", None, None),
        P("circ", "rad", "mode", None),
        P("circ", "rad", "mode", None),
        P("circ", "rad", "mode", None, None, None),
    )
    out_specs = (P(None, "circ", "rad", "mode"), P("mode", "circ"))
    return jax.shard_map(
        on_device, mesh=mesh, in_specs=in_specs, out_specs=out_specs, check_vma=False
    )
```

```python
import functools

import jax
import jax.numpy as jnp
from jax import lax
from jax.experimental import pallas as pl
from jax.experimental.pallas import tpu as pltpu
from jax.sharding import PartitionSpec as P

coupling = 0.5
relaxation = 0.6

face_own, face_other = 0.5 * (1.0 + coupling), 0.5
edge_own, edge_other = 0.25 * (1.0 + 0.5 * coupling), 0.25
corner_own = (1.0 + coupling / 3.0) / 6.0
edge_cross = 0.25 * coupling / 2.0
corner_cross = coupling / 18.0
centre_weight = 2 * face_own + 4 * face_other + 8 * edge_own + 4 * edge_other + 8 * corner_own

F32 = jnp.float32
BF16 = jnp.bfloat16
NT = (((1,), (1,)), ((), ()))


def split(x):
    high = x.astype(BF16).astype(F32)
    return high, x - high


def pack_kernel(
    moduli_in, count_in, prev_in, cls_in, sens_in, nodes_in, send, e_out,
    moduli, count, prev, cls, sens, nodes, sems,
):
    copies = [
        pltpu.make_async_copy(source, target, sems.at[i])
        for i, (source, target) in enumerate(
            (
                (sens_in, sens), (nodes_in, nodes), (prev_in, prev), (cls_in, cls),
                (count_in, count), (moduli_in, moduli),
            )
        )
    ]
    for copy in copies:
        copy.start()
    for copy in copies:
        copy.wait()
    _, blocks, slots = sens.shape
    ncirc, nrad, naxial = cls.shape
    lines = ncirc * nrad
    k = lax.axis_index("mode")
    lane = lax.broadcasted_iota(jnp.int32, (nrad, 128), 1)
    columns = []
    for c in range(ncirc):
        level = cls[c]
        e = jnp.zeros(level.shape, F32)
        for i in range(moduli.shape[0]):
            e = jnp.where(level == i, moduli[i], e)
        e_out[c] = e
        ends = jnp.zeros((nrad, 128), F32)
        for f in range(4):
            field = prev[f, c] if f < 3 else e
            first = pltpu.roll(field[:, :128], 4 * f + 2, 1)
            last = pltpu.roll(field[:, naxial - 128 :], 4 * f + 2, 1)
            ends = jnp.where((lane == 4 * f + 2) | (lane == 4 * f + 3), first, ends)
            ends = jnp.where((lane == 4 * f) | (lane == 4 * f + 1), last, ends)
        columns.append(ends)
    columns.append(jnp.zeros((128 - lines, 128), F32))
    items = jnp.concatenate(columns, axis=0).T
    halo = items[:8] + pltpu.roll(items[8:16], 32, 1)
    tall = lax.broadcasted_iota(jnp.int32, (8, 128), 0)
    to_high = jnp.where(tall % 4 < 2, halo, 0.0)
    to_low = halo - to_high

    node = nodes[...]
    axial, line = node % naxial, node // naxial
    key = jnp.where(axial == 0, line, jnp.where(axial == naxial - 1, line + lines, -1))
    key = key.astype(F32).astype(BF16)
    place = lax.broadcasted_iota(jnp.int32, (2 * lines, slots), 0).astype(F32).astype(BF16)
    slot = lax.broadcasted_iota(jnp.int32, (1, slots), 1)
    row = lax.broadcasted_iota(jnp.int32, (16, slots), 0) // 2
    zero, one = BF16(0.0), BF16(1.0)
    planes = []
    for d in range(blocks):
        live = slot < count[d]
        tile = jnp.zeros((16, slots), F32)
        for i in range(3):
            value = jnp.where(live, sens[i, d : d + 1], 0.0)
            for q in range(slots // 128):
                send[d, 4 * (i + 1) + q : 4 * (i + 1) + q + 1, :] = value[:, 128 * q : 128 * (q + 1)]
            high, low = split(value)
            tile = jnp.where(row == i, high, jnp.where(row == 4 + i, low, tile))
        for q in range(slots // 128):
            send[d, q : q + 1, :] = node[d : d + 1, 128 * q : 128 * (q + 1)].astype(F32)
        hits = jnp.where(place == jnp.broadcast_to(key[d : d + 1], place.shape), one, zero)
        plane = lax.dot_general(tile.astype(BF16), hits, NT, preferred_element_type=F32)
        plane = jnp.concatenate([plane[:8] + plane[8:], jnp.zeros((8, 128 - 2 * lines), F32)], axis=1)
        planes.append(plane)
    group = lax.broadcasted_iota(jnp.int32, (8, 128), 1) // lines == 2
    even, odd = group & (tall % 2 == 0), group & (tall % 2 == 1)
    for d in range(blocks):
        out = jnp.where(k == d + 1, to_low, 0.0) + jnp.where(k == d - 1, to_high, 0.0)
        if d + 1 < blocks:
            out = jnp.where(odd, pltpu.roll(planes[d + 1], 2 * lines, 1), out)
        if d > 0:
            out = jnp.where(even, pltpu.roll(planes[d - 1], lines, 1), out)
        send[d, 16:24, :] = out


def scatter_kernel(got, prev, e, rhs, ends, first, second):
    blocks = got.shape[0]
    _, ncirc, nrad, naxial = prev.shape
    lines = ncirc * nrad
    row = lax.broadcasted_iota(jnp.int32, (lines, 128), 0).astype(F32).astype(BF16)
    cell = lax.broadcasted_iota(jnp.int32, (128, naxial), 1).astype(F32).astype(BF16)
    nodes = jnp.concatenate([got[d, :4, :] for d in range(blocks)], axis=0).astype(jnp.int32)
    line = (nodes // naxial).astype(F32).astype(BF16)
    tall = jnp.concatenate([nodes % naxial, jnp.zeros((128 - 4 * blocks, 128), jnp.int32)], axis=0)
    tall = tall.astype(F32).T.astype(BF16)
    zero, one = BF16(0.0), BF16(1.0)
    dense = jnp.zeros((6 * lines, naxial), F32)
    for d in range(blocks):
        left, right = [], []
        for q in range(4):
            g = 4 * d + q
            at = jnp.broadcast_to(tall[:, g : g + 1], cell.shape)
            right.append(jnp.where(cell == at, one, zero))
            hit = row == jnp.broadcast_to(line[g : g + 1], row.shape)
            column = []
            for i in range(3):
                for part in split(got[d, 4 * (i + 1) + q : 4 * (i + 1) + q + 1, :]):
                    column.append(jnp.where(hit, jnp.broadcast_to(part.astype(BF16), row.shape), zero))
            left.append(jnp.concatenate(column, axis=0))
        left, right = jnp.concatenate(left, axis=1), jnp.concatenate(right, axis=0)
        dense = dense + jnp.dot(left, right, preferred_element_type=F32)
    for i in range(3):
        total = dense[2 * lines * i : 2 * lines * i + lines] + dense[2 * lines * i + lines : 2 * lines * (i + 1)]
        for c in range(ncirc):
            rhs[i, c] = total[nrad * c : nrad * (c + 1)]
    total = got[0, 16:24, :]
    for d in range(1, blocks):
        total = total + got[d, 16:24, :]
    groups = [total, pltpu.roll(total, 128 - lines, 1), pltpu.roll(total, 128 - 2 * lines, 1)]
    columns = jnp.concatenate(groups + [jnp.zeros((104, 128), F32)], axis=0).T
    for c in range(ncirc):
        ends[c] = columns[nrad * c : nrad * (c + 1)]
    for out, base, edge in ((first, ncirc - 2, ncirc - 1), (second, 0, 0)):
        for t in range(2):
            cut = slice(128 * t, 128 * (t + 1))
            for f in range(4):
                for j in range(2):
                    source = prev[f, base + j] if f < 3 else e[base + j]
                    out[4 * f + 2 * t + j] = source[:, cut]
            for i in range(3):
                out[16 + 2 * i + t] = rhs[i, edge][:, cut]
        for j in range(2):
            out[22 + j] = ends[base + j]


def turn_kernel(prev, e, rhs, ends, got_first, got_second, turned, first, second):
    _, ncirc, nrad, _ = prev.shape
    def put(index, c, plane):
        turned[index, pl.ds(c, nrad, stride=8), :] = plane

    for c in range(ncirc):
        for t in range(2):
            cut = slice(128 * t, 128 * (t + 1))
            for f in range(4):
                source = prev[f, c] if f < 3 else e[c]
                put(2 * f + t, c, source[:, cut])
            for i in range(3):
                put(8 + 2 * i + t, c, rhs[i, c][:, cut])
        put(14, c, ends[c])

    def sides(tile):
        return got_first[tile], got_second[tile]

    for index in range(8):
        for j in range(2):
            low, high = sides(2 * index + j)
            put(index, 6 + j, low)
            put(index, 4 + j, high)
    for index in range(6):
        low, high = sides(16 + index)
        put(8 + index, 7, low)
        put(8 + index, 4, high)
        put(8 + index, 6, low)
        put(8 + index, 5, high)
    for j in range(2):
        low, high = sides(22 + j)
        put(14, 6 + j, low)
        put(14, 4 + j, high)

    odd = lax.axis_index("rad") % 2
    for out, at_high in ((first, 1 - odd), (second, odd)):
        for index in range(15):
            for j in range(2):
                plane = at_high * (nrad - 2) + j
                at = 2 * index + j
                if 8 <= index < 14:
                    if j:
                        continue
                    plane = at_high * (nrad - 1)
                    at = 16 + index - 8
                elif index == 14:
                    at = 22 + j
                out[at] = turned[index, pl.ds(pl.multiple_of(8 * plane, 8), 8), :]


def sums(x):
    up = pltpu.roll(x, x.shape[1] - 1, 1)
    down = pltpu.roll(x, 1, 1)
    return up + down, up - down


def across(x):
    up = pltpu.roll(x, 7, 0)
    down = pltpu.roll(x, 1, 0)
    return up + down, up - down


def spread(x):
    sn, dn = sums(x)
    sm, dm = across(x)
    smsn, dmsn = across(sn)
    smdn, dmdn = across(dn)
    return sn, dn, sm, dm, smsn, dmsn, smdn, dmdn


def leading_terms(x, s):
    sn, _, sm, _, both = s[0], s[1], s[2], s[3], s[4]
    near = sm + sn
    return face_other * near + edge_other * both, face_own * x + edge_own * near + corner_own * both


def plane_terms(x, own, other, both):
    centre = face_own * own + face_other * other + edge_own * both
    side = face_other * x + edge_own * own + edge_other * other + corner_own * both
    return centre, side


def cross_terms(s):
    _, dn, _, dm, _, dmsn, smdn, dmdn = s
    return edge_cross * dm + corner_cross * dmsn, edge_cross * dn + corner_cross * smdn, dmdn


def vector_terms(v):
    s0, s1, s2 = spread(v[0]), spread(v[1]), spread(v[2])
    p0, q0 = plane_terms(v[0], s0[2], s0[0], s0[4])
    p1, q1 = leading_terms(v[1], s1)
    p2, q2 = plane_terms(v[2], s2[0], s2[2], s2[4])
    rm0, _, w0 = cross_terms(s0)
    rm1, rn1, _ = cross_terms(s1)
    _, rn2, w2 = cross_terms(s2)
    p0 = p0 + edge_cross * w2
    q0 = q0 + corner_cross * w2
    p2 = p2 + edge_cross * w0
    q2 = q2 + corner_cross * w0
    d0, d1, d2 = rm1, rm0 + rn2, rn1
    return (p0, p1, p2), (q0 + d0, q1 + d1, q2 + d2), (q0 - d0, q1 - d1, q2 - d2)


def scalar_terms(e):
    s = spread(e)
    p0, q0 = plane_terms(e, s[2], s[0], s[4])
    p1, q1 = leading_terms(e, s)
    p2, q2 = plane_terms(e, s[0], s[2], s[4])
    rm, rn, w = cross_terms(s)
    return (p0, p1, p2), (q0, q1, q2), rm, rn, w


def moved(v, e):
    plain, scaled = vector_terms(v), vector_terms([e * x for x in v])
    return [list(plain[j]) + list(scaled[j]) for j in range(3)]


def weighed(e):
    p, q, rm, rn, w = scalar_terms(e)
    zero = jnp.zeros_like(w)
    side = corner_cross * w
    return [
        list(p) + [zero, zero, edge_cross * w],
        list(q) + [rm, rn, side],
        list(q) + [-rm, -rn, side],
    ]


def plus(*parts):
    return [functools.reduce(lambda a, b: a + b, column) for column in zip(*parts)]


def stiffness(e, part):
    diag = [centre_weight * e + x for x in part[:3]]
    return diag, [relaxation / x for x in diag], part[3], part[4], part[5]


def remainder(v, e, rhs, stiff, part):
    (d0, d1, d2), _, c01, c12, c02 = stiff
    own = (
        d0 * v[0] + c01 * v[1] + c02 * v[2],
        c01 * v[0] + d1 * v[1] + c12 * v[2],
        c02 * v[0] + c12 * v[1] + d2 * v[2],
    )
    return [rhs[i] - own[i] + e * part[i] + part[3 + i] for i in range(3)]


def relaxed(v, stiff, rest):
    return [v[i] + stiff[1][i] * rest[i] for i in range(3)]


def outside_mask():
    lane = lax.broadcasted_iota(jnp.int32, (8, 384), 1)
    mode = lax.axis_index("mode")
    return ((lane == 383) & (mode == 0)) | ((lane == 256) & (mode == lax.axis_size("mode") - 1))


def own_tile(turned, index, plane):
    return turned[index, 8 * plane : 8 * (plane + 1), :]


def field_of(tile, f, ends):
    shift = 4 * f + 2 if f < 4 else 17 + 2 * (f - 4)
    return jnp.concatenate([tile(2 * f), tile(2 * f + 1), pltpu.roll(ends, 128 - shift, 1)], axis=1)


def cells_of(turned, plane, first, last):
    tile = lambda index: own_tile(turned, index, plane)
    ends = tile(14)
    return [field_of(tile, f, ends) for f in range(first, last)]


def put_final(keep, plane, final):
    for i in range(3):
        for t in range(2):
            keep[2 * i + t, 8 * plane : 8 * (plane + 1), :] = final[i][:, 128 * t : 128 * (t + 1)]


BEYOND, EDGE, CARRY, REST, HELD, SCALE, COUNT = 0, 12, 24, 30, 33, 36, 39
OWN, DOWN, UP = 0, 1, 2


def inner_kernel(turned, ids, left, keep, pick, nodes, sem):
    nrad = turned.shape[1] // 8
    copy = pltpu.make_async_copy(ids, nodes, sem)
    copy.start()
    outside = outside_mask()
    last = nrad - 1
    adds, middle, stiff = {}, {}, {}

    def leave(side, at, arrays):
        for j, x in enumerate(arrays):
            left[side, at + j] = x

    for plane in range(nrad):
        v, e = cells_of(turned, plane, 0, 3), cells_of(turned, plane, 3, 4)[0]
        adds[plane] = [a + b for a, b in zip(moved(v, e), weighed(e))]
        if plane == 0:
            leave(0, BEYOND, adds[0][DOWN])
        if plane == 1:
            leave(0, EDGE, plus(adds[0][OWN], adds[1][DOWN]))
        if plane == last:
            leave(1, EDGE, plus(adds[last][OWN], adds[last - 1][UP]))
            leave(1, BEYOND, adds[last][UP])
        at = plane - 1
        if at < 1:
            continue
        v, e = cells_of(turned, at, 0, 3), cells_of(turned, at, 3, 4)[0]
        part = plus(adds[at - 1][UP], adds[at][OWN], adds[at + 1][DOWN])
        stiff[at] = stiffness(e, part[6:])
        rest = remainder(v, e, cells_of(turned, at, 4, 7), stiff[at], part)
        middle[at] = [jnp.where(outside, 0.0, x) for x in relaxed(v, stiff[at], rest)]

    adds = {}
    for plane in range(1, last):
        e = cells_of(turned, plane, 3, 4)[0]
        adds[plane] = moved(middle[plane], e)
        if plane == 1:
            leave(0, CARRY, adds[1][DOWN])
        if plane == last - 1:
            leave(1, CARRY, adds[last - 1][UP])
        for at in (plane - 1, plane):
            if at < 1 or (at == plane and plane < last - 1):
                continue
            beside = []
            if at - 1 in adds:
                beside.append(adds[at - 1][UP])
            if at + 1 in adds:
                beside.append(adds[at + 1][DOWN])
            part = plus(adds[at][OWN], *beside)
            v, e = middle[at], cells_of(turned, at, 3, 4)[0]
            rest = remainder(v, e, cells_of(turned, at, 4, 7), stiff[at], part)
            if len(beside) == 2:
                put_final(keep, at, relaxed(v, stiff[at], rest))
            else:
                side = 0 if at == 1 else 1
                leave(side, REST, rest)
                leave(side, HELD, v)
                leave(side, SCALE, stiff[at][1])
    copy.wait()
    cell = lax.broadcasted_iota(jnp.int32, pick.shape, 0)
    pick[...] = jnp.where(cell == nodes[...] % 256, 1.0, 0.0).astype(BF16)


def sweep_kernel(
    devices, turned, got_second, got_first, left, kept, pick, ids, shapes,
    adjoint, force, keep, sums_of, result, sem,
):
    nrad = turned.shape[1] // 8
    ncirc = result.shape[1]
    rad = lax.axis_index("rad")
    odd = rad % 2 == 1
    outside = outside_mask()

    def halo(side, j, first, last):
        def tile(index):
            if index == 14:
                at = 22 + j
            elif index >= 8:
                at = 16 + index - 8
            else:
                at = 2 * index + j
            a, b = got_first[at], got_second[at]
            return jnp.where(odd, b, a) if side else jnp.where(odd, a, b)

        ends = tile(14)
        return [field_of(tile, f, ends) for f in range(first, last)]

    def handed(side, at, count):
        return [left[side, at + j] for j in range(count)]

    for side in range(2):
        inward = DOWN if side else UP
        near, far = (0, 1) if side else (1, 0)
        edge, next_in = (nrad - 1, nrad - 2) if side else (0, 1)
        v, e = halo(side, far, 0, 3), halo(side, far, 3, 4)[0]
        beyond = moved(v, e)[inward] + weighed(e)[inward]
        v, e = halo(side, near, 0, 3), halo(side, near, 3, 4)[0]
        here = [a + b for a, b in zip(moved(v, e), weighed(e))]
        part = plus(handed(side, BEYOND, 12), here[OWN], beyond)
        stiff = stiffness(e, part[6:])
        rest = remainder(v, e, halo(side, near, 4, 7), stiff, part)
        drop = outside | (rad == (lax.axis_size("rad") - 1 if side else 0))
        beside = moved([jnp.where(drop, 0.0, x) for x in relaxed(v, stiff, rest)], e)

        v, e = cells_of(turned, edge, 0, 3), cells_of(turned, edge, 3, 4)[0]
        rhs = cells_of(turned, edge, 4, 7)
        part = plus(handed(side, EDGE, 12), here[inward])
        stiff = stiffness(e, part[6:])
        v = [jnp.where(outside, 0.0, x) for x in relaxed(v, stiff, remainder(v, e, rhs, stiff, part))]
        here = moved(v, e)
        part = plus(handed(side, CARRY, 6), here[OWN], beside[inward])
        put_final(keep, edge, relaxed(v, stiff, remainder(v, e, rhs, stiff, part)))

        e = cells_of(turned, next_in, 3, 4)[0]
        add, rest = here[inward], handed(side, REST, 3)
        v, scale = handed(side, HELD, 3), handed(side, SCALE, 3)
        put_final(
            keep, next_in, [v[i] + scale[i] * (rest[i] + e * add[i] + add[3 + i]) for i in range(3)]
        )

    inside = slice(16, 8 * (nrad - 2))
    for index in range(6):
        keep[index, inside, :] = kept[index, inside, :]
    parts = []
    for i in range(3):
        for c in range(ncirc):
            both = [keep[2 * i + t, pl.ds(c, nrad, stride=8), :] for t in range(2)]
            plane = jnp.concatenate(both, axis=1)
            result[i, c] = plane
            parts.append(plane)
    copy = pltpu.make_async_copy(result, adjoint, sem)
    copy.start()
    lines = ncirc * nrad
    flat = jnp.concatenate(parts, axis=0)
    high, low = split(flat)
    table = jnp.concatenate([high, low], axis=0).astype(BF16)
    node = ids[...]
    rows = jnp.dot(table, pick[...], preferred_element_type=F32)
    rows = rows[: 3 * lines] + rows[3 * lines :]
    line = lax.broadcasted_iota(jnp.int32, (lines, node.shape[1]), 0)
    hit = line == node // 256
    picked = [
        jnp.sum(jnp.where(hit, rows[lines * i : lines * (i + 1)], 0.0), axis=0, keepdims=True)
        for i in range(3)
    ]
    weighted = sum(shapes[i] * picked[i] for i in range(3))
    sums_of[...] = jnp.broadcast_to(jnp.sum(weighted, axis=1, keepdims=True), sums_of.shape)
    owned = sums_of.shape[0] // devices
    lane = lax.broadcasted_iota(jnp.int32, (devices, 128), 1)
    out = jnp.zeros((devices, 128), F32)
    for j in range(owned):
        out = jnp.where(lane == j, sums_of[pl.ds(j, devices, stride=owned), :], out)
    for r in range(force.shape[0] // devices):
        force[devices * r : devices * (r + 1), 0, :] = out
    copy.wait()


def swaps(axis, start, wrap):
    count = lax.axis_size(axis)
    pairs = []
    for i in range(start, count, 2):
        j = (i + 1) % count
        if j > i or wrap:
            pairs += [(i, j), (j, i)]
    return pairs


VMEM = pl.BlockSpec(memory_space=pltpu.VMEM)
HBM = pl.BlockSpec(memory_space=pltpu.HBM)


def call(kernel, ins, outs, scratch=(), flops=1_000_000, limit=40 * 1024 * 1024, out_specs=None):
    outs = [o if isinstance(o, jax.ShapeDtypeStruct) else jax.ShapeDtypeStruct(o, F32) for o in outs]
    return pl.pallas_call(
        kernel,
        out_shape=outs,
        in_specs=ins,
        out_specs=out_specs or [VMEM] * len(outs),
        scratch_shapes=list(scratch),
        compiler_params=pltpu.CompilerParams(vmem_limit_bytes=limit),
        cost_estimate=pl.CostEstimate(flops=flops, bytes_accessed=1_000_000, transcendentals=0),
    )


def on_device(
    adjoint_prev, cell_class, class_moduli, flow_sens, flow_nodes, flow_count, surf_ids, mode_shapes
):
    _, ncirc, nrad, naxial = adjoint_prev.shape
    n_mode, n_rad = lax.axis_size("mode"), lax.axis_size("rad")
    slots = flow_nodes.shape[-1]
    lines = ncirc * nrad
    cells = (ncirc, nrad, naxial)
    message = (24, 8, 128)
    args = (
        class_moduli, flow_count[0, 0, 0], adjoint_prev, cell_class,
        jnp.swapaxes(flow_sens[0, 0, 0], 0, 1), flow_nodes[0, 0, 0],
    )
    send, e = call(
        pack_kernel,
        [HBM] * 6,
        [(n_mode, 24, 128), cells],
        [pltpu.SMEM(x.shape, x.dtype) for x in args[:2]]
        + [pltpu.VMEM(x.shape, x.dtype) for x in args[2:]]
        + [pltpu.SemaphoreType.DMA((6,))],
        limit=63 * 1024 * 1024 + 512 * 1024,
    )(*args)
    got = lax.all_to_all(send, "mode", split_axis=0, concat_axis=0, tiled=True)
    rhs, ends, first, second = call(
        scatter_kernel,
        [VMEM] * 3,
        [(3,) + cells, (ncirc, nrad, 128), message, message],
    )(got, adjoint_prev, e)
    n_circ = lax.axis_size("circ")
    first = lax.ppermute(first, "circ", [(i, (i + 1) % n_circ) for i in range(n_circ)])
    second = lax.ppermute(second, "circ", [((i + 1) % n_circ, i) for i in range(n_circ)])
    turned, first, second = call(turn_kernel, [VMEM] * 6, [(15, 8 * nrad, 128), message, message])(
        adjoint_prev, e, rhs, ends, first, second
    )
    second = lax.ppermute(second, "rad", swaps("rad", 1, False))
    first = lax.ppermute(first, "rad", swaps("rad", 0, False))
    modes = mode_shapes.shape[3]
    owned = modes // n_mode
    ids = surf_ids[0, 0]
    shapes = jnp.swapaxes(mode_shapes[0, 0, 0], 0, 1)
    kept = (6, 8 * nrad, 128)
    left, keep, pick = call(
        inner_kernel,
        [VMEM, HBM],
        [(2, COUNT, 8, 384), kept, jax.ShapeDtypeStruct((naxial, ids.shape[1]), BF16)],
        [pltpu.VMEM(ids.shape, ids.dtype), pltpu.SemaphoreType.DMA],
        flops=10_000_000,
    )(turned, ids)
    final, force = call(
        functools.partial(sweep_kernel, n_mode),
        [VMEM] * 8,
        [adjoint_prev.shape, (n_rad * n_mode, 1, 128)],
        [
            pltpu.VMEM(kept, F32), pltpu.VMEM((modes, 128), F32),
            pltpu.VMEM(adjoint_prev.shape, F32), pltpu.SemaphoreType.DMA,
        ],
        out_specs=[HBM, VMEM],
    )(turned, second, first, left, keep, pick, ids, shapes)
    parts = lax.all_to_all(force, ("rad", "mode"), split_axis=0, concat_axis=0, tiled=True)
    own_force = jnp.sum(parts[:, 0, :owned], axis=0)
    return (final, own_force.reshape(owned, 1))


def solution(mesh):
    in_specs = (
        P(None, "circ", "rad", "mode"),
        P("circ", "rad", "mode"),
        P(),
        P("circ", "rad", "mode", None, None, None),
        P("circ", "rad", "mode", None, None),
        P("circ", "rad", "mode", None),
        P("circ", "rad", "mode", None),
        P("circ", "rad", "mode", None, None, None),
    )
    out_specs = (P(None, "circ", "rad", "mode"), P("mode", "circ"))
    return jax.shard_map(
        on_device, mesh=mesh, in_specs=in_specs, out_specs=out_specs, check_vma=False
    )
```

```python
import functools

import jax
import jax.numpy as jnp
from jax import lax
from jax.experimental import pallas as pl
from jax.experimental.pallas import tpu as pltpu
from jax.sharding import PartitionSpec as P

coupling = 0.5
relaxation = 0.6

face_own, face_other = 0.5 * (1.0 + coupling), 0.5
edge_own, edge_other = 0.25 * (1.0 + 0.5 * coupling), 0.25
corner_own = (1.0 + coupling / 3.0) / 6.0
edge_cross = 0.25 * coupling / 2.0
corner_cross = coupling / 18.0
centre_weight = 2 * face_own + 4 * face_other + 8 * edge_own + 4 * edge_other + 8 * corner_own

F32 = jnp.float32
BF16 = jnp.bfloat16
NT = (((1,), (1,)), ((), ()))


def split(x):
    high = x.astype(BF16).astype(F32)
    return high, x - high


def pack_kernel(
    moduli_in, count_in, prev_in, cls_in, sens_in, nodes_in, send, e_out,
    moduli, count, prev, cls, sens, nodes, sems,
):
    copies = [
        pltpu.make_async_copy(source, target, sems.at[i])
        for i, (source, target) in enumerate(
            (
                (sens_in, sens), (nodes_in, nodes), (prev_in, prev), (cls_in, cls),
                (count_in, count), (moduli_in, moduli),
            )
        )
    ]
    for copy in copies:
        copy.start()
    for copy in copies:
        copy.wait()
    _, blocks, slots = sens.shape
    ncirc, nrad, naxial = cls.shape
    lines = ncirc * nrad
    k = lax.axis_index("mode")
    lane = lax.broadcasted_iota(jnp.int32, (nrad, 128), 1)
    columns = []
    for c in range(ncirc):
        level = cls[c]
        e = jnp.zeros(level.shape, F32)
        for i in range(moduli.shape[0]):
            e = jnp.where(level == i, moduli[i], e)
        e_out[c] = e
        ends = jnp.zeros((nrad, 128), F32)
        for f in range(4):
            field = prev[f, c] if f < 3 else e
            first = pltpu.roll(field[:, :128], 4 * f + 2, 1)
            last = pltpu.roll(field[:, naxial - 128 :], 4 * f + 2, 1)
            ends = jnp.where((lane == 4 * f + 2) | (lane == 4 * f + 3), first, ends)
            ends = jnp.where((lane == 4 * f) | (lane == 4 * f + 1), last, ends)
        columns.append(ends)
    columns.append(jnp.zeros((128 - lines, 128), F32))
    items = jnp.concatenate(columns, axis=0).T
    halo = items[:8] + pltpu.roll(items[8:16], 32, 1)
    tall = lax.broadcasted_iota(jnp.int32, (8, 128), 0)
    to_high = jnp.where(tall % 4 < 2, halo, 0.0)
    to_low = halo - to_high

    node = nodes[...]
    axial, line = node % naxial, node // naxial
    key = jnp.where(axial == 0, line, jnp.where(axial == naxial - 1, line + lines, -1))
    key = key.astype(F32).astype(BF16)
    place = lax.broadcasted_iota(jnp.int32, (2 * lines, slots), 0).astype(F32).astype(BF16)
    slot = lax.broadcasted_iota(jnp.int32, (1, slots), 1)
    row = lax.broadcasted_iota(jnp.int32, (16, slots), 0) // 2
    zero, one = BF16(0.0), BF16(1.0)
    planes = []
    for d in range(blocks):
        live = slot < count[d]
        tile = jnp.zeros((16, slots), F32)
        for i in range(3):
            value = jnp.where(live, sens[i, d : d + 1], 0.0)
            for q in range(slots // 128):
                send[d, 4 * (i + 1) + q : 4 * (i + 1) + q + 1, :] = value[:, 128 * q : 128 * (q + 1)]
            high, low = split(value)
            tile = jnp.where(row == i, high, jnp.where(row == 4 + i, low, tile))
        for q in range(slots // 128):
            send[d, q : q + 1, :] = node[d : d + 1, 128 * q : 128 * (q + 1)].astype(F32)
        hits = jnp.where(place == jnp.broadcast_to(key[d : d + 1], place.shape), one, zero)
        plane = lax.dot_general(tile.astype(BF16), hits, NT, preferred_element_type=F32)
        plane = jnp.concatenate([plane[:8] + plane[8:], jnp.zeros((8, 128 - 2 * lines), F32)], axis=1)
        planes.append(plane)
    group = lax.broadcasted_iota(jnp.int32, (8, 128), 1) // lines == 2
    even, odd = group & (tall % 2 == 0), group & (tall % 2 == 1)
    for d in range(blocks):
        out = jnp.where(k == d + 1, to_low, 0.0) + jnp.where(k == d - 1, to_high, 0.0)
        if d + 1 < blocks:
            out = jnp.where(odd, pltpu.roll(planes[d + 1], 2 * lines, 1), out)
        if d > 0:
            out = jnp.where(even, pltpu.roll(planes[d - 1], lines, 1), out)
        send[d, 16:24, :] = out


def scatter_kernel(got, prev, e, rhs, ends, first, second):
    blocks = got.shape[0]
    _, ncirc, nrad, naxial = prev.shape
    lines = ncirc * nrad
    row = lax.broadcasted_iota(jnp.int32, (lines, 128), 0).astype(F32).astype(BF16)
    cell = lax.broadcasted_iota(jnp.int32, (128, naxial), 1).astype(F32).astype(BF16)
    nodes = jnp.concatenate([got[d, :4, :] for d in range(blocks)], axis=0).astype(jnp.int32)
    line = (nodes // naxial).astype(F32).astype(BF16)
    tall = jnp.concatenate([nodes % naxial, jnp.zeros((128 - 4 * blocks, 128), jnp.int32)], axis=0)
    tall = tall.astype(F32).T.astype(BF16)
    zero, one = BF16(0.0), BF16(1.0)
    dense = jnp.zeros((6 * lines, naxial), F32)
    for d in range(blocks):
        left, right = [], []
        for q in range(4):
            g = 4 * d + q
            at = jnp.broadcast_to(tall[:, g : g + 1], cell.shape)
            right.append(jnp.where(cell == at, one, zero))
            hit = row == jnp.broadcast_to(line[g : g + 1], row.shape)
            column = []
            for i in range(3):
                for part in split(got[d, 4 * (i + 1) + q : 4 * (i + 1) + q + 1, :]):
                    column.append(jnp.where(hit, jnp.broadcast_to(part.astype(BF16), row.shape), zero))
            left.append(jnp.concatenate(column, axis=0))
        left, right = jnp.concatenate(left, axis=1), jnp.concatenate(right, axis=0)
        dense = dense + jnp.dot(left, right, preferred_element_type=F32)
    for i in range(3):
        total = dense[2 * lines * i : 2 * lines * i + lines] + dense[2 * lines * i + lines : 2 * lines * (i + 1)]
        for c in range(ncirc):
            rhs[i, c] = total[nrad * c : nrad * (c + 1)]
    total = got[0, 16:24, :]
    for d in range(1, blocks):
        total = total + got[d, 16:24, :]
    groups = [total, pltpu.roll(total, 128 - lines, 1), pltpu.roll(total, 128 - 2 * lines, 1)]
    columns = jnp.concatenate(groups + [jnp.zeros((104, 128), F32)], axis=0).T
    for c in range(ncirc):
        ends[c] = columns[nrad * c : nrad * (c + 1)]
    for out, base, edge in ((first, ncirc - 2, ncirc - 1), (second, 0, 0)):
        for t in range(2):
            cut = slice(128 * t, 128 * (t + 1))
            for f in range(4):
                for j in range(2):
                    source = prev[f, base + j] if f < 3 else e[base + j]
                    out[4 * f + 2 * t + j] = source[:, cut]
            for i in range(3):
                out[16 + 2 * i + t] = rhs[i, edge][:, cut]
        for j in range(2):
            out[22 + j] = ends[base + j]


def turn_kernel(prev, e, rhs, ends, got_first, got_second, turned, first, second, left, keep):
    _, ncirc, nrad, _ = prev.shape
    def put(index, c, plane):
        turned[index, pl.ds(c, nrad, stride=8), :] = plane

    for c in range(ncirc):
        for t in range(2):
            cut = slice(128 * t, 128 * (t + 1))
            for f in range(4):
                source = prev[f, c] if f < 3 else e[c]
                put(2 * f + t, c, source[:, cut])
            for i in range(3):
                put(8 + 2 * i + t, c, rhs[i, c][:, cut])
        put(14, c, ends[c])

    def sides(tile):
        return got_first[tile], got_second[tile]

    for index in range(8):
        for j in range(2):
            low, high = sides(2 * index + j)
            put(index, 6 + j, low)
            put(index, 4 + j, high)
    for index in range(6):
        low, high = sides(16 + index)
        put(8 + index, 7, low)
        put(8 + index, 4, high)
        put(8 + index, 6, low)
        put(8 + index, 5, high)
    for j in range(2):
        low, high = sides(22 + j)
        put(14, 6 + j, low)
        put(14, 4 + j, high)

    odd = lax.axis_index("rad") % 2
    for out, at_high in ((first, 1 - odd), (second, odd)):
        for index in range(15):
            for j in range(2):
                plane = at_high * (nrad - 2) + j
                at = 2 * index + j
                if 8 <= index < 14:
                    if j:
                        continue
                    plane = at_high * (nrad - 1)
                    at = 16 + index - 8
                elif index == 14:
                    at = 22 + j
                out[at] = turned[index, pl.ds(pl.multiple_of(8 * plane, 8), 8), :]

    @pl.when(works_ahead())
    def _():
        inner_work(turned, left, keep)


def sums(x):
    up = pltpu.roll(x, x.shape[1] - 1, 1)
    down = pltpu.roll(x, 1, 1)
    return up + down, up - down


def across(x):
    up = pltpu.roll(x, 7, 0)
    down = pltpu.roll(x, 1, 0)
    return up + down, up - down


def spread(x):
    sn, dn = sums(x)
    sm, dm = across(x)
    smsn, dmsn = across(sn)
    smdn, dmdn = across(dn)
    return sn, dn, sm, dm, smsn, dmsn, smdn, dmdn


def leading_terms(x, s):
    sn, _, sm, _, both = s[0], s[1], s[2], s[3], s[4]
    near = sm + sn
    return face_other * near + edge_other * both, face_own * x + edge_own * near + corner_own * both


def plane_terms(x, own, other, both):
    centre = face_own * own + face_other * other + edge_own * both
    side = face_other * x + edge_own * own + edge_other * other + corner_own * both
    return centre, side


def cross_terms(s):
    _, dn, _, dm, _, dmsn, smdn, dmdn = s
    return edge_cross * dm + corner_cross * dmsn, edge_cross * dn + corner_cross * smdn, dmdn


def vector_terms(v):
    s0, s1, s2 = spread(v[0]), spread(v[1]), spread(v[2])
    p0, q0 = plane_terms(v[0], s0[2], s0[0], s0[4])
    p1, q1 = leading_terms(v[1], s1)
    p2, q2 = plane_terms(v[2], s2[0], s2[2], s2[4])
    rm0, _, w0 = cross_terms(s0)
    rm1, rn1, _ = cross_terms(s1)
    _, rn2, w2 = cross_terms(s2)
    p0 = p0 + edge_cross * w2
    q0 = q0 + corner_cross * w2
    p2 = p2 + edge_cross * w0
    q2 = q2 + corner_cross * w0
    d0, d1, d2 = rm1, rm0 + rn2, rn1
    return (p0, p1, p2), (q0 + d0, q1 + d1, q2 + d2), (q0 - d0, q1 - d1, q2 - d2)


def scalar_terms(e):
    s = spread(e)
    p0, q0 = plane_terms(e, s[2], s[0], s[4])
    p1, q1 = leading_terms(e, s)
    p2, q2 = plane_terms(e, s[0], s[2], s[4])
    rm, rn, w = cross_terms(s)
    return (p0, p1, p2), (q0, q1, q2), rm, rn, w


def moved(v, e):
    plain, scaled = vector_terms(v), vector_terms([e * x for x in v])
    return [list(plain[j]) + list(scaled[j]) for j in range(3)]


def weighed(e):
    p, q, rm, rn, w = scalar_terms(e)
    zero = jnp.zeros_like(w)
    side = corner_cross * w
    return [
        list(p) + [zero, zero, edge_cross * w],
        list(q) + [rm, rn, side],
        list(q) + [-rm, -rn, side],
    ]


def plus(*parts):
    return [functools.reduce(lambda a, b: a + b, column) for column in zip(*parts)]


def stiffness(e, part):
    diag = [centre_weight * e + x for x in part[:3]]
    return diag, [relaxation / x for x in diag], part[3], part[4], part[5]


def remainder(v, e, rhs, stiff, part):
    (d0, d1, d2), _, c01, c12, c02 = stiff
    own = (
        d0 * v[0] + c01 * v[1] + c02 * v[2],
        c01 * v[0] + d1 * v[1] + c12 * v[2],
        c02 * v[0] + c12 * v[1] + d2 * v[2],
    )
    return [rhs[i] - own[i] + e * part[i] + part[3 + i] for i in range(3)]


def relaxed(v, stiff, rest):
    return [v[i] + stiff[1][i] * rest[i] for i in range(3)]


def outside_mask():
    lane = lax.broadcasted_iota(jnp.int32, (8, 384), 1)
    mode = lax.axis_index("mode")
    return ((lane == 383) & (mode == 0)) | ((lane == 256) & (mode == lax.axis_size("mode") - 1))


def own_tile(turned, index, plane):
    return turned[index, 8 * plane : 8 * (plane + 1), :]


def field_of(tile, f, ends):
    shift = 4 * f + 2 if f < 4 else 17 + 2 * (f - 4)
    return jnp.concatenate([tile(2 * f), tile(2 * f + 1), pltpu.roll(ends, 128 - shift, 1)], axis=1)


def cells_of(turned, plane, first, last):
    tile = lambda index: own_tile(turned, index, plane)
    ends = tile(14)
    return [field_of(tile, f, ends) for f in range(first, last)]


def put_final(keep, plane, final):
    for i in range(3):
        for t in range(2):
            keep[2 * i + t, 8 * plane : 8 * (plane + 1), :] = final[i][:, 128 * t : 128 * (t + 1)]


BEYOND, EDGE, CARRY, REST, HELD, SCALE, COUNT = 0, 12, 24, 30, 33, 36, 39
OWN, DOWN, UP = 0, 1, 2


def works_ahead():
    return lax.axis_index("circ") % 4 != 0


def inner_work(turned, left, keep):
    nrad = turned.shape[1] // 8
    outside = outside_mask()
    last = nrad - 1
    adds, middle, stiff = {}, {}, {}

    def leave(side, at, arrays):
        for j, x in enumerate(arrays):
            left[side, at + j] = x

    for plane in range(nrad):
        v, e = cells_of(turned, plane, 0, 3), cells_of(turned, plane, 3, 4)[0]
        adds[plane] = [a + b for a, b in zip(moved(v, e), weighed(e))]
        if plane == 0:
            leave(0, BEYOND, adds[0][DOWN])
        if plane == 1:
            leave(0, EDGE, plus(adds[0][OWN], adds[1][DOWN]))
        if plane == last:
            leave(1, EDGE, plus(adds[last][OWN], adds[last - 1][UP]))
            leave(1, BEYOND, adds[last][UP])
        at = plane - 1
        if at < 1:
            continue
        v, e = cells_of(turned, at, 0, 3), cells_of(turned, at, 3, 4)[0]
        part = plus(adds[at - 1][UP], adds[at][OWN], adds[at + 1][DOWN])
        stiff[at] = stiffness(e, part[6:])
        rest = remainder(v, e, cells_of(turned, at, 4, 7), stiff[at], part)
        middle[at] = [jnp.where(outside, 0.0, x) for x in relaxed(v, stiff[at], rest)]

    adds = {}
    for plane in range(1, last):
        e = cells_of(turned, plane, 3, 4)[0]
        adds[plane] = moved(middle[plane], e)
        if plane == 1:
            leave(0, CARRY, adds[1][DOWN])
        if plane == last - 1:
            leave(1, CARRY, adds[last - 1][UP])
        for at in (plane - 1, plane):
            if at < 1 or (at == plane and plane < last - 1):
                continue
            beside = []
            if at - 1 in adds:
                beside.append(adds[at - 1][UP])
            if at + 1 in adds:
                beside.append(adds[at + 1][DOWN])
            part = plus(adds[at][OWN], *beside)
            v, e = middle[at], cells_of(turned, at, 3, 4)[0]
            rest = remainder(v, e, cells_of(turned, at, 4, 7), stiff[at], part)
            if len(beside) == 2:
                put_final(keep, at, relaxed(v, stiff[at], rest))
            else:
                side = 0 if at == 1 else 1
                leave(side, REST, rest)
                leave(side, HELD, v)
                leave(side, SCALE, stiff[at][1])


def inner_kernel(turned, left_in, keep_in, ids, left, keep, pick, nodes, sem):
    copy = pltpu.make_async_copy(ids, nodes, sem)
    copy.start()
    ahead = works_ahead()

    @pl.when(ahead)
    def _():
        left[...] = left_in[...]
        keep[...] = keep_in[...]

    @pl.when(jnp.logical_not(ahead))
    def _():
        inner_work(turned, left, keep)

    copy.wait()
    cell = lax.broadcasted_iota(jnp.int32, pick.shape, 0)
    pick[...] = jnp.where(cell == nodes[...] % 256, 1.0, 0.0).astype(BF16)


def sweep_kernel(
    turned, got_second, got_first, left, kept, keep
):
    nrad = turned.shape[1] // 8
    rad = lax.axis_index("rad")
    odd = rad % 2 == 1
    outside = outside_mask()

    def halo(side, j, first, last):
        def tile(index):
            if index == 14:
                at = 22 + j
            elif index >= 8:
                at = 16 + index - 8
            else:
                at = 2 * index + j
            a, b = got_first[at], got_second[at]
            return jnp.where(odd, b, a) if side else jnp.where(odd, a, b)

        ends = tile(14)
        return [field_of(tile, f, ends) for f in range(first, last)]

    def handed(side, at, count):
        return [left[side, at + j] for j in range(count)]

    for side in range(2):
        inward = DOWN if side else UP
        near, far = (0, 1) if side else (1, 0)
        edge, next_in = (nrad - 1, nrad - 2) if side else (0, 1)
        v, e = halo(side, far, 0, 3), halo(side, far, 3, 4)[0]
        beyond = moved(v, e)[inward] + weighed(e)[inward]
        v, e = halo(side, near, 0, 3), halo(side, near, 3, 4)[0]
        here = [a + b for a, b in zip(moved(v, e), weighed(e))]
        part = plus(handed(side, BEYOND, 12), here[OWN], beyond)
        stiff = stiffness(e, part[6:])
        rest = remainder(v, e, halo(side, near, 4, 7), stiff, part)
        drop = outside | (rad == (lax.axis_size("rad") - 1 if side else 0))
        beside = moved([jnp.where(drop, 0.0, x) for x in relaxed(v, stiff, rest)], e)

        v, e = cells_of(turned, edge, 0, 3), cells_of(turned, edge, 3, 4)[0]
        rhs = cells_of(turned, edge, 4, 7)
        part = plus(handed(side, EDGE, 12), here[inward])
        stiff = stiffness(e, part[6:])
        v = [jnp.where(outside, 0.0, x) for x in relaxed(v, stiff, remainder(v, e, rhs, stiff, part))]
        here = moved(v, e)
        part = plus(handed(side, CARRY, 6), here[OWN], beside[inward])
        put_final(keep, edge, relaxed(v, stiff, remainder(v, e, rhs, stiff, part)))

        e = cells_of(turned, next_in, 3, 4)[0]
        add, rest = here[inward], handed(side, REST, 3)
        v, scale = handed(side, HELD, 3), handed(side, SCALE, 3)
        put_final(
            keep, next_in, [v[i] + scale[i] * (rest[i] + e * add[i] + add[3 + i]) for i in range(3)]
        )

    inside = slice(16, 8 * (nrad - 2))
    for index in range(6):
        keep[index, inside, :] = kept[index, inside, :]

def plane_of(keep, i, c, nrad):
    both = [keep[2 * i + t, pl.ds(c, nrad, stride=8), :] for t in range(2)]
    return jnp.concatenate(both, axis=1)


def emit_kernel(keep, adjoint):
    _, ncirc, nrad, _ = adjoint.shape
    for i in range(3):
        for c in range(ncirc):
            adjoint[i, c] = plane_of(keep, i, c, nrad)


def finish_kernel(keep, parts, adjoint, own, result, total, sems):
    emit_kernel(keep, result)
    first = pltpu.make_async_copy(result, adjoint, sems.at[0])
    first.start()
    total[...] = jnp.sum(parts[...], axis=0)[:, : total.shape[1]]
    second = pltpu.make_async_copy(total, own, sems.at[1])
    second.start()
    first.wait()
    second.wait()


def force_kernel(devices, ncirc, keep, pick, ids, shapes, force, sums_of):
    nrad = keep.shape[1] // 8
    lines = ncirc * nrad
    flat = jnp.concatenate([plane_of(keep, i, c, nrad) for i in range(3) for c in range(ncirc)], axis=0)
    high, low = split(flat)
    table = jnp.concatenate([high, low], axis=0).astype(BF16)
    node = ids[...]
    rows = jnp.dot(table, pick[...], preferred_element_type=F32)
    rows = rows[: 3 * lines] + rows[3 * lines :]
    line = lax.broadcasted_iota(jnp.int32, (lines, node.shape[1]), 0)
    hit = line == node // 256
    picked = [
        jnp.sum(jnp.where(hit, rows[lines * i : lines * (i + 1)], 0.0), axis=0, keepdims=True)
        for i in range(3)
    ]
    weighted = sum(shapes[i] * picked[i] for i in range(3))
    sums_of[...] = jnp.broadcast_to(jnp.sum(weighted, axis=1, keepdims=True), sums_of.shape)
    owned = sums_of.shape[0] // devices
    lane = lax.broadcasted_iota(jnp.int32, (devices, 128), 1)
    out = jnp.zeros((devices, 128), F32)
    for j in range(owned):
        out = jnp.where(lane == j, sums_of[pl.ds(j, devices, stride=owned), :], out)
    for r in range(force.shape[0] // devices):
        force[devices * r : devices * (r + 1), 0, :] = out


def swaps(axis, start, wrap):
    count = lax.axis_size(axis)
    pairs = []
    for i in range(start, count, 2):
        j = (i + 1) % count
        if j > i or wrap:
            pairs += [(i, j), (j, i)]
    return pairs


VMEM = pl.BlockSpec(memory_space=pltpu.VMEM)
HBM = pl.BlockSpec(memory_space=pltpu.HBM)


def call(kernel, ins, outs, scratch=(), flops=1_000_000, limit=40 * 1024 * 1024, out_specs=None):
    outs = [o if isinstance(o, jax.ShapeDtypeStruct) else jax.ShapeDtypeStruct(o, F32) for o in outs]
    return pl.pallas_call(
        kernel,
        out_shape=outs,
        in_specs=ins,
        out_specs=out_specs or [VMEM] * len(outs),
        scratch_shapes=list(scratch),
        compiler_params=pltpu.CompilerParams(vmem_limit_bytes=limit),
        cost_estimate=pl.CostEstimate(flops=flops, bytes_accessed=1_000_000, transcendentals=0),
    )


def on_device(
    adjoint_prev, cell_class, class_moduli, flow_sens, flow_nodes, flow_count, surf_ids, mode_shapes
):
    _, ncirc, nrad, naxial = adjoint_prev.shape
    n_mode, n_rad = lax.axis_size("mode"), lax.axis_size("rad")
    slots = flow_nodes.shape[-1]
    lines = ncirc * nrad
    cells = (ncirc, nrad, naxial)
    message = (24, 8, 128)
    args = (
        class_moduli, flow_count[0, 0, 0], adjoint_prev, cell_class,
        jnp.swapaxes(flow_sens[0, 0, 0], 0, 1), flow_nodes[0, 0, 0],
    )
    send, e = call(
        pack_kernel,
        [HBM] * 6,
        [(n_mode, 24, 128), cells],
        [pltpu.SMEM(x.shape, x.dtype) for x in args[:2]]
        + [pltpu.VMEM(x.shape, x.dtype) for x in args[2:]]
        + [pltpu.SemaphoreType.DMA((6,))],
        limit=63 * 1024 * 1024 + 512 * 1024,
    )(*args)
    got = lax.all_to_all(send, "mode", split_axis=0, concat_axis=0, tiled=True)
    rhs, ends, first, second = call(
        scatter_kernel,
        [VMEM] * 3,
        [(3,) + cells, (ncirc, nrad, 128), message, message],
    )(got, adjoint_prev, e)
    n_circ = lax.axis_size("circ")
    first = lax.ppermute(first, "circ", [(i, (i + 1) % n_circ) for i in range(n_circ)])
    second = lax.ppermute(second, "circ", [((i + 1) % n_circ, i) for i in range(n_circ)])
    kept = (6, 8 * nrad, 128)
    left = (2, COUNT, 8, 384)
    turned, first, second, left, keep = call(
        turn_kernel, [VMEM] * 6, [(15, 8 * nrad, 128), message, message, left, kept]
    )(
        adjoint_prev, e, rhs, ends, first, second
    )
    second = lax.ppermute(second, "rad", swaps("rad", 1, False))
    first = lax.ppermute(first, "rad", swaps("rad", 0, False))
    modes = mode_shapes.shape[3]
    owned = modes // n_mode
    ids = surf_ids[0, 0]
    shapes = jnp.swapaxes(mode_shapes[0, 0, 0], 0, 1)
    left, keep, pick = call(
        inner_kernel,
        [VMEM] * 3 + [HBM],
        [left.shape, kept, jax.ShapeDtypeStruct((naxial, ids.shape[1]), BF16)],
        [pltpu.VMEM(ids.shape, ids.dtype), pltpu.SemaphoreType.DMA],
        flops=10_000_000,
    )(turned, left, keep, ids)
    (keep,) = call(sweep_kernel, [VMEM] * 5, [kept])(turned, second, first, left, keep)
    (force,) = call(
        functools.partial(force_kernel, n_mode, ncirc),
        [VMEM] * 4,
        [(n_rad * n_mode, 1, 128)],
        [pltpu.VMEM((modes, 128), F32)],
    )(keep, pick, ids, shapes)
    parts = lax.all_to_all(force, ("rad", "mode"), split_axis=0, concat_axis=0, tiled=True)
    final, own_force = call(
        finish_kernel,
        [VMEM] * 2,
        [adjoint_prev.shape, (1, owned)],
        [
            pltpu.VMEM(adjoint_prev.shape, F32), pltpu.VMEM((1, owned), F32),
            pltpu.SemaphoreType.DMA((2,)),
        ],
        out_specs=[HBM, HBM],
    )(keep, parts)
    return (final, own_force.reshape(owned, 1))


def solution(mesh):
    in_specs = (
        P(None, "circ", "rad", "mode"),
        P("circ", "rad", "mode"),
        P(),
        P("circ", "rad", "mode", None, None, None),
        P("circ", "rad", "mode", None, None),
        P("circ", "rad", "mode", None),
        P("circ", "rad", "mode", None),
        P("circ", "rad", "mode", None, None, None),
    )
    out_specs = (P(None, "circ", "rad", "mode"), P("mode", "circ"))
    return jax.shard_map(
        on_device, mesh=mesh, in_specs=in_specs, out_specs=out_specs, check_vma=False
    )
```

```python
import functools

import jax
import jax.numpy as jnp
from jax import lax
from jax.experimental import pallas as pl
from jax.experimental.pallas import tpu as pltpu
from jax.sharding import PartitionSpec as P

coupling = 0.5
relaxation = 0.6

face_own, face_other = 0.5 * (1.0 + coupling), 0.5
edge_own, edge_other = 0.25 * (1.0 + 0.5 * coupling), 0.25
corner_own = (1.0 + coupling / 3.0) / 6.0
edge_cross = 0.25 * coupling / 2.0
corner_cross = coupling / 18.0
centre_weight = 2 * face_own + 4 * face_other + 8 * edge_own + 4 * edge_other + 8 * corner_own

F32 = jnp.float32
BF16 = jnp.bfloat16
NT = (((1,), (1,)), ((), ()))


def split(x):
    high = x.astype(BF16).astype(F32)
    return high, x - high


def pack_kernel(
    moduli_in, count_in, prev_in, cls_in, sens_in, nodes_in, send, e_out,
    moduli, count, prev, cls, sens, nodes, sems,
):
    copies = [
        pltpu.make_async_copy(source, target, sems.at[i])
        for i, (source, target) in enumerate(
            (
                (sens_in, sens), (nodes_in, nodes), (prev_in, prev), (cls_in, cls),
                (count_in, count), (moduli_in, moduli),
            )
        )
    ]
    for copy in copies:
        copy.start()
    for copy in copies:
        copy.wait()
    _, blocks, slots = sens.shape
    ncirc, nrad, naxial = cls.shape
    lines = ncirc * nrad
    k = lax.axis_index("mode")
    lane = lax.broadcasted_iota(jnp.int32, (nrad, 128), 1)
    columns = []
    for c in range(ncirc):
        level = cls[c]
        e = jnp.zeros(level.shape, F32)
        for i in range(moduli.shape[0]):
            e = jnp.where(level == i, moduli[i], e)
        e_out[c] = e
        ends = jnp.zeros((nrad, 128), F32)
        for f in range(4):
            field = prev[f, c] if f < 3 else e
            first = pltpu.roll(field[:, :128], 4 * f + 2, 1)
            last = pltpu.roll(field[:, naxial - 128 :], 4 * f + 2, 1)
            ends = jnp.where((lane == 4 * f + 2) | (lane == 4 * f + 3), first, ends)
            ends = jnp.where((lane == 4 * f) | (lane == 4 * f + 1), last, ends)
        columns.append(ends)
    columns.append(jnp.zeros((128 - lines, 128), F32))
    items = jnp.concatenate(columns, axis=0).T
    halo = items[:8] + pltpu.roll(items[8:16], 32, 1)
    tall = lax.broadcasted_iota(jnp.int32, (8, 128), 0)
    to_high = jnp.where(tall % 4 < 2, halo, 0.0)
    to_low = halo - to_high

    node = nodes[...]
    axial, line = node % naxial, node // naxial
    key = jnp.where(axial == 0, line, jnp.where(axial == naxial - 1, line + lines, -1))
    key = key.astype(F32).astype(BF16)
    place = lax.broadcasted_iota(jnp.int32, (2 * lines, slots), 0).astype(F32).astype(BF16)
    slot = lax.broadcasted_iota(jnp.int32, (1, slots), 1)
    row = lax.broadcasted_iota(jnp.int32, (16, slots), 0) // 2
    zero, one = BF16(0.0), BF16(1.0)
    planes = []
    for d in range(blocks):
        live = slot < count[d]
        tile = jnp.zeros((16, slots), F32)
        for i in range(3):
            value = jnp.where(live, sens[i, d : d + 1], 0.0)
            for q in range(slots // 128):
                send[d, 4 * (i + 1) + q : 4 * (i + 1) + q + 1, :] = value[:, 128 * q : 128 * (q + 1)]
            high, low = split(value)
            tile = jnp.where(row == i, high, jnp.where(row == 4 + i, low, tile))
        for q in range(slots // 128):
            send[d, q : q + 1, :] = node[d : d + 1, 128 * q : 128 * (q + 1)].astype(F32)
        hits = jnp.where(place == jnp.broadcast_to(key[d : d + 1], place.shape), one, zero)
        plane = lax.dot_general(tile.astype(BF16), hits, NT, preferred_element_type=F32)
        plane = jnp.concatenate([plane[:8] + plane[8:], jnp.zeros((8, 128 - 2 * lines), F32)], axis=1)
        planes.append(plane)
    group = lax.broadcasted_iota(jnp.int32, (8, 128), 1) // lines == 2
    even, odd = group & (tall % 2 == 0), group & (tall % 2 == 1)
    for d in range(blocks):
        out = jnp.where(k == d + 1, to_low, 0.0) + jnp.where(k == d - 1, to_high, 0.0)
        if d + 1 < blocks:
            out = jnp.where(odd, pltpu.roll(planes[d + 1], 2 * lines, 1), out)
        if d > 0:
            out = jnp.where(even, pltpu.roll(planes[d - 1], lines, 1), out)
        send[d, 16:24, :] = out


def scatter_kernel(got, prev, e, rhs, ends, first, second):
    blocks = got.shape[0]
    _, ncirc, nrad, naxial = prev.shape
    lines = ncirc * nrad
    row = lax.broadcasted_iota(jnp.int32, (lines, 128), 0).astype(F32).astype(BF16)
    cell = lax.broadcasted_iota(jnp.int32, (128, naxial), 1).astype(F32).astype(BF16)
    nodes = jnp.concatenate([got[d, :4, :] for d in range(blocks)], axis=0).astype(jnp.int32)
    line = (nodes // naxial).astype(F32).astype(BF16)
    tall = jnp.concatenate([nodes % naxial, jnp.zeros((128 - 4 * blocks, 128), jnp.int32)], axis=0)
    tall = tall.astype(F32).T.astype(BF16)
    zero, one = BF16(0.0), BF16(1.0)
    dense = jnp.zeros((6 * lines, naxial), F32)
    for d in range(blocks):
        left, right = [], []
        for q in range(4):
            g = 4 * d + q
            at = jnp.broadcast_to(tall[:, g : g + 1], cell.shape)
            right.append(jnp.where(cell == at, one, zero))
            hit = row == jnp.broadcast_to(line[g : g + 1], row.shape)
            column = []
            for i in range(3):
                for part in split(got[d, 4 * (i + 1) + q : 4 * (i + 1) + q + 1, :]):
                    column.append(jnp.where(hit, jnp.broadcast_to(part.astype(BF16), row.shape), zero))
            left.append(jnp.concatenate(column, axis=0))
        left, right = jnp.concatenate(left, axis=1), jnp.concatenate(right, axis=0)
        dense = dense + jnp.dot(left, right, preferred_element_type=F32)
    for i in range(3):
        total = dense[2 * lines * i : 2 * lines * i + lines] + dense[2 * lines * i + lines : 2 * lines * (i + 1)]
        for c in range(ncirc):
            rhs[i, c] = total[nrad * c : nrad * (c + 1)]
    total = got[0, 16:24, :]
    for d in range(1, blocks):
        total = total + got[d, 16:24, :]
    groups = [total, pltpu.roll(total, 128 - lines, 1), pltpu.roll(total, 128 - 2 * lines, 1)]
    columns = jnp.concatenate(groups + [jnp.zeros((104, 128), F32)], axis=0).T
    for c in range(ncirc):
        ends[c] = columns[nrad * c : nrad * (c + 1)]
    for out, base, edge in ((first, ncirc - 2, ncirc - 1), (second, 0, 0)):
        for t in range(2):
            cut = slice(128 * t, 128 * (t + 1))
            for f in range(4):
                for j in range(2):
                    source = prev[f, base + j] if f < 3 else e[base + j]
                    out[4 * f + 2 * t + j] = source[:, cut]
            for i in range(3):
                out[16 + 2 * i + t] = rhs[i, edge][:, cut]
        for j in range(2):
            out[22 + j] = ends[base + j]


def turn_kernel(prev, e, rhs, ends, got_first, got_second, turned, first, second, left, keep):
    _, ncirc, nrad, _ = prev.shape
    def put(index, c, plane):
        turned[index, pl.ds(c, nrad, stride=8), :] = plane

    for c in range(ncirc):
        for t in range(2):
            cut = slice(128 * t, 128 * (t + 1))
            for f in range(4):
                source = prev[f, c] if f < 3 else e[c]
                put(2 * f + t, c, source[:, cut])
            for i in range(3):
                put(8 + 2 * i + t, c, rhs[i, c][:, cut])
        put(14, c, ends[c])

    def sides(tile):
        return got_first[tile], got_second[tile]

    for index in range(8):
        for j in range(2):
            low, high = sides(2 * index + j)
            put(index, 6 + j, low)
            put(index, 4 + j, high)
    for index in range(6):
        low, high = sides(16 + index)
        put(8 + index, 7, low)
        put(8 + index, 4, high)
        put(8 + index, 6, low)
        put(8 + index, 5, high)
    for j in range(2):
        low, high = sides(22 + j)
        put(14, 6 + j, low)
        put(14, 4 + j, high)

    odd = lax.axis_index("rad") % 2
    for out, at_high in ((first, 1 - odd), (second, odd)):
        for index in range(15):
            for j in range(2):
                plane = at_high * (nrad - 2) + j
                at = 2 * index + j
                if 8 <= index < 14:
                    if j:
                        continue
                    plane = at_high * (nrad - 1)
                    at = 16 + index - 8
                elif index == 14:
                    at = 22 + j
                out[at] = turned[index, pl.ds(pl.multiple_of(8 * plane, 8), 8), :]

    @pl.when(works_ahead())
    def _():
        inner_work(turned, left, keep)


def sums(x):
    up = pltpu.roll(x, x.shape[1] - 1, 1)
    down = pltpu.roll(x, 1, 1)
    return up + down, up - down


def across(x):
    up = pltpu.roll(x, 7, 0)
    down = pltpu.roll(x, 1, 0)
    return up + down, up - down


def spread(x):
    sn, dn = sums(x)
    sm, dm = across(x)
    smsn, dmsn = across(sn)
    smdn, dmdn = across(dn)
    return sn, dn, sm, dm, smsn, dmsn, smdn, dmdn


def leading_terms(x, s):
    sn, _, sm, _, both = s[0], s[1], s[2], s[3], s[4]
    near = sm + sn
    return face_other * near + edge_other * both, face_own * x + edge_own * near + corner_own * both


def plane_terms(x, own, other, both):
    centre = face_own * own + face_other * other + edge_own * both
    side = face_other * x + edge_own * own + edge_other * other + corner_own * both
    return centre, side


def cross_terms(s):
    _, dn, _, dm, _, dmsn, smdn, dmdn = s
    return edge_cross * dm + corner_cross * dmsn, edge_cross * dn + corner_cross * smdn, dmdn


def vector_terms(v):
    s0, s1, s2 = spread(v[0]), spread(v[1]), spread(v[2])
    p0, q0 = plane_terms(v[0], s0[2], s0[0], s0[4])
    p1, q1 = leading_terms(v[1], s1)
    p2, q2 = plane_terms(v[2], s2[0], s2[2], s2[4])
    rm0, _, w0 = cross_terms(s0)
    rm1, rn1, _ = cross_terms(s1)
    _, rn2, w2 = cross_terms(s2)
    p0 = p0 + edge_cross * w2
    q0 = q0 + corner_cross * w2
    p2 = p2 + edge_cross * w0
    q2 = q2 + corner_cross * w0
    d0, d1, d2 = rm1, rm0 + rn2, rn1
    return (p0, p1, p2), (q0 + d0, q1 + d1, q2 + d2), (q0 - d0, q1 - d1, q2 - d2)


def scalar_terms(e):
    s = spread(e)
    p0, q0 = plane_terms(e, s[2], s[0], s[4])
    p1, q1 = leading_terms(e, s)
    p2, q2 = plane_terms(e, s[0], s[2], s[4])
    rm, rn, w = cross_terms(s)
    return (p0, p1, p2), (q0, q1, q2), rm, rn, w


def moved(v, e):
    plain, scaled = vector_terms(v), vector_terms([e * x for x in v])
    return [list(plain[j]) + list(scaled[j]) for j in range(3)]


def weighed(e):
    p, q, rm, rn, w = scalar_terms(e)
    zero = jnp.zeros_like(w)
    side = corner_cross * w
    return [
        list(p) + [zero, zero, edge_cross * w],
        list(q) + [rm, rn, side],
        list(q) + [-rm, -rn, side],
    ]


def plus(*parts):
    return [functools.reduce(lambda a, b: a + b, column) for column in zip(*parts)]


def stiffness(e, part):
    diag = [centre_weight * e + x for x in part[:3]]
    return diag, [relaxation / x for x in diag], part[3], part[4], part[5]


def remainder(v, e, rhs, stiff, part):
    (d0, d1, d2), _, c01, c12, c02 = stiff
    own = (
        d0 * v[0] + c01 * v[1] + c02 * v[2],
        c01 * v[0] + d1 * v[1] + c12 * v[2],
        c02 * v[0] + c12 * v[1] + d2 * v[2],
    )
    return [rhs[i] - own[i] + e * part[i] + part[3 + i] for i in range(3)]


def relaxed(v, stiff, rest):
    return [v[i] + stiff[1][i] * rest[i] for i in range(3)]


def outside_mask():
    lane = lax.broadcasted_iota(jnp.int32, (8, 384), 1)
    mode = lax.axis_index("mode")
    return ((lane == 383) & (mode == 0)) | ((lane == 256) & (mode == lax.axis_size("mode") - 1))


def own_tile(turned, index, plane):
    return turned[index, 8 * plane : 8 * (plane + 1), :]


def field_of(tile, f, ends):
    shift = 4 * f + 2 if f < 4 else 17 + 2 * (f - 4)
    return jnp.concatenate([tile(2 * f), tile(2 * f + 1), pltpu.roll(ends, 128 - shift, 1)], axis=1)


def cells_of(turned, plane, first, last):
    tile = lambda index: own_tile(turned, index, plane)
    ends = tile(14)
    return [field_of(tile, f, ends) for f in range(first, last)]


def put_final(keep, plane, final):
    for i in range(3):
        for t in range(2):
            keep[2 * i + t, 8 * plane : 8 * (plane + 1), :] = final[i][:, 128 * t : 128 * (t + 1)]


BEYOND, EDGE, CARRY, REST, HELD, SCALE, COUNT = 0, 12, 24, 30, 33, 36, 39
OWN, DOWN, UP = 0, 1, 2


def works_ahead():
    return lax.axis_index("circ") % 4 != 0


def inner_work(turned, left, keep):
    nrad = turned.shape[1] // 8
    outside = outside_mask()
    last = nrad - 1
    adds, middle, stiff = {}, {}, {}

    def leave(side, at, arrays):
        for j, x in enumerate(arrays):
            left[side, at + j] = x

    for plane in range(nrad):
        v, e = cells_of(turned, plane, 0, 3), cells_of(turned, plane, 3, 4)[0]
        adds[plane] = [a + b for a, b in zip(moved(v, e), weighed(e))]
        if plane == 0:
            leave(0, BEYOND, adds[0][DOWN])
        if plane == 1:
            leave(0, EDGE, plus(adds[0][OWN], adds[1][DOWN]))
        if plane == last:
            leave(1, EDGE, plus(adds[last][OWN], adds[last - 1][UP]))
            leave(1, BEYOND, adds[last][UP])
        at = plane - 1
        if at < 1:
            continue
        v, e = cells_of(turned, at, 0, 3), cells_of(turned, at, 3, 4)[0]
        part = plus(adds[at - 1][UP], adds[at][OWN], adds[at + 1][DOWN])
        stiff[at] = stiffness(e, part[6:])
        rest = remainder(v, e, cells_of(turned, at, 4, 7), stiff[at], part)
        middle[at] = [jnp.where(outside, 0.0, x) for x in relaxed(v, stiff[at], rest)]

    adds = {}
    for plane in range(1, last):
        e = cells_of(turned, plane, 3, 4)[0]
        adds[plane] = moved(middle[plane], e)
        if plane == 1:
            leave(0, CARRY, adds[1][DOWN])
        if plane == last - 1:
            leave(1, CARRY, adds[last - 1][UP])
        for at in (plane - 1, plane):
            if at < 1 or (at == plane and plane < last - 1):
                continue
            beside = []
            if at - 1 in adds:
                beside.append(adds[at - 1][UP])
            if at + 1 in adds:
                beside.append(adds[at + 1][DOWN])
            part = plus(adds[at][OWN], *beside)
            v, e = middle[at], cells_of(turned, at, 3, 4)[0]
            rest = remainder(v, e, cells_of(turned, at, 4, 7), stiff[at], part)
            if len(beside) == 2:
                put_final(keep, at, relaxed(v, stiff[at], rest))
            else:
                side = 0 if at == 1 else 1
                leave(side, REST, rest)
                leave(side, HELD, v)
                leave(side, SCALE, stiff[at][1])


def inner_kernel(turned, left_in, keep_in, ids, left, keep, pick, nodes, sem):
    copy = pltpu.make_async_copy(ids, nodes, sem)
    copy.start()
    ahead = works_ahead()

    @pl.when(ahead)
    def _():
        left[...] = left_in[...]
        keep[...] = keep_in[...]

    @pl.when(jnp.logical_not(ahead))
    def _():
        inner_work(turned, left, keep)

    copy.wait()
    cell = lax.broadcasted_iota(jnp.int32, pick.shape, 0)
    pick[...] = jnp.where(cell == nodes[...] % 256, 1.0, 0.0).astype(BF16)


def sweep_kernel(
    devices, ncirc, turned, got_second, got_first, left, kept, pick, ids, shapes, keep, force, sums_of
):
    nrad = turned.shape[1] // 8
    rad = lax.axis_index("rad")
    odd = rad % 2 == 1
    outside = outside_mask()

    def halo(side, j, first, last):
        def tile(index):
            if index == 14:
                at = 22 + j
            elif index >= 8:
                at = 16 + index - 8
            else:
                at = 2 * index + j
            a, b = got_first[at], got_second[at]
            return jnp.where(odd, b, a) if side else jnp.where(odd, a, b)

        ends = tile(14)
        return [field_of(tile, f, ends) for f in range(first, last)]

    def handed(side, at, count):
        return [left[side, at + j] for j in range(count)]

    for side in range(2):
        inward = DOWN if side else UP
        near, far = (0, 1) if side else (1, 0)
        edge, next_in = (nrad - 1, nrad - 2) if side else (0, 1)
        v, e = halo(side, far, 0, 3), halo(side, far, 3, 4)[0]
        beyond = moved(v, e)[inward] + weighed(e)[inward]
        v, e = halo(side, near, 0, 3), halo(side, near, 3, 4)[0]
        here = [a + b for a, b in zip(moved(v, e), weighed(e))]
        part = plus(handed(side, BEYOND, 12), here[OWN], beyond)
        stiff = stiffness(e, part[6:])
        rest = remainder(v, e, halo(side, near, 4, 7), stiff, part)
        drop = outside | (rad == (lax.axis_size("rad") - 1 if side else 0))
        beside = moved([jnp.where(drop, 0.0, x) for x in relaxed(v, stiff, rest)], e)

        v, e = cells_of(turned, edge, 0, 3), cells_of(turned, edge, 3, 4)[0]
        rhs = cells_of(turned, edge, 4, 7)
        part = plus(handed(side, EDGE, 12), here[inward])
        stiff = stiffness(e, part[6:])
        v = [jnp.where(outside, 0.0, x) for x in relaxed(v, stiff, remainder(v, e, rhs, stiff, part))]
        here = moved(v, e)
        part = plus(handed(side, CARRY, 6), here[OWN], beside[inward])
        put_final(keep, edge, relaxed(v, stiff, remainder(v, e, rhs, stiff, part)))

        e = cells_of(turned, next_in, 3, 4)[0]
        add, rest = here[inward], handed(side, REST, 3)
        v, scale = handed(side, HELD, 3), handed(side, SCALE, 3)
        put_final(
            keep, next_in, [v[i] + scale[i] * (rest[i] + e * add[i] + add[3 + i]) for i in range(3)]
        )

    inside = slice(16, 8 * (nrad - 2))
    for index in range(6):
        keep[index, inside, :] = kept[index, inside, :]
    force_of(devices, ncirc, keep, pick, ids, shapes, force, sums_of)

def plane_of(keep, i, c, nrad):
    both = [keep[2 * i + t, pl.ds(c, nrad, stride=8), :] for t in range(2)]
    return jnp.concatenate(both, axis=1)


def emit_kernel(keep, adjoint):
    _, ncirc, nrad, _ = adjoint.shape
    for i in range(3):
        for c in range(ncirc):
            adjoint[i, c] = plane_of(keep, i, c, nrad)


def finish_kernel(keep, parts, adjoint, own, result, total, sems):
    emit_kernel(keep, result)
    first = pltpu.make_async_copy(result, adjoint, sems.at[0])
    first.start()
    total[...] = jnp.sum(parts[...], axis=0)[:, : total.shape[1]]
    second = pltpu.make_async_copy(total, own, sems.at[1])
    second.start()
    first.wait()
    second.wait()


def force_of(devices, ncirc, keep, pick, ids, shapes, force, sums_of):
    nrad = keep.shape[1] // 8
    lines = ncirc * nrad
    flat = jnp.concatenate([plane_of(keep, i, c, nrad) for i in range(3) for c in range(ncirc)], axis=0)
    high, low = split(flat)
    table = jnp.concatenate([high, low], axis=0).astype(BF16)
    node = ids[...]
    rows = jnp.dot(table, pick[...], preferred_element_type=F32)
    rows = rows[: 3 * lines] + rows[3 * lines :]
    line = lax.broadcasted_iota(jnp.int32, (lines, node.shape[1]), 0)
    hit = line == node // 256
    picked = [
        jnp.sum(jnp.where(hit, rows[lines * i : lines * (i + 1)], 0.0), axis=0, keepdims=True)
        for i in range(3)
    ]
    weighted = sum(shapes[i] * picked[i] for i in range(3))
    sums_of[...] = jnp.broadcast_to(jnp.sum(weighted, axis=1, keepdims=True), sums_of.shape)
    owned = sums_of.shape[0] // devices
    lane = lax.broadcasted_iota(jnp.int32, (devices, 128), 1)
    out = jnp.zeros((devices, 128), F32)
    for j in range(owned):
        out = jnp.where(lane == j, sums_of[pl.ds(j, devices, stride=owned), :], out)
    for r in range(force.shape[0] // devices):
        force[devices * r : devices * (r + 1), 0, :] = out


def swaps(axis, start, wrap):
    count = lax.axis_size(axis)
    pairs = []
    for i in range(start, count, 2):
        j = (i + 1) % count
        if j > i or wrap:
            pairs += [(i, j), (j, i)]
    return pairs


VMEM = pl.BlockSpec(memory_space=pltpu.VMEM)
HBM = pl.BlockSpec(memory_space=pltpu.HBM)


def call(kernel, ins, outs, scratch=(), flops=1_000_000, limit=40 * 1024 * 1024, out_specs=None):
    outs = [o if isinstance(o, jax.ShapeDtypeStruct) else jax.ShapeDtypeStruct(o, F32) for o in outs]
    return pl.pallas_call(
        kernel,
        out_shape=outs,
        in_specs=ins,
        out_specs=out_specs or [VMEM] * len(outs),
        scratch_shapes=list(scratch),
        compiler_params=pltpu.CompilerParams(vmem_limit_bytes=limit),
        cost_estimate=pl.CostEstimate(flops=flops, bytes_accessed=1_000_000, transcendentals=0),
    )


def on_device(
    adjoint_prev, cell_class, class_moduli, flow_sens, flow_nodes, flow_count, surf_ids, mode_shapes
):
    _, ncirc, nrad, naxial = adjoint_prev.shape
    n_mode, n_rad = lax.axis_size("mode"), lax.axis_size("rad")
    slots = flow_nodes.shape[-1]
    lines = ncirc * nrad
    cells = (ncirc, nrad, naxial)
    message = (24, 8, 128)
    args = (
        class_moduli, flow_count[0, 0, 0], adjoint_prev, cell_class,
        jnp.swapaxes(flow_sens[0, 0, 0], 0, 1), flow_nodes[0, 0, 0],
    )
    send, e = call(
        pack_kernel,
        [HBM] * 6,
        [(n_mode, 24, 128), cells],
        [pltpu.SMEM(x.shape, x.dtype) for x in args[:2]]
        + [pltpu.VMEM(x.shape, x.dtype) for x in args[2:]]
        + [pltpu.SemaphoreType.DMA((6,))],
        limit=63 * 1024 * 1024 + 512 * 1024,
    )(*args)
    got = lax.all_to_all(send, "mode", split_axis=0, concat_axis=0, tiled=True)
    rhs, ends, first, second = call(
        scatter_kernel,
        [VMEM] * 3,
        [(3,) + cells, (ncirc, nrad, 128), message, message],
    )(got, adjoint_prev, e)
    n_circ = lax.axis_size("circ")
    first = lax.ppermute(first, "circ", [(i, (i + 1) % n_circ) for i in range(n_circ)])
    second = lax.ppermute(second, "circ", [((i + 1) % n_circ, i) for i in range(n_circ)])
    kept = (6, 8 * nrad, 128)
    left = (2, COUNT, 8, 384)
    turned, first, second, left, keep = call(
        turn_kernel, [VMEM] * 6, [(15, 8 * nrad, 128), message, message, left, kept]
    )(
        adjoint_prev, e, rhs, ends, first, second
    )
    second = lax.ppermute(second, "rad", swaps("rad", 1, False))
    first = lax.ppermute(first, "rad", swaps("rad", 0, False))
    modes = mode_shapes.shape[3]
    owned = modes // n_mode
    ids = surf_ids[0, 0]
    shapes = jnp.swapaxes(mode_shapes[0, 0, 0], 0, 1)
    left, keep, pick = call(
        inner_kernel,
        [VMEM] * 3 + [HBM],
        [left.shape, kept, jax.ShapeDtypeStruct((naxial, ids.shape[1]), BF16)],
        [pltpu.VMEM(ids.shape, ids.dtype), pltpu.SemaphoreType.DMA],
        flops=10_000_000,
    )(turned, left, keep, ids)
    keep, force = call(
        functools.partial(sweep_kernel, n_mode, ncirc),
        [VMEM] * 8,
        [kept, (n_rad * n_mode, 1, 128)],
        [pltpu.VMEM((modes, 128), F32)],
    )(turned, second, first, left, keep, pick, ids, shapes)
    parts = lax.all_to_all(force, ("rad", "mode"), split_axis=0, concat_axis=0, tiled=True)
    final, own_force = call(
        finish_kernel,
        [VMEM] * 2,
        [adjoint_prev.shape, (1, owned)],
        [
            pltpu.VMEM(adjoint_prev.shape, F32), pltpu.VMEM((1, owned), F32),
            pltpu.SemaphoreType.DMA((2,)),
        ],
        out_specs=[HBM, HBM],
    )(keep, parts)
    return (final, own_force.reshape(owned, 1))


def solution(mesh):
    in_specs = (
        P(None, "circ", "rad", "mode"),
        P("circ", "rad", "mode"),
        P(),
        P("circ", "rad", "mode", None, None, None),
        P("circ", "rad", "mode", None, None),
        P("circ", "rad", "mode", None),
        P("circ", "rad", "mode", None),
        P("circ", "rad", "mode", None, None, None),
    )
    out_specs = (P(None, "circ", "rad", "mode"), P("mode", "circ"))
    return jax.shard_map(
        on_device, mesh=mesh, in_specs=in_specs, out_specs=out_specs, check_vma=False
    )
```

```python
import functools

import jax
import jax.numpy as jnp
from jax import lax
from jax.experimental import pallas as pl
from jax.experimental.pallas import tpu as pltpu
from jax.sharding import PartitionSpec as P

coupling = 0.5
relaxation = 0.6

face_own, face_other = 0.5 * (1.0 + coupling), 0.5
edge_own, edge_other = 0.25 * (1.0 + 0.5 * coupling), 0.25
corner_own = (1.0 + coupling / 3.0) / 6.0
edge_cross = 0.25 * coupling / 2.0
corner_cross = coupling / 18.0
centre_weight = 2 * face_own + 4 * face_other + 8 * edge_own + 4 * edge_other + 8 * corner_own

F32 = jnp.float32
BF16 = jnp.bfloat16
NT = (((1,), (1,)), ((), ()))


def split(x):
    high = x.astype(BF16).astype(F32)
    return high, x - high


def pack_kernel(
    moduli_in, count_in, prev_in, cls_in, sens_in, nodes_in, send, e_out,
    moduli, count, prev, cls, sens, nodes, sems,
):
    copies = [
        pltpu.make_async_copy(source, target, sems.at[i])
        for i, (source, target) in enumerate(
            (
                (sens_in, sens), (nodes_in, nodes), (prev_in, prev), (cls_in, cls),
                (count_in, count), (moduli_in, moduli),
            )
        )
    ]
    for copy in copies:
        copy.start()
    for copy in copies:
        copy.wait()
    _, blocks, slots = sens.shape
    ncirc, nrad, naxial = cls.shape
    lines = ncirc * nrad
    k = lax.axis_index("mode")
    lane = lax.broadcasted_iota(jnp.int32, (nrad, 128), 1)
    columns = []
    for c in range(ncirc):
        level = cls[c]
        e = jnp.zeros(level.shape, F32)
        for i in range(moduli.shape[0]):
            e = jnp.where(level == i, moduli[i], e)
        e_out[c] = e
        ends = jnp.zeros((nrad, 128), F32)
        for f in range(4):
            field = prev[f, c] if f < 3 else e
            first = pltpu.roll(field[:, :128], 4 * f + 2, 1)
            last = pltpu.roll(field[:, naxial - 128 :], 4 * f + 2, 1)
            ends = jnp.where((lane == 4 * f + 2) | (lane == 4 * f + 3), first, ends)
            ends = jnp.where((lane == 4 * f) | (lane == 4 * f + 1), last, ends)
        columns.append(ends)
    columns.append(jnp.zeros((128 - lines, 128), F32))
    items = jnp.concatenate(columns, axis=0).T
    halo = items[:8] + pltpu.roll(items[8:16], 32, 1)
    tall = lax.broadcasted_iota(jnp.int32, (8, 128), 0)
    to_high = jnp.where(tall % 4 < 2, halo, 0.0)
    to_low = halo - to_high

    node = nodes[...]
    axial, line = node % naxial, node // naxial
    key = jnp.where(axial == 0, line, jnp.where(axial == naxial - 1, line + lines, -1))
    key = key.astype(F32).astype(BF16)
    place = lax.broadcasted_iota(jnp.int32, (2 * lines, slots), 0).astype(F32).astype(BF16)
    slot = lax.broadcasted_iota(jnp.int32, (1, slots), 1)
    row = lax.broadcasted_iota(jnp.int32, (16, slots), 0) // 2
    zero, one = BF16(0.0), BF16(1.0)
    planes = []
    for d in range(blocks):
        live = slot < count[d]
        tile = jnp.zeros((16, slots), F32)
        for i in range(3):
            value = jnp.where(live, sens[i, d : d + 1], 0.0)
            for q in range(slots // 128):
                send[d, 4 * (i + 1) + q : 4 * (i + 1) + q + 1, :] = value[:, 128 * q : 128 * (q + 1)]
            high, low = split(value)
            tile = jnp.where(row == i, high, jnp.where(row == 4 + i, low, tile))
        for q in range(slots // 128):
            send[d, q : q + 1, :] = node[d : d + 1, 128 * q : 128 * (q + 1)].astype(F32)
        hits = jnp.where(place == jnp.broadcast_to(key[d : d + 1], place.shape), one, zero)
        plane = lax.dot_general(tile.astype(BF16), hits, NT, preferred_element_type=F32)
        plane = jnp.concatenate([plane[:8] + plane[8:], jnp.zeros((8, 128 - 2 * lines), F32)], axis=1)
        planes.append(plane)
    group = lax.broadcasted_iota(jnp.int32, (8, 128), 1) // lines == 2
    even, odd = group & (tall % 2 == 0), group & (tall % 2 == 1)
    for d in range(blocks):
        out = jnp.where(k == d + 1, to_low, 0.0) + jnp.where(k == d - 1, to_high, 0.0)
        if d + 1 < blocks:
            out = jnp.where(odd, pltpu.roll(planes[d + 1], 2 * lines, 1), out)
        if d > 0:
            out = jnp.where(even, pltpu.roll(planes[d - 1], lines, 1), out)
        send[d, 16:24, :] = out


def scatter_kernel(got, prev, e, rhs, ends, first, second):
    blocks = got.shape[0]
    _, ncirc, nrad, naxial = prev.shape
    lines = ncirc * nrad
    row = lax.broadcasted_iota(jnp.int32, (lines, 128), 0).astype(F32).astype(BF16)
    cell = lax.broadcasted_iota(jnp.int32, (128, naxial), 1).astype(F32).astype(BF16)
    nodes = jnp.concatenate([got[d, :4, :] for d in range(blocks)], axis=0).astype(jnp.int32)
    line = (nodes // naxial).astype(F32).astype(BF16)
    tall = jnp.concatenate([nodes % naxial, jnp.zeros((128 - 4 * blocks, 128), jnp.int32)], axis=0)
    tall = tall.astype(F32).T.astype(BF16)
    zero, one = BF16(0.0), BF16(1.0)
    dense = jnp.zeros((6 * lines, naxial), F32)
    for d in range(blocks):
        left, right = [], []
        for q in range(4):
            g = 4 * d + q
            at = jnp.broadcast_to(tall[:, g : g + 1], cell.shape)
            right.append(jnp.where(cell == at, one, zero))
            hit = row == jnp.broadcast_to(line[g : g + 1], row.shape)
            column = []
            for i in range(3):
                for part in split(got[d, 4 * (i + 1) + q : 4 * (i + 1) + q + 1, :]):
                    column.append(jnp.where(hit, jnp.broadcast_to(part.astype(BF16), row.shape), zero))
            left.append(jnp.concatenate(column, axis=0))
        left, right = jnp.concatenate(left, axis=1), jnp.concatenate(right, axis=0)
        dense = dense + jnp.dot(left, right, preferred_element_type=F32)
    for i in range(3):
        total = dense[2 * lines * i : 2 * lines * i + lines] + dense[2 * lines * i + lines : 2 * lines * (i + 1)]
        for c in range(ncirc):
            rhs[i, c] = total[nrad * c : nrad * (c + 1)]
    total = got[0, 16:24, :]
    for d in range(1, blocks):
        total = total + got[d, 16:24, :]
    groups = [total, pltpu.roll(total, 128 - lines, 1), pltpu.roll(total, 128 - 2 * lines, 1)]
    columns = jnp.concatenate(groups + [jnp.zeros((104, 128), F32)], axis=0).T
    for c in range(ncirc):
        ends[c] = columns[nrad * c : nrad * (c + 1)]
    for out, base, edge in ((first, ncirc - 2, ncirc - 1), (second, 0, 0)):
        for t in range(2):
            cut = slice(128 * t, 128 * (t + 1))
            for f in range(4):
                for j in range(2):
                    source = prev[f, base + j] if f < 3 else e[base + j]
                    out[4 * f + 2 * t + j] = source[:, cut]
            for i in range(3):
                out[16 + 2 * i + t] = rhs[i, edge][:, cut]
        for j in range(2):
            out[22 + j] = ends[base + j]


def turn_kernel(prev, e, rhs, ends, got_first, got_second, turned, first, second, left, keep):
    _, ncirc, nrad, _ = prev.shape
    def put(index, c, plane):
        turned[index, pl.ds(c, nrad, stride=8), :] = plane

    for c in range(ncirc):
        for t in range(2):
            cut = slice(128 * t, 128 * (t + 1))
            for f in range(4):
                source = prev[f, c] if f < 3 else e[c]
                put(2 * f + t, c, source[:, cut])
            for i in range(3):
                put(8 + 2 * i + t, c, rhs[i, c][:, cut])
        put(14, c, ends[c])

    def sides(tile):
        return got_first[tile], got_second[tile]

    for index in range(8):
        for j in range(2):
            low, high = sides(2 * index + j)
            put(index, 6 + j, low)
            put(index, 4 + j, high)
    for index in range(6):
        low, high = sides(16 + index)
        put(8 + index, 7, low)
        put(8 + index, 4, high)
        put(8 + index, 6, low)
        put(8 + index, 5, high)
    for j in range(2):
        low, high = sides(22 + j)
        put(14, 6 + j, low)
        put(14, 4 + j, high)

    odd = lax.axis_index("rad") % 2
    for out, at_high in ((first, 1 - odd), (second, odd)):
        for index in range(15):
            for j in range(2):
                plane = at_high * (nrad - 2) + j
                at = 2 * index + j
                if 8 <= index < 14:
                    if j:
                        continue
                    plane = at_high * (nrad - 1)
                    at = 16 + index - 8
                elif index == 14:
                    at = 22 + j
                out[at] = turned[index, pl.ds(pl.multiple_of(8 * plane, 8), 8), :]

    @pl.when(works_ahead())
    def _():
        inner_work(turned, left, keep)


def sums(x):
    up = pltpu.roll(x, x.shape[1] - 1, 1)
    down = pltpu.roll(x, 1, 1)
    return up + down, up - down


def across(x):
    up = pltpu.roll(x, 7, 0)
    down = pltpu.roll(x, 1, 0)
    return up + down, up - down


def spread(x):
    sn, dn = sums(x)
    sm, dm = across(x)
    smsn, dmsn = across(sn)
    smdn, dmdn = across(dn)
    return sn, dn, sm, dm, smsn, dmsn, smdn, dmdn


def leading_terms(x, s):
    sn, _, sm, _, both = s[0], s[1], s[2], s[3], s[4]
    near = sm + sn
    return face_other * near + edge_other * both, face_own * x + edge_own * near + corner_own * both


def plane_terms(x, own, other, both):
    centre = face_own * own + face_other * other + edge_own * both
    side = face_other * x + edge_own * own + edge_other * other + corner_own * both
    return centre, side


def cross_terms(s):
    _, dn, _, dm, _, dmsn, smdn, dmdn = s
    return edge_cross * dm + corner_cross * dmsn, edge_cross * dn + corner_cross * smdn, dmdn


def vector_terms(v):
    s0, s1, s2 = spread(v[0]), spread(v[1]), spread(v[2])
    p0, q0 = plane_terms(v[0], s0[2], s0[0], s0[4])
    p1, q1 = leading_terms(v[1], s1)
    p2, q2 = plane_terms(v[2], s2[0], s2[2], s2[4])
    rm0, _, w0 = cross_terms(s0)
    rm1, rn1, _ = cross_terms(s1)
    _, rn2, w2 = cross_terms(s2)
    p0 = p0 + edge_cross * w2
    q0 = q0 + corner_cross * w2
    p2 = p2 + edge_cross * w0
    q2 = q2 + corner_cross * w0
    d0, d1, d2 = rm1, rm0 + rn2, rn1
    return (p0, p1, p2), (q0 + d0, q1 + d1, q2 + d2), (q0 - d0, q1 - d1, q2 - d2)


def scalar_terms(e):
    s = spread(e)
    p0, q0 = plane_terms(e, s[2], s[0], s[4])
    p1, q1 = leading_terms(e, s)
    p2, q2 = plane_terms(e, s[0], s[2], s[4])
    rm, rn, w = cross_terms(s)
    return (p0, p1, p2), (q0, q1, q2), rm, rn, w


def moved(v, e):
    plain, scaled = vector_terms(v), vector_terms([e * x for x in v])
    return [list(plain[j]) + list(scaled[j]) for j in range(3)]


def weighed(e):
    p, q, rm, rn, w = scalar_terms(e)
    zero = jnp.zeros_like(w)
    side = corner_cross * w
    return [
        list(p) + [zero, zero, edge_cross * w],
        list(q) + [rm, rn, side],
        list(q) + [-rm, -rn, side],
    ]


def plus(*parts):
    return [functools.reduce(lambda a, b: a + b, column) for column in zip(*parts)]


def stiffness(e, part):
    diag = [centre_weight * e + x for x in part[:3]]
    return diag, [relaxation / x for x in diag], part[3], part[4], part[5]


def remainder(v, e, rhs, stiff, part):
    (d0, d1, d2), _, c01, c12, c02 = stiff
    own = (
        d0 * v[0] + c01 * v[1] + c02 * v[2],
        c01 * v[0] + d1 * v[1] + c12 * v[2],
        c02 * v[0] + c12 * v[1] + d2 * v[2],
    )
    return [rhs[i] - own[i] + e * part[i] + part[3 + i] for i in range(3)]


def relaxed(v, stiff, rest):
    return [v[i] + stiff[1][i] * rest[i] for i in range(3)]


def outside_mask():
    lane = lax.broadcasted_iota(jnp.int32, (8, 384), 1)
    mode = lax.axis_index("mode")
    return ((lane == 383) & (mode == 0)) | ((lane == 256) & (mode == lax.axis_size("mode") - 1))


def own_tile(turned, index, plane):
    return turned[index, 8 * plane : 8 * (plane + 1), :]


def field_of(tile, f, ends):
    shift = 4 * f + 2 if f < 4 else 17 + 2 * (f - 4)
    return jnp.concatenate([tile(2 * f), tile(2 * f + 1), pltpu.roll(ends, 128 - shift, 1)], axis=1)


def cells_of(turned, plane, first, last):
    tile = lambda index: own_tile(turned, index, plane)
    ends = tile(14)
    return [field_of(tile, f, ends) for f in range(first, last)]


def put_final(keep, plane, final):
    for i in range(3):
        for t in range(2):
            keep[2 * i + t, 8 * plane : 8 * (plane + 1), :] = final[i][:, 128 * t : 128 * (t + 1)]


BEYOND, EDGE, CARRY, REST, HELD, SCALE, COUNT = 0, 12, 24, 30, 33, 36, 39
OWN, DOWN, UP = 0, 1, 2


def works_ahead():
    return (lax.axis_index("circ") % 4 != 0) | (lax.axis_index("rad") % 2 == 1)


def inner_work(turned, left, keep):
    nrad = turned.shape[1] // 8
    outside = outside_mask()
    last = nrad - 1
    adds, middle, stiff = {}, {}, {}

    def leave(side, at, arrays):
        for j, x in enumerate(arrays):
            left[side, at + j] = x

    for plane in range(nrad):
        v, e = cells_of(turned, plane, 0, 3), cells_of(turned, plane, 3, 4)[0]
        adds[plane] = [a + b for a, b in zip(moved(v, e), weighed(e))]
        if plane == 0:
            leave(0, BEYOND, adds[0][DOWN])
        if plane == 1:
            leave(0, EDGE, plus(adds[0][OWN], adds[1][DOWN]))
        if plane == last:
            leave(1, EDGE, plus(adds[last][OWN], adds[last - 1][UP]))
            leave(1, BEYOND, adds[last][UP])
        at = plane - 1
        if at < 1:
            continue
        v, e = cells_of(turned, at, 0, 3), cells_of(turned, at, 3, 4)[0]
        part = plus(adds[at - 1][UP], adds[at][OWN], adds[at + 1][DOWN])
        stiff[at] = stiffness(e, part[6:])
        rest = remainder(v, e, cells_of(turned, at, 4, 7), stiff[at], part)
        middle[at] = [jnp.where(outside, 0.0, x) for x in relaxed(v, stiff[at], rest)]

    adds = {}
    for plane in range(1, last):
        e = cells_of(turned, plane, 3, 4)[0]
        adds[plane] = moved(middle[plane], e)
        if plane == 1:
            leave(0, CARRY, adds[1][DOWN])
        if plane == last - 1:
            leave(1, CARRY, adds[last - 1][UP])
        for at in (plane - 1, plane):
            if at < 1 or (at == plane and plane < last - 1):
                continue
            beside = []
            if at - 1 in adds:
                beside.append(adds[at - 1][UP])
            if at + 1 in adds:
                beside.append(adds[at + 1][DOWN])
            part = plus(adds[at][OWN], *beside)
            v, e = middle[at], cells_of(turned, at, 3, 4)[0]
            rest = remainder(v, e, cells_of(turned, at, 4, 7), stiff[at], part)
            if len(beside) == 2:
                put_final(keep, at, relaxed(v, stiff[at], rest))
            else:
                side = 0 if at == 1 else 1
                leave(side, REST, rest)
                leave(side, HELD, v)
                leave(side, SCALE, stiff[at][1])


def inner_kernel(turned, left_in, keep_in, ids, left, keep, pick, nodes, sem):
    copy = pltpu.make_async_copy(ids, nodes, sem)
    copy.start()
    ahead = works_ahead()

    @pl.when(ahead)
    def _():
        left[...] = left_in[...]
        keep[...] = keep_in[...]

    @pl.when(jnp.logical_not(ahead))
    def _():
        inner_work(turned, left, keep)

    copy.wait()
    cell = lax.broadcasted_iota(jnp.int32, pick.shape, 0)
    pick[...] = jnp.where(cell == nodes[...] % 256, 1.0, 0.0).astype(BF16)


def sweep_kernel(
    devices, ncirc, turned, got_second, got_first, left, kept, pick, ids, shapes, keep, force, sums_of
):
    nrad = turned.shape[1] // 8
    rad = lax.axis_index("rad")
    odd = rad % 2 == 1
    outside = outside_mask()

    def halo(side, j, first, last):
        def tile(index):
            if index == 14:
                at = 22 + j
            elif index >= 8:
                at = 16 + index - 8
            else:
                at = 2 * index + j
            a, b = got_first[at], got_second[at]
            return jnp.where(odd, b, a) if side else jnp.where(odd, a, b)

        ends = tile(14)
        return [field_of(tile, f, ends) for f in range(first, last)]

    def handed(side, at, count):
        return [left[side, at + j] for j in range(count)]

    for side in range(2):
        inward = DOWN if side else UP
        near, far = (0, 1) if side else (1, 0)
        edge, next_in = (nrad - 1, nrad - 2) if side else (0, 1)
        v, e = halo(side, far, 0, 3), halo(side, far, 3, 4)[0]
        beyond = moved(v, e)[inward] + weighed(e)[inward]
        v, e = halo(side, near, 0, 3), halo(side, near, 3, 4)[0]
        here = [a + b for a, b in zip(moved(v, e), weighed(e))]
        part = plus(handed(side, BEYOND, 12), here[OWN], beyond)
        stiff = stiffness(e, part[6:])
        rest = remainder(v, e, halo(side, near, 4, 7), stiff, part)
        drop = outside | (rad == (lax.axis_size("rad") - 1 if side else 0))
        beside = moved([jnp.where(drop, 0.0, x) for x in relaxed(v, stiff, rest)], e)

        v, e = cells_of(turned, edge, 0, 3), cells_of(turned, edge, 3, 4)[0]
        rhs = cells_of(turned, edge, 4, 7)
        part = plus(handed(side, EDGE, 12), here[inward])
        stiff = stiffness(e, part[6:])
        v = [jnp.where(outside, 0.0, x) for x in relaxed(v, stiff, remainder(v, e, rhs, stiff, part))]
        here = moved(v, e)
        part = plus(handed(side, CARRY, 6), here[OWN], beside[inward])
        put_final(keep, edge, relaxed(v, stiff, remainder(v, e, rhs, stiff, part)))

        e = cells_of(turned, next_in, 3, 4)[0]
        add, rest = here[inward], handed(side, REST, 3)
        v, scale = handed(side, HELD, 3), handed(side, SCALE, 3)
        put_final(
            keep, next_in, [v[i] + scale[i] * (rest[i] + e * add[i] + add[3 + i]) for i in range(3)]
        )

    inside = slice(16, 8 * (nrad - 2))
    for index in range(6):
        keep[index, inside, :] = kept[index, inside, :]
    force_of(devices, ncirc, keep, pick, ids, shapes, force, sums_of)

def plane_of(keep, i, c, nrad):
    both = [keep[2 * i + t, pl.ds(c, nrad, stride=8), :] for t in range(2)]
    return jnp.concatenate(both, axis=1)


def emit_kernel(keep, adjoint):
    _, ncirc, nrad, _ = adjoint.shape
    for i in range(3):
        for c in range(ncirc):
            adjoint[i, c] = plane_of(keep, i, c, nrad)


def finish_kernel(keep, parts, adjoint, own, result, total, sems):
    emit_kernel(keep, result)
    first = pltpu.make_async_copy(result, adjoint, sems.at[0])
    first.start()
    total[...] = jnp.sum(parts[...], axis=0)[:, : total.shape[1]]
    second = pltpu.make_async_copy(total, own, sems.at[1])
    second.start()
    first.wait()
    second.wait()


def force_of(devices, ncirc, keep, pick, ids, shapes, force, sums_of):
    nrad = keep.shape[1] // 8
    lines = ncirc * nrad
    flat = jnp.concatenate([plane_of(keep, i, c, nrad) for i in range(3) for c in range(ncirc)], axis=0)
    high, low = split(flat)
    table = jnp.concatenate([high, low], axis=0).astype(BF16)
    node = ids[...]
    rows = jnp.dot(table, pick[...], preferred_element_type=F32)
    rows = rows[: 3 * lines] + rows[3 * lines :]
    line = lax.broadcasted_iota(jnp.int32, (lines, node.shape[1]), 0)
    hit = line == node // 256
    picked = [
        jnp.sum(jnp.where(hit, rows[lines * i : lines * (i + 1)], 0.0), axis=0, keepdims=True)
        for i in range(3)
    ]
    weighted = sum(shapes[i] * picked[i] for i in range(3))
    sums_of[...] = jnp.broadcast_to(jnp.sum(weighted, axis=1, keepdims=True), sums_of.shape)
    owned = sums_of.shape[0] // devices
    lane = lax.broadcasted_iota(jnp.int32, (devices, 128), 1)
    out = jnp.zeros((devices, 128), F32)
    for j in range(owned):
        out = jnp.where(lane == j, sums_of[pl.ds(j, devices, stride=owned), :], out)
    for r in range(force.shape[0] // devices):
        force[devices * r : devices * (r + 1), 0, :] = out


def swaps(axis, start, wrap):
    count = lax.axis_size(axis)
    pairs = []
    for i in range(start, count, 2):
        j = (i + 1) % count
        if j > i or wrap:
            pairs += [(i, j), (j, i)]
    return pairs


VMEM = pl.BlockSpec(memory_space=pltpu.VMEM)
HBM = pl.BlockSpec(memory_space=pltpu.HBM)


def call(kernel, ins, outs, scratch=(), flops=1_000_000, limit=40 * 1024 * 1024, out_specs=None):
    outs = [o if isinstance(o, jax.ShapeDtypeStruct) else jax.ShapeDtypeStruct(o, F32) for o in outs]
    return pl.pallas_call(
        kernel,
        out_shape=outs,
        in_specs=ins,
        out_specs=out_specs or [VMEM] * len(outs),
        scratch_shapes=list(scratch),
        compiler_params=pltpu.CompilerParams(vmem_limit_bytes=limit),
        cost_estimate=pl.CostEstimate(flops=flops, bytes_accessed=1_000_000, transcendentals=0),
    )


def on_device(
    adjoint_prev, cell_class, class_moduli, flow_sens, flow_nodes, flow_count, surf_ids, mode_shapes
):
    _, ncirc, nrad, naxial = adjoint_prev.shape
    n_mode, n_rad = lax.axis_size("mode"), lax.axis_size("rad")
    slots = flow_nodes.shape[-1]
    lines = ncirc * nrad
    cells = (ncirc, nrad, naxial)
    message = (24, 8, 128)
    args = (
        class_moduli, flow_count[0, 0, 0], adjoint_prev, cell_class,
        jnp.swapaxes(flow_sens[0, 0, 0], 0, 1), flow_nodes[0, 0, 0],
    )
    send, e = call(
        pack_kernel,
        [HBM] * 6,
        [(n_mode, 24, 128), cells],
        [pltpu.SMEM(x.shape, x.dtype) for x in args[:2]]
        + [pltpu.VMEM(x.shape, x.dtype) for x in args[2:]]
        + [pltpu.SemaphoreType.DMA((6,))],
        limit=63 * 1024 * 1024 + 512 * 1024,
    )(*args)
    got = lax.all_to_all(send, "mode", split_axis=0, concat_axis=0, tiled=True)
    rhs, ends, first, second = call(
        scatter_kernel,
        [VMEM] * 3,
        [(3,) + cells, (ncirc, nrad, 128), message, message],
    )(got, adjoint_prev, e)
    n_circ = lax.axis_size("circ")
    first = lax.ppermute(first, "circ", [(i, (i + 1) % n_circ) for i in range(n_circ)])
    second = lax.ppermute(second, "circ", [((i + 1) % n_circ, i) for i in range(n_circ)])
    kept = (6, 8 * nrad, 128)
    left = (2, COUNT, 8, 384)
    turned, first, second, left, keep = call(
        turn_kernel, [VMEM] * 6, [(15, 8 * nrad, 128), message, message, left, kept]
    )(
        adjoint_prev, e, rhs, ends, first, second
    )
    second = lax.ppermute(second, "rad", swaps("rad", 1, False))
    first = lax.ppermute(first, "rad", swaps("rad", 0, False))
    modes = mode_shapes.shape[3]
    owned = modes // n_mode
    ids = surf_ids[0, 0]
    shapes = jnp.swapaxes(mode_shapes[0, 0, 0], 0, 1)
    left, keep, pick = call(
        inner_kernel,
        [VMEM] * 3 + [HBM],
        [left.shape, kept, jax.ShapeDtypeStruct((naxial, ids.shape[1]), BF16)],
        [pltpu.VMEM(ids.shape, ids.dtype), pltpu.SemaphoreType.DMA],
        flops=10_000_000,
    )(turned, left, keep, ids)
    keep, force = call(
        functools.partial(sweep_kernel, n_mode, ncirc),
        [VMEM] * 8,
        [kept, (n_rad * n_mode, 1, 128)],
        [pltpu.VMEM((modes, 128), F32)],
    )(turned, second, first, left, keep, pick, ids, shapes)
    parts = lax.all_to_all(force, ("rad", "mode"), split_axis=0, concat_axis=0, tiled=True)
    final, own_force = call(
        finish_kernel,
        [VMEM] * 2,
        [adjoint_prev.shape, (1, owned)],
        [
            pltpu.VMEM(adjoint_prev.shape, F32), pltpu.VMEM((1, owned), F32),
            pltpu.SemaphoreType.DMA((2,)),
        ],
        out_specs=[HBM, HBM],
    )(keep, parts)
    return (final, own_force.reshape(owned, 1))


def solution(mesh):
    in_specs = (
        P(None, "circ", "rad", "mode"),
        P("circ", "rad", "mode"),
        P(),
        P("circ", "rad", "mode", None, None, None),
        P("circ", "rad", "mode", None, None),
        P("circ", "rad", "mode", None),
        P("circ", "rad", "mode", None),
        P("circ", "rad", "mode", None, None, None),
    )
    out_specs = (P(None, "circ", "rad", "mode"), P("mode", "circ"))
    return jax.shard_map(
        on_device, mesh=mesh, in_specs=in_specs, out_specs=out_specs, check_vma=False
    )
```

```python
import functools

import jax
import jax.numpy as jnp
from jax import lax
from jax.experimental import pallas as pl
from jax.experimental.pallas import tpu as pltpu
from jax.sharding import PartitionSpec as P

coupling = 0.5
relaxation = 0.6

face_own, face_other = 0.5 * (1.0 + coupling), 0.5
edge_own, edge_other = 0.25 * (1.0 + 0.5 * coupling), 0.25
corner_own = (1.0 + coupling / 3.0) / 6.0
edge_cross = 0.25 * coupling / 2.0
corner_cross = coupling / 18.0
centre_weight = 2 * face_own + 4 * face_other + 8 * edge_own + 4 * edge_other + 8 * corner_own

F32 = jnp.float32
BF16 = jnp.bfloat16
NT = (((1,), (1,)), ((), ()))


def split(x):
    high = x.astype(BF16).astype(F32)
    return high, x - high


def pack_kernel(
    moduli_in, count_in, prev_in, cls_in, sens_in, nodes_in, ids_in, send, e_out,
    moduli, count, prev, cls, sens, nodes, ids, sems,
):
    copies = [
        pltpu.make_async_copy(source, target, sems.at[i])
        for i, (source, target) in enumerate(
            (
                (sens_in, sens), (nodes_in, nodes), (prev_in, prev), (cls_in, cls),
                (count_in, count), (moduli_in, moduli), (ids_in, ids),
            )
        )
    ]
    for copy in copies:
        copy.start()
    for copy in copies:
        copy.wait()
    _, blocks, slots = sens.shape
    e_out[cls.shape[0]] = jnp.zeros(e_out.shape[1:], F32)
    for q in range(ids.shape[1] // cls.shape[2]):
        e_out[cls.shape[0], q : q + 1, :] = ids[:, cls.shape[2] * q : cls.shape[2] * (q + 1)].astype(F32)
    ncirc, nrad, naxial = cls.shape
    lines = ncirc * nrad
    k = lax.axis_index("mode")
    lane = lax.broadcasted_iota(jnp.int32, (nrad, 128), 1)
    columns = []
    for c in range(ncirc):
        level = cls[c]
        e = jnp.zeros(level.shape, F32)
        for i in range(moduli.shape[0]):
            e = jnp.where(level == i, moduli[i], e)
        e_out[c] = e
        ends = jnp.zeros((nrad, 128), F32)
        for f in range(4):
            field = prev[f, c] if f < 3 else e
            first = pltpu.roll(field[:, :128], 4 * f + 2, 1)
            last = pltpu.roll(field[:, naxial - 128 :], 4 * f + 2, 1)
            ends = jnp.where((lane == 4 * f + 2) | (lane == 4 * f + 3), first, ends)
            ends = jnp.where((lane == 4 * f) | (lane == 4 * f + 1), last, ends)
        columns.append(ends)
    columns.append(jnp.zeros((128 - lines, 128), F32))
    items = jnp.concatenate(columns, axis=0).T
    halo = items[:8] + pltpu.roll(items[8:16], 32, 1)
    tall = lax.broadcasted_iota(jnp.int32, (8, 128), 0)
    to_high = jnp.where(tall % 4 < 2, halo, 0.0)
    to_low = halo - to_high

    node = nodes[...]
    axial, line = node % naxial, node // naxial
    key = jnp.where(axial == 0, line, jnp.where(axial == naxial - 1, line + lines, -1))
    key = key.astype(F32).astype(BF16)
    place = lax.broadcasted_iota(jnp.int32, (2 * lines, slots), 0).astype(F32).astype(BF16)
    slot = lax.broadcasted_iota(jnp.int32, (1, slots), 1)
    row = lax.broadcasted_iota(jnp.int32, (16, slots), 0) // 2
    zero, one = BF16(0.0), BF16(1.0)
    planes = []
    for d in range(blocks):
        live = slot < count[d]
        tile = jnp.zeros((16, slots), F32)
        for i in range(3):
            value = jnp.where(live, sens[i, d : d + 1], 0.0)
            for q in range(slots // 128):
                send[d, 4 * (i + 1) + q : 4 * (i + 1) + q + 1, :] = value[:, 128 * q : 128 * (q + 1)]
            high, low = split(value)
            tile = jnp.where(row == i, high, jnp.where(row == 4 + i, low, tile))
        for q in range(slots // 128):
            send[d, q : q + 1, :] = node[d : d + 1, 128 * q : 128 * (q + 1)].astype(F32)
        hits = jnp.where(place == jnp.broadcast_to(key[d : d + 1], place.shape), one, zero)
        plane = lax.dot_general(tile.astype(BF16), hits, NT, preferred_element_type=F32)
        plane = jnp.concatenate([plane[:8] + plane[8:], jnp.zeros((8, 128 - 2 * lines), F32)], axis=1)
        planes.append(plane)
    group = lax.broadcasted_iota(jnp.int32, (8, 128), 1) // lines == 2
    even, odd = group & (tall % 2 == 0), group & (tall % 2 == 1)
    for d in range(blocks):
        out = jnp.where(k == d + 1, to_low, 0.0) + jnp.where(k == d - 1, to_high, 0.0)
        if d + 1 < blocks:
            out = jnp.where(odd, pltpu.roll(planes[d + 1], 2 * lines, 1), out)
        if d > 0:
            out = jnp.where(even, pltpu.roll(planes[d - 1], lines, 1), out)
        send[d, 16:24, :] = out


def scatter_kernel(got, prev, e, rhs, ends, first, second):
    blocks = got.shape[0]
    _, ncirc, nrad, naxial = prev.shape
    lines = ncirc * nrad
    row = lax.broadcasted_iota(jnp.int32, (lines, 128), 0).astype(F32).astype(BF16)
    cell = lax.broadcasted_iota(jnp.int32, (128, naxial), 1).astype(F32).astype(BF16)
    nodes = jnp.concatenate([got[d, :4, :] for d in range(blocks)], axis=0).astype(jnp.int32)
    line = (nodes // naxial).astype(F32).astype(BF16)
    tall = jnp.concatenate([nodes % naxial, jnp.zeros((128 - 4 * blocks, 128), jnp.int32)], axis=0)
    tall = tall.astype(F32).T.astype(BF16)
    zero, one = BF16(0.0), BF16(1.0)
    dense = jnp.zeros((6 * lines, naxial), F32)
    for d in range(blocks):
        left, right = [], []
        for q in range(4):
            g = 4 * d + q
            at = jnp.broadcast_to(tall[:, g : g + 1], cell.shape)
            right.append(jnp.where(cell == at, one, zero))
            hit = row == jnp.broadcast_to(line[g : g + 1], row.shape)
            column = []
            for i in range(3):
                for part in split(got[d, 4 * (i + 1) + q : 4 * (i + 1) + q + 1, :]):
                    column.append(jnp.where(hit, jnp.broadcast_to(part.astype(BF16), row.shape), zero))
            left.append(jnp.concatenate(column, axis=0))
        left, right = jnp.concatenate(left, axis=1), jnp.concatenate(right, axis=0)
        dense = dense + jnp.dot(left, right, preferred_element_type=F32)
    for i in range(3):
        total = dense[2 * lines * i : 2 * lines * i + lines] + dense[2 * lines * i + lines : 2 * lines * (i + 1)]
        for c in range(ncirc):
            rhs[i, c] = total[nrad * c : nrad * (c + 1)]
    total = got[0, 16:24, :]
    for d in range(1, blocks):
        total = total + got[d, 16:24, :]
    groups = [total, pltpu.roll(total, 128 - lines, 1), pltpu.roll(total, 128 - 2 * lines, 1)]
    columns = jnp.concatenate(groups + [jnp.zeros((104, 128), F32)], axis=0).T
    for c in range(ncirc):
        ends[c] = columns[nrad * c : nrad * (c + 1)]
    for out, base, edge in ((first, ncirc - 2, ncirc - 1), (second, 0, 0)):
        for t in range(2):
            cut = slice(128 * t, 128 * (t + 1))
            for f in range(4):
                for j in range(2):
                    source = prev[f, base + j] if f < 3 else e[base + j]
                    out[4 * f + 2 * t + j] = source[:, cut]
            for i in range(3):
                out[16 + 2 * i + t] = rhs[i, edge][:, cut]
        for j in range(2):
            out[22 + j] = ends[base + j]


def turn_kernel(prev, e, rhs, ends, got_first, got_second, turned, first, second, left, keep):
    _, ncirc, nrad, _ = prev.shape
    def put(index, c, plane):
        turned[index, pl.ds(c, nrad, stride=8), :] = plane

    for c in range(ncirc):
        for t in range(2):
            cut = slice(128 * t, 128 * (t + 1))
            for f in range(4):
                source = prev[f, c] if f < 3 else e[c]
                put(2 * f + t, c, source[:, cut])
            for i in range(3):
                put(8 + 2 * i + t, c, rhs[i, c][:, cut])
        put(14, c, ends[c])

    def sides(tile):
        return got_first[tile], got_second[tile]

    for index in range(8):
        for j in range(2):
            low, high = sides(2 * index + j)
            put(index, 6 + j, low)
            put(index, 4 + j, high)
    for index in range(6):
        low, high = sides(16 + index)
        put(8 + index, 7, low)
        put(8 + index, 4, high)
        put(8 + index, 6, low)
        put(8 + index, 5, high)
    for j in range(2):
        low, high = sides(22 + j)
        put(14, 6 + j, low)
        put(14, 4 + j, high)

    odd = lax.axis_index("rad") % 2
    for out, at_high in ((first, 1 - odd), (second, odd)):
        for index in range(15):
            for j in range(2):
                plane = at_high * (nrad - 2) + j
                at = 2 * index + j
                if 8 <= index < 14:
                    if j:
                        continue
                    plane = at_high * (nrad - 1)
                    at = 16 + index - 8
                elif index == 14:
                    at = 22 + j
                out[at] = turned[index, pl.ds(pl.multiple_of(8 * plane, 8), 8), :]

    @pl.when(works_ahead())
    def _():
        inner_work(turned, left, keep)


def sums(x):
    up = pltpu.roll(x, x.shape[1] - 1, 1)
    down = pltpu.roll(x, 1, 1)
    return up + down, up - down


def across(x):
    up = pltpu.roll(x, 7, 0)
    down = pltpu.roll(x, 1, 0)
    return up + down, up - down


def spread(x):
    sn, dn = sums(x)
    sm, dm = across(x)
    smsn, dmsn = across(sn)
    smdn, dmdn = across(dn)
    return sn, dn, sm, dm, smsn, dmsn, smdn, dmdn


def leading_terms(x, s):
    sn, _, sm, _, both = s[0], s[1], s[2], s[3], s[4]
    near = sm + sn
    return face_other * near + edge_other * both, face_own * x + edge_own * near + corner_own * both


def plane_terms(x, own, other, both):
    centre = face_own * own + face_other * other + edge_own * both
    side = face_other * x + edge_own * own + edge_other * other + corner_own * both
    return centre, side


def cross_terms(s):
    _, dn, _, dm, _, dmsn, smdn, dmdn = s
    return edge_cross * dm + corner_cross * dmsn, edge_cross * dn + corner_cross * smdn, dmdn


def vector_terms(v):
    s0, s1, s2 = spread(v[0]), spread(v[1]), spread(v[2])
    p0, q0 = plane_terms(v[0], s0[2], s0[0], s0[4])
    p1, q1 = leading_terms(v[1], s1)
    p2, q2 = plane_terms(v[2], s2[0], s2[2], s2[4])
    rm0, _, w0 = cross_terms(s0)
    rm1, rn1, _ = cross_terms(s1)
    _, rn2, w2 = cross_terms(s2)
    p0 = p0 + edge_cross * w2
    q0 = q0 + corner_cross * w2
    p2 = p2 + edge_cross * w0
    q2 = q2 + corner_cross * w0
    d0, d1, d2 = rm1, rm0 + rn2, rn1
    return (p0, p1, p2), (q0 + d0, q1 + d1, q2 + d2), (q0 - d0, q1 - d1, q2 - d2)


def scalar_terms(e):
    s = spread(e)
    p0, q0 = plane_terms(e, s[2], s[0], s[4])
    p1, q1 = leading_terms(e, s)
    p2, q2 = plane_terms(e, s[0], s[2], s[4])
    rm, rn, w = cross_terms(s)
    return (p0, p1, p2), (q0, q1, q2), rm, rn, w


def moved(v, e):
    plain, scaled = vector_terms(v), vector_terms([e * x for x in v])
    return [list(plain[j]) + list(scaled[j]) for j in range(3)]


def weighed(e):
    p, q, rm, rn, w = scalar_terms(e)
    zero = jnp.zeros_like(w)
    side = corner_cross * w
    return [
        list(p) + [zero, zero, edge_cross * w],
        list(q) + [rm, rn, side],
        list(q) + [-rm, -rn, side],
    ]


def plus(*parts):
    return [functools.reduce(lambda a, b: a + b, column) for column in zip(*parts)]


def stiffness(e, part):
    diag = [centre_weight * e + x for x in part[:3]]
    return diag, [relaxation / x for x in diag], part[3], part[4], part[5]


def remainder(v, e, rhs, stiff, part):
    (d0, d1, d2), _, c01, c12, c02 = stiff
    own = (
        d0 * v[0] + c01 * v[1] + c02 * v[2],
        c01 * v[0] + d1 * v[1] + c12 * v[2],
        c02 * v[0] + c12 * v[1] + d2 * v[2],
    )
    return [rhs[i] - own[i] + e * part[i] + part[3 + i] for i in range(3)]


def relaxed(v, stiff, rest):
    return [v[i] + stiff[1][i] * rest[i] for i in range(3)]


def outside_mask():
    lane = lax.broadcasted_iota(jnp.int32, (8, 384), 1)
    mode = lax.axis_index("mode")
    return ((lane == 383) & (mode == 0)) | ((lane == 256) & (mode == lax.axis_size("mode") - 1))


def own_tile(turned, index, plane):
    return turned[index, 8 * plane : 8 * (plane + 1), :]


def field_of(tile, f, ends):
    shift = 4 * f + 2 if f < 4 else 17 + 2 * (f - 4)
    return jnp.concatenate([tile(2 * f), tile(2 * f + 1), pltpu.roll(ends, 128 - shift, 1)], axis=1)


def cells_of(turned, plane, first, last):
    tile = lambda index: own_tile(turned, index, plane)
    ends = tile(14)
    return [field_of(tile, f, ends) for f in range(first, last)]


def put_final(keep, plane, final):
    for i in range(3):
        for t in range(2):
            keep[2 * i + t, 8 * plane : 8 * (plane + 1), :] = final[i][:, 128 * t : 128 * (t + 1)]


BEYOND, EDGE, CARRY, REST, HELD, SCALE, COUNT = 0, 12, 24, 30, 33, 36, 39
OWN, DOWN, UP = 0, 1, 2


def works_ahead():
    return (lax.axis_index("circ") % 4 != 0) | (lax.axis_index("rad") % 2 == 1)


def inner_work(turned, left, keep):
    nrad = turned.shape[1] // 8
    outside = outside_mask()
    last = nrad - 1
    adds, middle, stiff = {}, {}, {}

    def leave(side, at, arrays):
        for j, x in enumerate(arrays):
            left[side, at + j] = x

    for plane in range(nrad):
        v, e = cells_of(turned, plane, 0, 3), cells_of(turned, plane, 3, 4)[0]
        adds[plane] = [a + b for a, b in zip(moved(v, e), weighed(e))]
        if plane == 0:
            leave(0, BEYOND, adds[0][DOWN])
        if plane == 1:
            leave(0, EDGE, plus(adds[0][OWN], adds[1][DOWN]))
        if plane == last:
            leave(1, EDGE, plus(adds[last][OWN], adds[last - 1][UP]))
            leave(1, BEYOND, adds[last][UP])
        at = plane - 1
        if at < 1:
            continue
        v, e = cells_of(turned, at, 0, 3), cells_of(turned, at, 3, 4)[0]
        part = plus(adds[at - 1][UP], adds[at][OWN], adds[at + 1][DOWN])
        stiff[at] = stiffness(e, part[6:])
        rest = remainder(v, e, cells_of(turned, at, 4, 7), stiff[at], part)
        middle[at] = [jnp.where(outside, 0.0, x) for x in relaxed(v, stiff[at], rest)]

    adds = {}
    for plane in range(1, last):
        e = cells_of(turned, plane, 3, 4)[0]
        adds[plane] = moved(middle[plane], e)
        if plane == 1:
            leave(0, CARRY, adds[1][DOWN])
        if plane == last - 1:
            leave(1, CARRY, adds[last - 1][UP])
        for at in (plane - 1, plane):
            if at < 1 or (at == plane and plane < last - 1):
                continue
            beside = []
            if at - 1 in adds:
                beside.append(adds[at - 1][UP])
            if at + 1 in adds:
                beside.append(adds[at + 1][DOWN])
            part = plus(adds[at][OWN], *beside)
            v, e = middle[at], cells_of(turned, at, 3, 4)[0]
            rest = remainder(v, e, cells_of(turned, at, 4, 7), stiff[at], part)
            if len(beside) == 2:
                put_final(keep, at, relaxed(v, stiff[at], rest))
            else:
                side = 0 if at == 1 else 1
                leave(side, REST, rest)
                leave(side, HELD, v)
                leave(side, SCALE, stiff[at][1])


def listed(e, count):
    last, width = e.shape[0] - 1, e.shape[2]
    return jnp.concatenate([e[last, q : q + 1, :] for q in range(count // width)], axis=1).astype(jnp.int32)


def inner_kernel(turned, left_in, keep_in, e, left, keep, pick):
    ahead = works_ahead()

    @pl.when(ahead)
    def _():
        left[...] = left_in[...]
        keep[...] = keep_in[...]

    @pl.when(jnp.logical_not(ahead))
    def _():
        inner_work(turned, left, keep)

    cell = lax.broadcasted_iota(jnp.int32, pick.shape, 0)
    pick[...] = jnp.where(cell == listed(e, pick.shape[1]) % 256, 1.0, 0.0).astype(BF16)


def sweep_kernel(
    devices, ncirc, turned, got_second, got_first, left, kept, pick, riding, shapes, keep, force, sums_of
):
    nrad = turned.shape[1] // 8
    rad = lax.axis_index("rad")
    odd = rad % 2 == 1
    outside = outside_mask()

    def halo(side, j, first, last):
        def tile(index):
            if index == 14:
                at = 22 + j
            elif index >= 8:
                at = 16 + index - 8
            else:
                at = 2 * index + j
            a, b = got_first[at], got_second[at]
            return jnp.where(odd, b, a) if side else jnp.where(odd, a, b)

        ends = tile(14)
        return [field_of(tile, f, ends) for f in range(first, last)]

    def handed(side, at, count):
        return [left[side, at + j] for j in range(count)]

    for side in range(2):
        inward = DOWN if side else UP
        near, far = (0, 1) if side else (1, 0)
        edge, next_in = (nrad - 1, nrad - 2) if side else (0, 1)
        v, e = halo(side, far, 0, 3), halo(side, far, 3, 4)[0]
        beyond = moved(v, e)[inward] + weighed(e)[inward]
        v, e = halo(side, near, 0, 3), halo(side, near, 3, 4)[0]
        here = [a + b for a, b in zip(moved(v, e), weighed(e))]
        part = plus(handed(side, BEYOND, 12), here[OWN], beyond)
        stiff = stiffness(e, part[6:])
        rest = remainder(v, e, halo(side, near, 4, 7), stiff, part)
        drop = outside | (rad == (lax.axis_size("rad") - 1 if side else 0))
        beside = moved([jnp.where(drop, 0.0, x) for x in relaxed(v, stiff, rest)], e)

        v, e = cells_of(turned, edge, 0, 3), cells_of(turned, edge, 3, 4)[0]
        rhs = cells_of(turned, edge, 4, 7)
        part = plus(handed(side, EDGE, 12), here[inward])
        stiff = stiffness(e, part[6:])
        v = [jnp.where(outside, 0.0, x) for x in relaxed(v, stiff, remainder(v, e, rhs, stiff, part))]
        here = moved(v, e)
        part = plus(handed(side, CARRY, 6), here[OWN], beside[inward])
        put_final(keep, edge, relaxed(v, stiff, remainder(v, e, rhs, stiff, part)))

        e = cells_of(turned, next_in, 3, 4)[0]
        add, rest = here[inward], handed(side, REST, 3)
        v, scale = handed(side, HELD, 3), handed(side, SCALE, 3)
        put_final(
            keep, next_in, [v[i] + scale[i] * (rest[i] + e * add[i] + add[3 + i]) for i in range(3)]
        )

    inside = slice(16, 8 * (nrad - 2))
    for index in range(6):
        keep[index, inside, :] = kept[index, inside, :]
    force_of(devices, ncirc, keep, pick, riding, shapes, force, sums_of)

def plane_of(keep, i, c, nrad):
    both = [keep[2 * i + t, pl.ds(c, nrad, stride=8), :] for t in range(2)]
    return jnp.concatenate(both, axis=1)


def emit_kernel(keep, adjoint):
    _, ncirc, nrad, _ = adjoint.shape
    for i in range(3):
        for c in range(ncirc):
            adjoint[i, c] = plane_of(keep, i, c, nrad)


def finish_kernel(keep, parts, adjoint, own, result, total, sems):
    emit_kernel(keep, result)
    first = pltpu.make_async_copy(result, adjoint, sems.at[0])
    first.start()
    total[...] = jnp.sum(parts[...], axis=0)[:, : total.shape[1]]
    second = pltpu.make_async_copy(total, own, sems.at[1])
    second.start()
    first.wait()
    second.wait()


def force_of(devices, ncirc, keep, pick, riding, shapes, force, sums_of):
    nrad = keep.shape[1] // 8
    lines = ncirc * nrad
    flat = jnp.concatenate([plane_of(keep, i, c, nrad) for i in range(3) for c in range(ncirc)], axis=0)
    high, low = split(flat)
    table = jnp.concatenate([high, low], axis=0).astype(BF16)
    node = listed(riding, pick.shape[1])
    rows = jnp.dot(table, pick[...], preferred_element_type=F32)
    rows = rows[: 3 * lines] + rows[3 * lines :]
    line = lax.broadcasted_iota(jnp.int32, (lines, node.shape[1]), 0)
    hit = line == node // 256
    picked = [
        jnp.sum(jnp.where(hit, rows[lines * i : lines * (i + 1)], 0.0), axis=0, keepdims=True)
        for i in range(3)
    ]
    weighted = sum(shapes[i] * picked[i] for i in range(3))
    sums_of[...] = jnp.broadcast_to(jnp.sum(weighted, axis=1, keepdims=True), sums_of.shape)
    owned = sums_of.shape[0] // devices
    lane = lax.broadcasted_iota(jnp.int32, (devices, 128), 1)
    out = jnp.zeros((devices, 128), F32)
    for j in range(owned):
        out = jnp.where(lane == j, sums_of[pl.ds(j, devices, stride=owned), :], out)
    for r in range(force.shape[0] // devices):
        force[devices * r : devices * (r + 1), 0, :] = out


def swaps(axis, start, wrap):
    count = lax.axis_size(axis)
    pairs = []
    for i in range(start, count, 2):
        j = (i + 1) % count
        if j > i or wrap:
            pairs += [(i, j), (j, i)]
    return pairs


VMEM = pl.BlockSpec(memory_space=pltpu.VMEM)
HBM = pl.BlockSpec(memory_space=pltpu.HBM)


def call(kernel, ins, outs, scratch=(), flops=1_000_000, limit=40 * 1024 * 1024, out_specs=None):
    outs = [o if isinstance(o, jax.ShapeDtypeStruct) else jax.ShapeDtypeStruct(o, F32) for o in outs]
    return pl.pallas_call(
        kernel,
        out_shape=outs,
        in_specs=ins,
        out_specs=out_specs or [VMEM] * len(outs),
        scratch_shapes=list(scratch),
        compiler_params=pltpu.CompilerParams(vmem_limit_bytes=limit),
        cost_estimate=pl.CostEstimate(flops=flops, bytes_accessed=1_000_000, transcendentals=0),
    )


def on_device(
    adjoint_prev, cell_class, class_moduli, flow_sens, flow_nodes, flow_count, surf_ids, mode_shapes
):
    _, ncirc, nrad, naxial = adjoint_prev.shape
    n_mode, n_rad = lax.axis_size("mode"), lax.axis_size("rad")
    slots = flow_nodes.shape[-1]
    lines = ncirc * nrad
    cells = (ncirc, nrad, naxial)
    message = (24, 8, 128)
    args = (
        class_moduli, flow_count[0, 0, 0], adjoint_prev, cell_class,
        jnp.swapaxes(flow_sens[0, 0, 0], 0, 1), flow_nodes[0, 0, 0], surf_ids[0, 0],
    )
    send, e = call(
        pack_kernel,
        [HBM] * 7,
        [(n_mode, 24, 128), (ncirc + 1, nrad, naxial)],
        [pltpu.SMEM(x.shape, x.dtype) for x in args[:2]]
        + [pltpu.VMEM(x.shape, x.dtype) for x in args[2:]]
        + [pltpu.SemaphoreType.DMA((7,))],
        limit=63 * 1024 * 1024 + 512 * 1024,
    )(*args)
    got = lax.all_to_all(send, "mode", split_axis=0, concat_axis=0, tiled=True)
    rhs, ends, first, second = call(
        scatter_kernel,
        [VMEM] * 3,
        [(3,) + cells, (ncirc, nrad, 128), message, message],
    )(got, adjoint_prev, e)
    n_circ = lax.axis_size("circ")
    first = lax.ppermute(first, "circ", [(i, (i + 1) % n_circ) for i in range(n_circ)])
    second = lax.ppermute(second, "circ", [((i + 1) % n_circ, i) for i in range(n_circ)])
    kept = (6, 8 * nrad, 128)
    left = (2, COUNT, 8, 384)
    turned, first, second, left, keep = call(
        turn_kernel, [VMEM] * 6, [(15, 8 * nrad, 128), message, message, left, kept]
    )(
        adjoint_prev, e, rhs, ends, first, second
    )
    second = lax.ppermute(second, "rad", swaps("rad", 1, False))
    first = lax.ppermute(first, "rad", swaps("rad", 0, False))
    modes = mode_shapes.shape[3]
    owned = modes // n_mode
    shapes = jnp.swapaxes(mode_shapes[0, 0, 0], 0, 1)
    left, keep, pick = call(
        inner_kernel,
        [VMEM] * 4,
        [left.shape, kept, jax.ShapeDtypeStruct((naxial, surf_ids.shape[-1]), BF16)],
        flops=10_000_000,
    )(turned, left, keep, e)
    keep, force = call(
        functools.partial(sweep_kernel, n_mode, ncirc),
        [VMEM] * 8,
        [kept, (n_rad * n_mode, 1, 128)],
        [pltpu.VMEM((modes, 128), F32)],
    )(turned, second, first, left, keep, pick, e, shapes)
    parts = lax.all_to_all(force, ("rad", "mode"), split_axis=0, concat_axis=0, tiled=True)
    final, own_force = call(
        finish_kernel,
        [VMEM] * 2,
        [adjoint_prev.shape, (1, owned)],
        [
            pltpu.VMEM(adjoint_prev.shape, F32), pltpu.VMEM((1, owned), F32),
            pltpu.SemaphoreType.DMA((2,)),
        ],
        out_specs=[HBM, HBM],
    )(keep, parts)
    return (final, own_force.reshape(owned, 1))


def solution(mesh):
    in_specs = (
        P(None, "circ", "rad", "mode"),
        P("circ", "rad", "mode"),
        P(),
        P("circ", "rad", "mode", None, None, None),
        P("circ", "rad", "mode", None, None),
        P("circ", "rad", "mode", None),
        P("circ", "rad", "mode", None),
        P("circ", "rad", "mode", None, None, None),
    )
    out_specs = (P(None, "circ", "rad", "mode"), P("mode", "circ"))
    return jax.shard_map(
        on_device, mesh=mesh, in_specs=in_specs, out_specs=out_specs, check_vma=False
    )
```

```python
import functools

import jax
import jax.numpy as jnp
from jax import lax
from jax.experimental import pallas as pl
from jax.experimental.pallas import tpu as pltpu
from jax.sharding import PartitionSpec as P

coupling = 0.5
relaxation = 0.6

face_own, face_other = 0.5 * (1.0 + coupling), 0.5
edge_own, edge_other = 0.25 * (1.0 + 0.5 * coupling), 0.25
corner_own = (1.0 + coupling / 3.0) / 6.0
edge_cross = 0.25 * coupling / 2.0
corner_cross = coupling / 18.0
centre_weight = 2 * face_own + 4 * face_other + 8 * edge_own + 4 * edge_other + 8 * corner_own

F32 = jnp.float32
BF16 = jnp.bfloat16
NT = (((1,), (1,)), ((), ()))


def split(x):
    high = x.astype(BF16).astype(F32)
    return high, x - high


def pack_kernel(
    moduli_in, count_in, prev_in, cls_in, sens_in, nodes_in, send, e_out,
    moduli, count, prev, cls, sens, nodes, sems,
):
    copies = [
        pltpu.make_async_copy(source, target, sems.at[i])
        for i, (source, target) in enumerate(
            (
                (sens_in, sens), (nodes_in, nodes), (prev_in, prev), (cls_in, cls),
                (count_in, count), (moduli_in, moduli),
            )
        )
    ]
    for copy in copies:
        copy.start()
    for copy in copies:
        copy.wait()
    _, blocks, slots = sens.shape
    ncirc, nrad, naxial = cls.shape
    lines = ncirc * nrad
    k = lax.axis_index("mode")
    lane = lax.broadcasted_iota(jnp.int32, (nrad, 128), 1)
    columns = []
    for c in range(ncirc):
        level = cls[c]
        e = jnp.zeros(level.shape, F32)
        for i in range(moduli.shape[0]):
            e = jnp.where(level == i, moduli[i], e)
        e_out[c] = e
        ends = jnp.zeros((nrad, 128), F32)
        for f in range(4):
            field = prev[f, c] if f < 3 else e
            first = pltpu.roll(field[:, :128], 4 * f + 2, 1)
            last = pltpu.roll(field[:, naxial - 128 :], 4 * f + 2, 1)
            ends = jnp.where((lane == 4 * f + 2) | (lane == 4 * f + 3), first, ends)
            ends = jnp.where((lane == 4 * f) | (lane == 4 * f + 1), last, ends)
        columns.append(ends)
    columns.append(jnp.zeros((128 - lines, 128), F32))
    items = jnp.concatenate(columns, axis=0).T
    halo = items[:8] + pltpu.roll(items[8:16], 32, 1)
    tall = lax.broadcasted_iota(jnp.int32, (8, 128), 0)
    to_high = jnp.where(tall % 4 < 2, halo, 0.0)
    to_low = halo - to_high

    node = nodes[...]
    axial, line = node % naxial, node // naxial
    key = jnp.where(axial == 0, line, jnp.where(axial == naxial - 1, line + lines, -1))
    key = key.astype(F32).astype(BF16)
    place = lax.broadcasted_iota(jnp.int32, (2 * lines, slots), 0).astype(F32).astype(BF16)
    slot = lax.broadcasted_iota(jnp.int32, (1, slots), 1)
    row = lax.broadcasted_iota(jnp.int32, (16, slots), 0) // 2
    zero, one = BF16(0.0), BF16(1.0)
    planes = []
    for d in range(blocks):
        live = slot < count[d]
        tile = jnp.zeros((16, slots), F32)
        for i in range(3):
            value = jnp.where(live, sens[i, d : d + 1], 0.0)
            for q in range(slots // 128):
                send[d, 4 * (i + 1) + q : 4 * (i + 1) + q + 1, :] = value[:, 128 * q : 128 * (q + 1)]
            high, low = split(value)
            tile = jnp.where(row == i, high, jnp.where(row == 4 + i, low, tile))
        for q in range(slots // 128):
            send[d, q : q + 1, :] = node[d : d + 1, 128 * q : 128 * (q + 1)].astype(F32)
        hits = jnp.where(place == jnp.broadcast_to(key[d : d + 1], place.shape), one, zero)
        plane = lax.dot_general(tile.astype(BF16), hits, NT, preferred_element_type=F32)
        plane = jnp.concatenate([plane[:8] + plane[8:], jnp.zeros((8, 128 - 2 * lines), F32)], axis=1)
        planes.append(plane)
    group = lax.broadcasted_iota(jnp.int32, (8, 128), 1) // lines == 2
    even, odd = group & (tall % 2 == 0), group & (tall % 2 == 1)
    for d in range(blocks):
        out = jnp.where(k == d + 1, to_low, 0.0) + jnp.where(k == d - 1, to_high, 0.0)
        if d + 1 < blocks:
            out = jnp.where(odd, pltpu.roll(planes[d + 1], 2 * lines, 1), out)
        if d > 0:
            out = jnp.where(even, pltpu.roll(planes[d - 1], lines, 1), out)
        send[d, 16:24, :] = out


def scatter_kernel(got, prev, e, rhs, ends, first, second):
    blocks = got.shape[0]
    _, ncirc, nrad, naxial = prev.shape
    lines = ncirc * nrad
    row = lax.broadcasted_iota(jnp.int32, (lines, 128), 0).astype(F32).astype(BF16)
    cell = lax.broadcasted_iota(jnp.int32, (128, naxial), 1).astype(F32).astype(BF16)
    nodes = jnp.concatenate([got[d, :4, :] for d in range(blocks)], axis=0).astype(jnp.int32)
    line = (nodes // naxial).astype(F32).astype(BF16)
    tall = jnp.concatenate([nodes % naxial, jnp.zeros((128 - 4 * blocks, 128), jnp.int32)], axis=0)
    tall = tall.astype(F32).T.astype(BF16)
    zero, one = BF16(0.0), BF16(1.0)
    dense = jnp.zeros((6 * lines, naxial), F32)
    for d in range(blocks):
        left, right = [], []
        for q in range(4):
            g = 4 * d + q
            at = jnp.broadcast_to(tall[:, g : g + 1], cell.shape)
            right.append(jnp.where(cell == at, one, zero))
            hit = row == jnp.broadcast_to(line[g : g + 1], row.shape)
            column = []
            for i in range(3):
                for part in split(got[d, 4 * (i + 1) + q : 4 * (i + 1) + q + 1, :]):
                    column.append(jnp.where(hit, jnp.broadcast_to(part.astype(BF16), row.shape), zero))
            left.append(jnp.concatenate(column, axis=0))
        left, right = jnp.concatenate(left, axis=1), jnp.concatenate(right, axis=0)
        dense = dense + jnp.dot(left, right, preferred_element_type=F32)
    for i in range(3):
        total = dense[2 * lines * i : 2 * lines * i + lines] + dense[2 * lines * i + lines : 2 * lines * (i + 1)]
        for c in range(ncirc):
            rhs[i, c] = total[nrad * c : nrad * (c + 1)]
    total = got[0, 16:24, :]
    for d in range(1, blocks):
        total = total + got[d, 16:24, :]
    groups = [total, pltpu.roll(total, 128 - lines, 1), pltpu.roll(total, 128 - 2 * lines, 1)]
    columns = jnp.concatenate(groups + [jnp.zeros((104, 128), F32)], axis=0).T
    for c in range(ncirc):
        ends[c] = columns[nrad * c : nrad * (c + 1)]
    for out, base, edge in ((first, ncirc - 2, ncirc - 1), (second, 0, 0)):
        for t in range(2):
            cut = slice(128 * t, 128 * (t + 1))
            for f in range(4):
                for j in range(2):
                    source = prev[f, base + j] if f < 3 else e[base + j]
                    out[4 * f + 2 * t + j] = source[:, cut]
            for i in range(3):
                out[16 + 2 * i + t] = rhs[i, edge][:, cut]
        for j in range(2):
            out[22 + j] = ends[base + j]


def turn_kernel(prev, e, rhs, ends, got_first, got_second, turned, first, second, left, keep):
    _, ncirc, nrad, _ = prev.shape
    def put(index, c, plane):
        turned[index, pl.ds(c, nrad, stride=8), :] = plane

    for c in range(ncirc):
        for t in range(2):
            cut = slice(128 * t, 128 * (t + 1))
            for f in range(4):
                source = prev[f, c] if f < 3 else e[c]
                put(2 * f + t, c, source[:, cut])
            for i in range(3):
                put(8 + 2 * i + t, c, rhs[i, c][:, cut])
        put(14, c, ends[c])

    def sides(tile):
        return got_first[tile], got_second[tile]

    for index in range(8):
        for j in range(2):
            low, high = sides(2 * index + j)
            put(index, 6 + j, low)
            put(index, 4 + j, high)
    for index in range(6):
        low, high = sides(16 + index)
        put(8 + index, 7, low)
        put(8 + index, 4, high)
        put(8 + index, 6, low)
        put(8 + index, 5, high)
    for j in range(2):
        low, high = sides(22 + j)
        put(14, 6 + j, low)
        put(14, 4 + j, high)

    odd = lax.axis_index("rad") % 2
    for out, at_high in ((first, 1 - odd), (second, odd)):
        for index in range(15):
            for j in range(2):
                plane = at_high * (nrad - 2) + j
                at = 2 * index + j
                if 8 <= index < 14:
                    if j:
                        continue
                    plane = at_high * (nrad - 1)
                    at = 16 + index - 8
                elif index == 14:
                    at = 22 + j
                out[at] = turned[index, pl.ds(pl.multiple_of(8 * plane, 8), 8), :]

    @pl.when(works_ahead())
    def _():
        inner_work(turned, left, keep)


def sums(x):
    up = pltpu.roll(x, x.shape[1] - 1, 1)
    down = pltpu.roll(x, 1, 1)
    return up + down, up - down


def across(x):
    up = pltpu.roll(x, 7, 0)
    down = pltpu.roll(x, 1, 0)
    return up + down, up - down


def spread(x):
    sn, dn = sums(x)
    sm, dm = across(x)
    smsn, dmsn = across(sn)
    smdn, dmdn = across(dn)
    return sn, dn, sm, dm, smsn, dmsn, smdn, dmdn


def leading_terms(x, s):
    sn, _, sm, _, both = s[0], s[1], s[2], s[3], s[4]
    near = sm + sn
    return face_other * near + edge_other * both, face_own * x + edge_own * near + corner_own * both


def plane_terms(x, own, other, both):
    centre = face_own * own + face_other * other + edge_own * both
    side = face_other * x + edge_own * own + edge_other * other + corner_own * both
    return centre, side


def cross_terms(s):
    _, dn, _, dm, _, dmsn, smdn, dmdn = s
    return edge_cross * dm + corner_cross * dmsn, edge_cross * dn + corner_cross * smdn, dmdn


def vector_terms(v):
    s0, s1, s2 = spread(v[0]), spread(v[1]), spread(v[2])
    p0, q0 = plane_terms(v[0], s0[2], s0[0], s0[4])
    p1, q1 = leading_terms(v[1], s1)
    p2, q2 = plane_terms(v[2], s2[0], s2[2], s2[4])
    rm0, _, w0 = cross_terms(s0)
    rm1, rn1, _ = cross_terms(s1)
    _, rn2, w2 = cross_terms(s2)
    p0 = p0 + edge_cross * w2
    q0 = q0 + corner_cross * w2
    p2 = p2 + edge_cross * w0
    q2 = q2 + corner_cross * w0
    d0, d1, d2 = rm1, rm0 + rn2, rn1
    return (p0, p1, p2), (q0 + d0, q1 + d1, q2 + d2), (q0 - d0, q1 - d1, q2 - d2)


def scalar_terms(e):
    s = spread(e)
    p0, q0 = plane_terms(e, s[2], s[0], s[4])
    p1, q1 = leading_terms(e, s)
    p2, q2 = plane_terms(e, s[0], s[2], s[4])
    rm, rn, w = cross_terms(s)
    return (p0, p1, p2), (q0, q1, q2), rm, rn, w


def moved(v, e):
    plain, scaled = vector_terms(v), vector_terms([e * x for x in v])
    return [list(plain[j]) + list(scaled[j]) for j in range(3)]


def weighed(e):
    p, q, rm, rn, w = scalar_terms(e)
    zero = jnp.zeros_like(w)
    side = corner_cross * w
    return [
        list(p) + [zero, zero, edge_cross * w],
        list(q) + [rm, rn, side],
        list(q) + [-rm, -rn, side],
    ]


def plus(*parts):
    return [functools.reduce(lambda a, b: a + b, column) for column in zip(*parts)]


def stiffness(e, part):
    diag = [centre_weight * e + x for x in part[:3]]
    return diag, [relaxation / x for x in diag], part[3], part[4], part[5]


def remainder(v, e, rhs, stiff, part):
    (d0, d1, d2), _, c01, c12, c02 = stiff
    own = (
        d0 * v[0] + c01 * v[1] + c02 * v[2],
        c01 * v[0] + d1 * v[1] + c12 * v[2],
        c02 * v[0] + c12 * v[1] + d2 * v[2],
    )
    return [rhs[i] - own[i] + e * part[i] + part[3 + i] for i in range(3)]


def relaxed(v, stiff, rest):
    return [v[i] + stiff[1][i] * rest[i] for i in range(3)]


def outside_mask():
    lane = lax.broadcasted_iota(jnp.int32, (8, 384), 1)
    mode = lax.axis_index("mode")
    return ((lane == 383) & (mode == 0)) | ((lane == 256) & (mode == lax.axis_size("mode") - 1))


def own_tile(turned, index, plane):
    return turned[index, 8 * plane : 8 * (plane + 1), :]


def field_of(tile, f, ends):
    shift = 4 * f + 2 if f < 4 else 17 + 2 * (f - 4)
    return jnp.concatenate([tile(2 * f), tile(2 * f + 1), pltpu.roll(ends, 128 - shift, 1)], axis=1)


def cells_of(turned, plane, first, last):
    tile = lambda index: own_tile(turned, index, plane)
    ends = tile(14)
    return [field_of(tile, f, ends) for f in range(first, last)]


def put_final(keep, plane, final):
    for i in range(3):
        for t in range(2):
            keep[2 * i + t, 8 * plane : 8 * (plane + 1), :] = final[i][:, 128 * t : 128 * (t + 1)]


BEYOND, EDGE, CARRY, REST, HELD, SCALE, COUNT = 0, 12, 24, 30, 33, 36, 39
OWN, DOWN, UP = 0, 1, 2


def works_ahead():
    rad = lax.axis_index("rad")
    return (lax.axis_index("circ") % 4 != 0) | (rad % 2 == 1) | (rad == 0)


def inner_work(turned, left, keep):
    nrad = turned.shape[1] // 8
    outside = outside_mask()
    last = nrad - 1
    adds, middle, stiff = {}, {}, {}

    def leave(side, at, arrays):
        for j, x in enumerate(arrays):
            left[side, at + j] = x

    for plane in range(nrad):
        v, e = cells_of(turned, plane, 0, 3), cells_of(turned, plane, 3, 4)[0]
        adds[plane] = [a + b for a, b in zip(moved(v, e), weighed(e))]
        if plane == 0:
            leave(0, BEYOND, adds[0][DOWN])
        if plane == 1:
            leave(0, EDGE, plus(adds[0][OWN], adds[1][DOWN]))
        if plane == last:
            leave(1, EDGE, plus(adds[last][OWN], adds[last - 1][UP]))
            leave(1, BEYOND, adds[last][UP])
        at = plane - 1
        if at < 1:
            continue
        v, e = cells_of(turned, at, 0, 3), cells_of(turned, at, 3, 4)[0]
        part = plus(adds[at - 1][UP], adds[at][OWN], adds[at + 1][DOWN])
        stiff[at] = stiffness(e, part[6:])
        rest = remainder(v, e, cells_of(turned, at, 4, 7), stiff[at], part)
        middle[at] = [jnp.where(outside, 0.0, x) for x in relaxed(v, stiff[at], rest)]

    adds = {}
    for plane in range(1, last):
        e = cells_of(turned, plane, 3, 4)[0]
        adds[plane] = moved(middle[plane], e)
        if plane == 1:
            leave(0, CARRY, adds[1][DOWN])
        if plane == last - 1:
            leave(1, CARRY, adds[last - 1][UP])
        for at in (plane - 1, plane):
            if at < 1 or (at == plane and plane < last - 1):
                continue
            beside = []
            if at - 1 in adds:
                beside.append(adds[at - 1][UP])
            if at + 1 in adds:
                beside.append(adds[at + 1][DOWN])
            part = plus(adds[at][OWN], *beside)
            v, e = middle[at], cells_of(turned, at, 3, 4)[0]
            rest = remainder(v, e, cells_of(turned, at, 4, 7), stiff[at], part)
            if len(beside) == 2:
                put_final(keep, at, relaxed(v, stiff[at], rest))
            else:
                side = 0 if at == 1 else 1
                leave(side, REST, rest)
                leave(side, HELD, v)
                leave(side, SCALE, stiff[at][1])


def inner_kernel(turned, left_in, keep_in, ids, left, keep, pick, nodes, sem):
    copy = pltpu.make_async_copy(ids, nodes, sem)
    copy.start()
    ahead = works_ahead()

    @pl.when(ahead)
    def _():
        left[...] = left_in[...]
        keep[...] = keep_in[...]

    @pl.when(jnp.logical_not(ahead))
    def _():
        inner_work(turned, left, keep)

    copy.wait()
    cell = lax.broadcasted_iota(jnp.int32, pick.shape, 0)
    pick[...] = jnp.where(cell == nodes[...] % 256, 1.0, 0.0).astype(BF16)


def sweep_kernel(
    devices, ncirc, turned, got_second, got_first, left, kept, pick, ids, shapes, keep, force, sums_of
):
    nrad = turned.shape[1] // 8
    rad = lax.axis_index("rad")
    odd = rad % 2 == 1
    outside = outside_mask()

    def halo(side, j, first, last):
        def tile(index):
            if index == 14:
                at = 22 + j
            elif index >= 8:
                at = 16 + index - 8
            else:
                at = 2 * index + j
            a, b = got_first[at], got_second[at]
            return jnp.where(odd, b, a) if side else jnp.where(odd, a, b)

        ends = tile(14)
        return [field_of(tile, f, ends) for f in range(first, last)]

    def handed(side, at, count):
        return [left[side, at + j] for j in range(count)]

    for side in range(2):
        inward = DOWN if side else UP
        near, far = (0, 1) if side else (1, 0)
        edge, next_in = (nrad - 1, nrad - 2) if side else (0, 1)
        v, e = halo(side, far, 0, 3), halo(side, far, 3, 4)[0]
        beyond = moved(v, e)[inward] + weighed(e)[inward]
        v, e = halo(side, near, 0, 3), halo(side, near, 3, 4)[0]
        here = [a + b for a, b in zip(moved(v, e), weighed(e))]
        part = plus(handed(side, BEYOND, 12), here[OWN], beyond)
        stiff = stiffness(e, part[6:])
        rest = remainder(v, e, halo(side, near, 4, 7), stiff, part)
        drop = outside | (rad == (lax.axis_size("rad") - 1 if side else 0))
        beside = moved([jnp.where(drop, 0.0, x) for x in relaxed(v, stiff, rest)], e)

        v, e = cells_of(turned, edge, 0, 3), cells_of(turned, edge, 3, 4)[0]
        rhs = cells_of(turned, edge, 4, 7)
        part = plus(handed(side, EDGE, 12), here[inward])
        stiff = stiffness(e, part[6:])
        v = [jnp.where(outside, 0.0, x) for x in relaxed(v, stiff, remainder(v, e, rhs, stiff, part))]
        here = moved(v, e)
        part = plus(handed(side, CARRY, 6), here[OWN], beside[inward])
        put_final(keep, edge, relaxed(v, stiff, remainder(v, e, rhs, stiff, part)))

        e = cells_of(turned, next_in, 3, 4)[0]
        add, rest = here[inward], handed(side, REST, 3)
        v, scale = handed(side, HELD, 3), handed(side, SCALE, 3)
        put_final(
            keep, next_in, [v[i] + scale[i] * (rest[i] + e * add[i] + add[3 + i]) for i in range(3)]
        )

    inside = slice(16, 8 * (nrad - 2))
    for index in range(6):
        keep[index, inside, :] = kept[index, inside, :]
    force_of(devices, ncirc, keep, pick, ids, shapes, force, sums_of)

def plane_of(keep, i, c, nrad):
    both = [keep[2 * i + t, pl.ds(c, nrad, stride=8), :] for t in range(2)]
    return jnp.concatenate(both, axis=1)


def emit_kernel(keep, adjoint):
    _, ncirc, nrad, _ = adjoint.shape
    for i in range(3):
        for c in range(ncirc):
            adjoint[i, c] = plane_of(keep, i, c, nrad)


def finish_kernel(keep, parts, adjoint, own, result, total, sems):
    emit_kernel(keep, result)
    first = pltpu.make_async_copy(result, adjoint, sems.at[0])
    first.start()
    total[...] = jnp.sum(parts[...], axis=0)[:, : total.shape[1]]
    second = pltpu.make_async_copy(total, own, sems.at[1])
    second.start()
    first.wait()
    second.wait()


def force_of(devices, ncirc, keep, pick, ids, shapes, force, sums_of):
    nrad = keep.shape[1] // 8
    lines = ncirc * nrad
    flat = jnp.concatenate([plane_of(keep, i, c, nrad) for i in range(3) for c in range(ncirc)], axis=0)
    high, low = split(flat)
    table = jnp.concatenate([high, low], axis=0).astype(BF16)
    node = ids[...]
    rows = jnp.dot(table, pick[...], preferred_element_type=F32)
    rows = rows[: 3 * lines] + rows[3 * lines :]
    line = lax.broadcasted_iota(jnp.int32, (lines, node.shape[1]), 0)
    hit = line == node // 256
    picked = [
        jnp.sum(jnp.where(hit, rows[lines * i : lines * (i + 1)], 0.0), axis=0, keepdims=True)
        for i in range(3)
    ]
    weighted = sum(shapes[i] * picked[i] for i in range(3))
    sums_of[...] = jnp.broadcast_to(jnp.sum(weighted, axis=1, keepdims=True), sums_of.shape)
    owned = sums_of.shape[0] // devices
    lane = lax.broadcasted_iota(jnp.int32, (devices, 128), 1)
    out = jnp.zeros((devices, 128), F32)
    for j in range(owned):
        out = jnp.where(lane == j, sums_of[pl.ds(j, devices, stride=owned), :], out)
    for r in range(force.shape[0] // devices):
        force[devices * r : devices * (r + 1), 0, :] = out


def swaps(axis, start, wrap):
    count = lax.axis_size(axis)
    pairs = []
    for i in range(start, count, 2):
        j = (i + 1) % count
        if j > i or wrap:
            pairs += [(i, j), (j, i)]
    return pairs


VMEM = pl.BlockSpec(memory_space=pltpu.VMEM)
HBM = pl.BlockSpec(memory_space=pltpu.HBM)


def call(kernel, ins, outs, scratch=(), flops=1_000_000, limit=40 * 1024 * 1024, out_specs=None):
    outs = [o if isinstance(o, jax.ShapeDtypeStruct) else jax.ShapeDtypeStruct(o, F32) for o in outs]
    return pl.pallas_call(
        kernel,
        out_shape=outs,
        in_specs=ins,
        out_specs=out_specs or [VMEM] * len(outs),
        scratch_shapes=list(scratch),
        compiler_params=pltpu.CompilerParams(vmem_limit_bytes=limit),
        cost_estimate=pl.CostEstimate(flops=flops, bytes_accessed=1_000_000, transcendentals=0),
    )


def on_device(
    adjoint_prev, cell_class, class_moduli, flow_sens, flow_nodes, flow_count, surf_ids, mode_shapes
):
    _, ncirc, nrad, naxial = adjoint_prev.shape
    n_mode, n_rad = lax.axis_size("mode"), lax.axis_size("rad")
    slots = flow_nodes.shape[-1]
    lines = ncirc * nrad
    cells = (ncirc, nrad, naxial)
    message = (24, 8, 128)
    args = (
        class_moduli, flow_count[0, 0, 0], adjoint_prev, cell_class,
        jnp.swapaxes(flow_sens[0, 0, 0], 0, 1), flow_nodes[0, 0, 0],
    )
    send, e = call(
        pack_kernel,
        [HBM] * 6,
        [(n_mode, 24, 128), cells],
        [pltpu.SMEM(x.shape, x.dtype) for x in args[:2]]
        + [pltpu.VMEM(x.shape, x.dtype) for x in args[2:]]
        + [pltpu.SemaphoreType.DMA((6,))],
        limit=63 * 1024 * 1024 + 512 * 1024,
    )(*args)
    got = lax.all_to_all(send, "mode", split_axis=0, concat_axis=0, tiled=True)
    rhs, ends, first, second = call(
        scatter_kernel,
        [VMEM] * 3,
        [(3,) + cells, (ncirc, nrad, 128), message, message],
    )(got, adjoint_prev, e)
    n_circ = lax.axis_size("circ")
    first = lax.ppermute(first, "circ", [(i, (i + 1) % n_circ) for i in range(n_circ)])
    second = lax.ppermute(second, "circ", [((i + 1) % n_circ, i) for i in range(n_circ)])
    kept = (6, 8 * nrad, 128)
    left = (2, COUNT, 8, 384)
    turned, first, second, left, keep = call(
        turn_kernel, [VMEM] * 6, [(15, 8 * nrad, 128), message, message, left, kept]
    )(
        adjoint_prev, e, rhs, ends, first, second
    )
    second = lax.ppermute(second, "rad", swaps("rad", 1, False))
    first = lax.ppermute(first, "rad", swaps("rad", 0, False))
    modes = mode_shapes.shape[3]
    owned = modes // n_mode
    ids = surf_ids[0, 0]
    shapes = jnp.swapaxes(mode_shapes[0, 0, 0], 0, 1)
    left, keep, pick = call(
        inner_kernel,
        [VMEM] * 3 + [HBM],
        [left.shape, kept, jax.ShapeDtypeStruct((naxial, ids.shape[1]), BF16)],
        [pltpu.VMEM(ids.shape, ids.dtype), pltpu.SemaphoreType.DMA],
        flops=10_000_000,
    )(turned, left, keep, ids)
    keep, force = call(
        functools.partial(sweep_kernel, n_mode, ncirc),
        [VMEM] * 8,
        [kept, (n_rad * n_mode, 1, 128)],
        [pltpu.VMEM((modes, 128), F32)],
    )(turned, second, first, left, keep, pick, ids, shapes)
    parts = lax.all_to_all(force, ("rad", "mode"), split_axis=0, concat_axis=0, tiled=True)
    final, own_force = call(
        finish_kernel,
        [VMEM] * 2,
        [adjoint_prev.shape, (1, owned)],
        [
            pltpu.VMEM(adjoint_prev.shape, F32), pltpu.VMEM((1, owned), F32),
            pltpu.SemaphoreType.DMA((2,)),
        ],
        out_specs=[HBM, HBM],
    )(keep, parts)
    return (final, own_force.reshape(owned, 1))


def solution(mesh):
    in_specs = (
        P(None, "circ", "rad", "mode"),
        P("circ", "rad", "mode"),
        P(),
        P("circ", "rad", "mode", None, None, None),
        P("circ", "rad", "mode", None, None),
        P("circ", "rad", "mode", None),
        P("circ", "rad", "mode", None),
        P("circ", "rad", "mode", None, None, None),
    )
    out_specs = (P(None, "circ", "rad", "mode"), P("mode", "circ"))
    return jax.shard_map(
        on_device, mesh=mesh, in_specs=in_specs, out_specs=out_specs, check_vma=False
    )
```

```python
import functools

import jax
import jax.numpy as jnp
from jax import lax
from jax.experimental import pallas as pl
from jax.experimental.pallas import tpu as pltpu
from jax.sharding import PartitionSpec as P

coupling = 0.5
relaxation = 0.6

face_own, face_other = 0.5 * (1.0 + coupling), 0.5
edge_own, edge_other = 0.25 * (1.0 + 0.5 * coupling), 0.25
corner_own = (1.0 + coupling / 3.0) / 6.0
edge_cross = 0.25 * coupling / 2.0
corner_cross = coupling / 18.0
centre_weight = 2 * face_own + 4 * face_other + 8 * edge_own + 4 * edge_other + 8 * corner_own

F32 = jnp.float32
BF16 = jnp.bfloat16
NT = (((1,), (1,)), ((), ()))


def split(x):
    high = x.astype(BF16).astype(F32)
    return high, x - high


def pack_kernel(
    moduli_in, count_in, prev_in, cls_in, sens_in, nodes_in, send, e_out,
    moduli, count, prev, cls, sens, nodes, sems,
):
    copies = [
        pltpu.make_async_copy(source, target, sems.at[i])
        for i, (source, target) in enumerate(
            (
                (sens_in, sens), (nodes_in, nodes), (prev_in, prev), (cls_in, cls),
                (count_in, count), (moduli_in, moduli),
            )
        )
    ]
    for copy in copies:
        copy.start()
    for copy in copies:
        copy.wait()
    _, blocks, slots = sens.shape
    ncirc, nrad, naxial = cls.shape
    lines = ncirc * nrad
    k = lax.axis_index("mode")
    lane = lax.broadcasted_iota(jnp.int32, (nrad, 128), 1)
    columns = []
    for c in range(ncirc):
        level = cls[c]
        e = jnp.zeros(level.shape, F32)
        for i in range(moduli.shape[0]):
            e = jnp.where(level == i, moduli[i], e)
        e_out[c] = e
        ends = jnp.zeros((nrad, 128), F32)
        for f in range(4):
            field = prev[f, c] if f < 3 else e
            first = pltpu.roll(field[:, :128], 4 * f + 2, 1)
            last = pltpu.roll(field[:, naxial - 128 :], 4 * f + 2, 1)
            ends = jnp.where((lane == 4 * f + 2) | (lane == 4 * f + 3), first, ends)
            ends = jnp.where((lane == 4 * f) | (lane == 4 * f + 1), last, ends)
        columns.append(ends)
    columns.append(jnp.zeros((128 - lines, 128), F32))
    items = jnp.concatenate(columns, axis=0).T
    halo = items[:8] + pltpu.roll(items[8:16], 32, 1)
    tall = lax.broadcasted_iota(jnp.int32, (8, 128), 0)
    to_high = jnp.where(tall % 4 < 2, halo, 0.0)
    to_low = halo - to_high

    node = nodes[...]
    axial, line = node % naxial, node // naxial
    key = jnp.where(axial == 0, line, jnp.where(axial == naxial - 1, line + lines, -1))
    key = key.astype(F32).astype(BF16)
    place = lax.broadcasted_iota(jnp.int32, (2 * lines, slots), 0).astype(F32).astype(BF16)
    slot = lax.broadcasted_iota(jnp.int32, (1, slots), 1)
    row = lax.broadcasted_iota(jnp.int32, (16, slots), 0) // 2
    zero, one = BF16(0.0), BF16(1.0)
    planes = []
    for d in range(blocks):
        live = slot < count[d]
        tile = jnp.zeros((16, slots), F32)
        for i in range(3):
            value = jnp.where(live, sens[i, d : d + 1], 0.0)
            for q in range(slots // 128):
                send[d, 4 * (i + 1) + q : 4 * (i + 1) + q + 1, :] = value[:, 128 * q : 128 * (q + 1)]
            high, low = split(value)
            tile = jnp.where(row == i, high, jnp.where(row == 4 + i, low, tile))
        for q in range(slots // 128):
            send[d, q : q + 1, :] = node[d : d + 1, 128 * q : 128 * (q + 1)].astype(F32)
        hits = jnp.where(place == jnp.broadcast_to(key[d : d + 1], place.shape), one, zero)
        plane = lax.dot_general(tile.astype(BF16), hits, NT, preferred_element_type=F32)
        plane = jnp.concatenate([plane[:8] + plane[8:], jnp.zeros((8, 128 - 2 * lines), F32)], axis=1)
        planes.append(plane)
    group = lax.broadcasted_iota(jnp.int32, (8, 128), 1) // lines == 2
    even, odd = group & (tall % 2 == 0), group & (tall % 2 == 1)
    for d in range(blocks):
        out = jnp.where(k == d + 1, to_low, 0.0) + jnp.where(k == d - 1, to_high, 0.0)
        if d + 1 < blocks:
            out = jnp.where(odd, pltpu.roll(planes[d + 1], 2 * lines, 1), out)
        if d > 0:
            out = jnp.where(even, pltpu.roll(planes[d - 1], lines, 1), out)
        send[d, 16:24, :] = out


def scatter_kernel(got, prev, e, rhs, ends, first, second):
    blocks = got.shape[0]
    _, ncirc, nrad, naxial = prev.shape
    lines = ncirc * nrad
    row = lax.broadcasted_iota(jnp.int32, (lines, 128), 0).astype(F32).astype(BF16)
    cell = lax.broadcasted_iota(jnp.int32, (128, naxial), 1).astype(F32).astype(BF16)
    nodes = jnp.concatenate([got[d, :4, :] for d in range(blocks)], axis=0).astype(jnp.int32)
    line = (nodes // naxial).astype(F32).astype(BF16)
    tall = jnp.concatenate([nodes % naxial, jnp.zeros((128 - 4 * blocks, 128), jnp.int32)], axis=0)
    tall = tall.astype(F32).T.astype(BF16)
    zero, one = BF16(0.0), BF16(1.0)
    dense = jnp.zeros((6 * lines, naxial), F32)
    for d in range(blocks):
        left, right = [], []
        for q in range(4):
            g = 4 * d + q
            at = jnp.broadcast_to(tall[:, g : g + 1], cell.shape)
            right.append(jnp.where(cell == at, one, zero))
            hit = row == jnp.broadcast_to(line[g : g + 1], row.shape)
            column = []
            for i in range(3):
                for part in split(got[d, 4 * (i + 1) + q : 4 * (i + 1) + q + 1, :]):
                    column.append(jnp.where(hit, jnp.broadcast_to(part.astype(BF16), row.shape), zero))
            left.append(jnp.concatenate(column, axis=0))
        left, right = jnp.concatenate(left, axis=1), jnp.concatenate(right, axis=0)
        dense = dense + jnp.dot(left, right, preferred_element_type=F32)
    for i in range(3):
        total = dense[2 * lines * i : 2 * lines * i + lines] + dense[2 * lines * i + lines : 2 * lines * (i + 1)]
        for c in range(ncirc):
            rhs[i, c] = total[nrad * c : nrad * (c + 1)]
    total = got[0, 16:24, :]
    for d in range(1, blocks):
        total = total + got[d, 16:24, :]
    groups = [total, pltpu.roll(total, 128 - lines, 1), pltpu.roll(total, 128 - 2 * lines, 1)]
    columns = jnp.concatenate(groups + [jnp.zeros((104, 128), F32)], axis=0).T
    for c in range(ncirc):
        ends[c] = columns[nrad * c : nrad * (c + 1)]
    for out, base, edge in ((first, ncirc - 2, ncirc - 1), (second, 0, 0)):
        for t in range(2):
            cut = slice(128 * t, 128 * (t + 1))
            for f in range(4):
                for j in range(2):
                    if base == 0:
                        source = prev[f, base + j] if f < 3 else e[base + j]
                        out[4 * f + 2 * t + j] = source[:, cut]
            for i in range(3):
                out[out.shape[0] - 8 + 2 * i + t] = rhs[i, edge][:, cut]
        for j in range(2):
            out[out.shape[0] - 2 + j] = ends[base + j]


def early_kernel(prev, e, up):
    ncirc = prev.shape[1]
    for f in range(4):
        for t in range(2):
            for j in range(2):
                plane = prev[f, ncirc - 2 + j] if f < 3 else e[ncirc - 2 + j]
                up[4 * f + 2 * t + j] = plane[:, 128 * t : 128 * (t + 1)]


def join_kernel(early, late, whole):
    whole[: early.shape[0]] = early[...]
    whole[early.shape[0] :] = late[...]


def turn_kernel(prev, e, rhs, ends, got_first, got_second, turned, first, second, left, keep):
    _, ncirc, nrad, _ = prev.shape
    def put(index, c, plane):
        turned[index, pl.ds(c, nrad, stride=8), :] = plane

    for c in range(ncirc):
        for t in range(2):
            cut = slice(128 * t, 128 * (t + 1))
            for f in range(4):
                source = prev[f, c] if f < 3 else e[c]
                put(2 * f + t, c, source[:, cut])
            for i in range(3):
                put(8 + 2 * i + t, c, rhs[i, c][:, cut])
        put(14, c, ends[c])

    def sides(tile):
        return got_first[tile], got_second[tile]

    for index in range(8):
        for j in range(2):
            low, high = sides(2 * index + j)
            put(index, 6 + j, low)
            put(index, 4 + j, high)
    for index in range(6):
        low, high = sides(16 + index)
        put(8 + index, 7, low)
        put(8 + index, 4, high)
        put(8 + index, 6, low)
        put(8 + index, 5, high)
    for j in range(2):
        low, high = sides(22 + j)
        put(14, 6 + j, low)
        put(14, 4 + j, high)

    odd = lax.axis_index("rad") % 2
    for out, at_high in ((first, 1 - odd), (second, odd)):
        for index in range(15):
            for j in range(2):
                plane = at_high * (nrad - 2) + j
                at = 2 * index + j
                if 8 <= index < 14:
                    if j:
                        continue
                    plane = at_high * (nrad - 1)
                    at = 16 + index - 8
                elif index == 14:
                    at = 22 + j
                out[at] = turned[index, pl.ds(pl.multiple_of(8 * plane, 8), 8), :]

    @pl.when(works_ahead())
    def _():
        inner_work(turned, left, keep)


def sums(x):
    up = pltpu.roll(x, x.shape[1] - 1, 1)
    down = pltpu.roll(x, 1, 1)
    return up + down, up - down


def across(x):
    up = pltpu.roll(x, 7, 0)
    down = pltpu.roll(x, 1, 0)
    return up + down, up - down


def spread(x):
    sn, dn = sums(x)
    sm, dm = across(x)
    smsn, dmsn = across(sn)
    smdn, dmdn = across(dn)
    return sn, dn, sm, dm, smsn, dmsn, smdn, dmdn


def leading_terms(x, s):
    sn, _, sm, _, both = s[0], s[1], s[2], s[3], s[4]
    near = sm + sn
    return face_other * near + edge_other * both, face_own * x + edge_own * near + corner_own * both


def plane_terms(x, own, other, both):
    centre = face_own * own + face_other * other + edge_own * both
    side = face_other * x + edge_own * own + edge_other * other + corner_own * both
    return centre, side


def cross_terms(s):
    _, dn, _, dm, _, dmsn, smdn, dmdn = s
    return edge_cross * dm + corner_cross * dmsn, edge_cross * dn + corner_cross * smdn, dmdn


def vector_terms(v):
    s0, s1, s2 = spread(v[0]), spread(v[1]), spread(v[2])
    p0, q0 = plane_terms(v[0], s0[2], s0[0], s0[4])
    p1, q1 = leading_terms(v[1], s1)
    p2, q2 = plane_terms(v[2], s2[0], s2[2], s2[4])
    rm0, _, w0 = cross_terms(s0)
    rm1, rn1, _ = cross_terms(s1)
    _, rn2, w2 = cross_terms(s2)
    p0 = p0 + edge_cross * w2
    q0 = q0 + corner_cross * w2
    p2 = p2 + edge_cross * w0
    q2 = q2 + corner_cross * w0
    d0, d1, d2 = rm1, rm0 + rn2, rn1
    return (p0, p1, p2), (q0 + d0, q1 + d1, q2 + d2), (q0 - d0, q1 - d1, q2 - d2)


def scalar_terms(e):
    s = spread(e)
    p0, q0 = plane_terms(e, s[2], s[0], s[4])
    p1, q1 = leading_terms(e, s)
    p2, q2 = plane_terms(e, s[0], s[2], s[4])
    rm, rn, w = cross_terms(s)
    return (p0, p1, p2), (q0, q1, q2), rm, rn, w


def moved(v, e):
    plain, scaled = vector_terms(v), vector_terms([e * x for x in v])
    return [list(plain[j]) + list(scaled[j]) for j in range(3)]


def weighed(e):
    p, q, rm, rn, w = scalar_terms(e)
    zero = jnp.zeros_like(w)
    side = corner_cross * w
    return [
        list(p) + [zero, zero, edge_cross * w],
        list(q) + [rm, rn, side],
        list(q) + [-rm, -rn, side],
    ]


def plus(*parts):
    return [functools.reduce(lambda a, b: a + b, column) for column in zip(*parts)]


def stiffness(e, part):
    diag = [centre_weight * e + x for x in part[:3]]
    return diag, [relaxation / x for x in diag], part[3], part[4], part[5]


def remainder(v, e, rhs, stiff, part):
    (d0, d1, d2), _, c01, c12, c02 = stiff
    own = (
        d0 * v[0] + c01 * v[1] + c02 * v[2],
        c01 * v[0] + d1 * v[1] + c12 * v[2],
        c02 * v[0] + c12 * v[1] + d2 * v[2],
    )
    return [rhs[i] - own[i] + e * part[i] + part[3 + i] for i in range(3)]


def relaxed(v, stiff, rest):
    return [v[i] + stiff[1][i] * rest[i] for i in range(3)]


def outside_mask():
    lane = lax.broadcasted_iota(jnp.int32, (8, 384), 1)
    mode = lax.axis_index("mode")
    return ((lane == 383) & (mode == 0)) | ((lane == 256) & (mode == lax.axis_size("mode") - 1))


def own_tile(turned, index, plane):
    return turned[index, 8 * plane : 8 * (plane + 1), :]


def field_of(tile, f, ends):
    shift = 4 * f + 2 if f < 4 else 17 + 2 * (f - 4)
    return jnp.concatenate([tile(2 * f), tile(2 * f + 1), pltpu.roll(ends, 128 - shift, 1)], axis=1)


def cells_of(turned, plane, first, last):
    tile = lambda index: own_tile(turned, index, plane)
    ends = tile(14)
    return [field_of(tile, f, ends) for f in range(first, last)]


def put_final(keep, plane, final):
    for i in range(3):
        for t in range(2):
            keep[2 * i + t, 8 * plane : 8 * (plane + 1), :] = final[i][:, 128 * t : 128 * (t + 1)]


BEYOND, EDGE, CARRY, REST, HELD, SCALE, COUNT = 0, 12, 24, 30, 33, 36, 39
OWN, DOWN, UP = 0, 1, 2


def works_ahead():
    return (lax.axis_index("circ") % 4 != 0) | (lax.axis_index("rad") % 2 == 1)


def inner_work(turned, left, keep):
    nrad = turned.shape[1] // 8
    outside = outside_mask()
    last = nrad - 1
    adds, middle, stiff = {}, {}, {}

    def leave(side, at, arrays):
        for j, x in enumerate(arrays):
            left[side, at + j] = x

    for plane in range(nrad):
        v, e = cells_of(turned, plane, 0, 3), cells_of(turned, plane, 3, 4)[0]
        adds[plane] = [a + b for a, b in zip(moved(v, e), weighed(e))]
        if plane == 0:
            leave(0, BEYOND, adds[0][DOWN])
        if plane == 1:
            leave(0, EDGE, plus(adds[0][OWN], adds[1][DOWN]))
        if plane == last:
            leave(1, EDGE, plus(adds[last][OWN], adds[last - 1][UP]))
            leave(1, BEYOND, adds[last][UP])
        at = plane - 1
        if at < 1:
            continue
        v, e = cells_of(turned, at, 0, 3), cells_of(turned, at, 3, 4)[0]
        part = plus(adds[at - 1][UP], adds[at][OWN], adds[at + 1][DOWN])
        stiff[at] = stiffness(e, part[6:])
        rest = remainder(v, e, cells_of(turned, at, 4, 7), stiff[at], part)
        middle[at] = [jnp.where(outside, 0.0, x) for x in relaxed(v, stiff[at], rest)]

    adds = {}
    for plane in range(1, last):
        e = cells_of(turned, plane, 3, 4)[0]
        adds[plane] = moved(middle[plane], e)
        if plane == 1:
            leave(0, CARRY, adds[1][DOWN])
        if plane == last - 1:
            leave(1, CARRY, adds[last - 1][UP])
        for at in (plane - 1, plane):
            if at < 1 or (at == plane and plane < last - 1):
                continue
            beside = []
            if at - 1 in adds:
                beside.append(adds[at - 1][UP])
            if at + 1 in adds:
                beside.append(adds[at + 1][DOWN])
            part = plus(adds[at][OWN], *beside)
            v, e = middle[at], cells_of(turned, at, 3, 4)[0]
            rest = remainder(v, e, cells_of(turned, at, 4, 7), stiff[at], part)
            if len(beside) == 2:
                put_final(keep, at, relaxed(v, stiff[at], rest))
            else:
                side = 0 if at == 1 else 1
                leave(side, REST, rest)
                leave(side, HELD, v)
                leave(side, SCALE, stiff[at][1])


def inner_kernel(turned, left_in, keep_in, ids, left, keep, pick, nodes, sem):
    copy = pltpu.make_async_copy(ids, nodes, sem)
    copy.start()
    ahead = works_ahead()

    @pl.when(ahead)
    def _():
        left[...] = left_in[...]
        keep[...] = keep_in[...]

    @pl.when(jnp.logical_not(ahead))
    def _():
        inner_work(turned, left, keep)

    copy.wait()
    cell = lax.broadcasted_iota(jnp.int32, pick.shape, 0)
    pick[...] = jnp.where(cell == nodes[...] % 256, 1.0, 0.0).astype(BF16)


def sweep_kernel(
    devices, ncirc, turned, got_second, got_first, left, kept, pick, ids, shapes, keep, force, sums_of
):
    nrad = turned.shape[1] // 8
    rad = lax.axis_index("rad")
    odd = rad % 2 == 1
    outside = outside_mask()

    def halo(side, j, first, last):
        def tile(index):
            if index == 14:
                at = 22 + j
            elif index >= 8:
                at = 16 + index - 8
            else:
                at = 2 * index + j
            a, b = got_first[at], got_second[at]
            return jnp.where(odd, b, a) if side else jnp.where(odd, a, b)

        ends = tile(14)
        return [field_of(tile, f, ends) for f in range(first, last)]

    def handed(side, at, count):
        return [left[side, at + j] for j in range(count)]

    for side in range(2):
        inward = DOWN if side else UP
        near, far = (0, 1) if side else (1, 0)
        edge, next_in = (nrad - 1, nrad - 2) if side else (0, 1)
        v, e = halo(side, far, 0, 3), halo(side, far, 3, 4)[0]
        beyond = moved(v, e)[inward] + weighed(e)[inward]
        v, e = halo(side, near, 0, 3), halo(side, near, 3, 4)[0]
        here = [a + b for a, b in zip(moved(v, e), weighed(e))]
        part = plus(handed(side, BEYOND, 12), here[OWN], beyond)
        stiff = stiffness(e, part[6:])
        rest = remainder(v, e, halo(side, near, 4, 7), stiff, part)
        drop = outside | (rad == (lax.axis_size("rad") - 1 if side else 0))
        beside = moved([jnp.where(drop, 0.0, x) for x in relaxed(v, stiff, rest)], e)

        v, e = cells_of(turned, edge, 0, 3), cells_of(turned, edge, 3, 4)[0]
        rhs = cells_of(turned, edge, 4, 7)
        part = plus(handed(side, EDGE, 12), here[inward])
        stiff = stiffness(e, part[6:])
        v = [jnp.where(outside, 0.0, x) for x in relaxed(v, stiff, remainder(v, e, rhs, stiff, part))]
        here = moved(v, e)
        part = plus(handed(side, CARRY, 6), here[OWN], beside[inward])
        put_final(keep, edge, relaxed(v, stiff, remainder(v, e, rhs, stiff, part)))

        e = cells_of(turned, next_in, 3, 4)[0]
        add, rest = here[inward], handed(side, REST, 3)
        v, scale = handed(side, HELD, 3), handed(side, SCALE, 3)
        put_final(
            keep, next_in, [v[i] + scale[i] * (rest[i] + e * add[i] + add[3 + i]) for i in range(3)]
        )

    inside = slice(16, 8 * (nrad - 2))
    for index in range(6):
        keep[index, inside, :] = kept[index, inside, :]
    force_of(devices, ncirc, keep, pick, ids, shapes, force, sums_of)

def plane_of(keep, i, c, nrad):
    both = [keep[2 * i + t, pl.ds(c, nrad, stride=8), :] for t in range(2)]
    return jnp.concatenate(both, axis=1)


def emit_kernel(keep, adjoint):
    _, ncirc, nrad, _ = adjoint.shape
    for i in range(3):
        for c in range(ncirc):
            adjoint[i, c] = plane_of(keep, i, c, nrad)


def finish_kernel(keep, parts, adjoint, own, result, total, sems):
    emit_kernel(keep, result)
    first = pltpu.make_async_copy(result, adjoint, sems.at[0])
    first.start()
    total[...] = jnp.sum(parts[...], axis=0)[:, : total.shape[1]]
    second = pltpu.make_async_copy(total, own, sems.at[1])
    second.start()
    first.wait()
    second.wait()


def force_of(devices, ncirc, keep, pick, ids, shapes, force, sums_of):
    nrad = keep.shape[1] // 8
    lines = ncirc * nrad
    flat = jnp.concatenate([plane_of(keep, i, c, nrad) for i in range(3) for c in range(ncirc)], axis=0)
    high, low = split(flat)
    table = jnp.concatenate([high, low], axis=0).astype(BF16)
    node = ids[...]
    rows = jnp.dot(table, pick[...], preferred_element_type=F32)
    rows = rows[: 3 * lines] + rows[3 * lines :]
    line = lax.broadcasted_iota(jnp.int32, (lines, node.shape[1]), 0)
    hit = line == node // 256
    picked = [
        jnp.sum(jnp.where(hit, rows[lines * i : lines * (i + 1)], 0.0), axis=0, keepdims=True)
        for i in range(3)
    ]
    weighted = sum(shapes[i] * picked[i] for i in range(3))
    sums_of[...] = jnp.broadcast_to(jnp.sum(weighted, axis=1, keepdims=True), sums_of.shape)
    owned = sums_of.shape[0] // devices
    lane = lax.broadcasted_iota(jnp.int32, (devices, 128), 1)
    out = jnp.zeros((devices, 128), F32)
    for j in range(owned):
        out = jnp.where(lane == j, sums_of[pl.ds(j, devices, stride=owned), :], out)
    for r in range(force.shape[0] // devices):
        force[devices * r : devices * (r + 1), 0, :] = out


def swaps(axis, start, wrap):
    count = lax.axis_size(axis)
    pairs = []
    for i in range(start, count, 2):
        j = (i + 1) % count
        if j > i or wrap:
            pairs += [(i, j), (j, i)]
    return pairs


VMEM = pl.BlockSpec(memory_space=pltpu.VMEM)
HBM = pl.BlockSpec(memory_space=pltpu.HBM)


def call(kernel, ins, outs, scratch=(), flops=1_000_000, limit=40 * 1024 * 1024, out_specs=None):
    outs = [o if isinstance(o, jax.ShapeDtypeStruct) else jax.ShapeDtypeStruct(o, F32) for o in outs]
    return pl.pallas_call(
        kernel,
        out_shape=outs,
        in_specs=ins,
        out_specs=out_specs or [VMEM] * len(outs),
        scratch_shapes=list(scratch),
        compiler_params=pltpu.CompilerParams(vmem_limit_bytes=limit),
        cost_estimate=pl.CostEstimate(flops=flops, bytes_accessed=1_000_000, transcendentals=0),
    )


def on_device(
    adjoint_prev, cell_class, class_moduli, flow_sens, flow_nodes, flow_count, surf_ids, mode_shapes
):
    _, ncirc, nrad, naxial = adjoint_prev.shape
    n_mode, n_rad = lax.axis_size("mode"), lax.axis_size("rad")
    slots = flow_nodes.shape[-1]
    lines = ncirc * nrad
    cells = (ncirc, nrad, naxial)
    message = (24, 8, 128)
    args = (
        class_moduli, flow_count[0, 0, 0], adjoint_prev, cell_class,
        jnp.swapaxes(flow_sens[0, 0, 0], 0, 1), flow_nodes[0, 0, 0],
    )
    send, e = call(
        pack_kernel,
        [HBM] * 6,
        [(n_mode, 24, 128), cells],
        [pltpu.SMEM(x.shape, x.dtype) for x in args[:2]]
        + [pltpu.VMEM(x.shape, x.dtype) for x in args[2:]]
        + [pltpu.SemaphoreType.DMA((6,))],
        limit=63 * 1024 * 1024 + 512 * 1024,
    )(*args)
    got = lax.all_to_all(send, "mode", split_axis=0, concat_axis=0, tiled=True)
    rhs, ends, first, second = call(
        scatter_kernel,
        [VMEM] * 3,
        [(3,) + cells, (ncirc, nrad, 128), (8, 8, 128), message],
        flops=1,
    )(got, adjoint_prev, e)
    n_circ = lax.axis_size("circ")
    upward = [(i, (i + 1) % n_circ) for i in range(n_circ)]
    (up,) = call(early_kernel, [VMEM] * 2, [(16, 8, 128)])(adjoint_prev, e)
    up = lax.ppermute(up, "circ", upward)
    first = lax.ppermute(first, "circ", upward)
    (first,) = call(join_kernel, [VMEM] * 2, [message], flops=20_000_000_000)(up, first)
    second = lax.ppermute(second, "circ", [(j, i) for i, j in upward])
    kept = (6, 8 * nrad, 128)
    left = (2, COUNT, 8, 384)
    turned, first, second, left, keep = call(
        turn_kernel, [VMEM] * 6, [(15, 8 * nrad, 128), message, message, left, kept]
    )(
        adjoint_prev, e, rhs, ends, first, second
    )
    second = lax.ppermute(second, "rad", swaps("rad", 1, False))
    first = lax.ppermute(first, "rad", swaps("rad", 0, False))
    modes = mode_shapes.shape[3]
    owned = modes // n_mode
    ids = surf_ids[0, 0]
    shapes = jnp.swapaxes(mode_shapes[0, 0, 0], 0, 1)
    left, keep, pick = call(
        inner_kernel,
        [VMEM] * 3 + [HBM],
        [left.shape, kept, jax.ShapeDtypeStruct((naxial, ids.shape[1]), BF16)],
        [pltpu.VMEM(ids.shape, ids.dtype), pltpu.SemaphoreType.DMA],
        flops=10_000_000,
    )(turned, left, keep, ids)
    keep, force = call(
        functools.partial(sweep_kernel, n_mode, ncirc),
        [VMEM] * 8,
        [kept, (n_rad * n_mode, 1, 128)],
        [pltpu.VMEM((modes, 128), F32)],
    )(turned, second, first, left, keep, pick, ids, shapes)
    parts = lax.all_to_all(force, ("rad", "mode"), split_axis=0, concat_axis=0, tiled=True)
    final, own_force = call(
        finish_kernel,
        [VMEM] * 2,
        [adjoint_prev.shape, (1, owned)],
        [
            pltpu.VMEM(adjoint_prev.shape, F32), pltpu.VMEM((1, owned), F32),
            pltpu.SemaphoreType.DMA((2,)),
        ],
        out_specs=[HBM, HBM],
    )(keep, parts)
    return (final, own_force.reshape(owned, 1))


def solution(mesh):
    in_specs = (
        P(None, "circ", "rad", "mode"),
        P("circ", "rad", "mode"),
        P(),
        P("circ", "rad", "mode", None, None, None),
        P("circ", "rad", "mode", None, None),
        P("circ", "rad", "mode", None),
        P("circ", "rad", "mode", None),
        P("circ", "rad", "mode", None, None, None),
    )
    out_specs = (P(None, "circ", "rad", "mode"), P("mode", "circ"))
    return jax.shard_map(
        on_device, mesh=mesh, in_specs=in_specs, out_specs=out_specs, check_vma=False
    )
```
